32 devices in a mesh: px: 8 (over y, x, core), py: 4 (over z).
Axes of the slice: x: 2, y: 2, z: 4, core: 2. Of those that a mesh axis runs over, the one named last changes fastest.
Arguments:
- source: float32 [8, 256, 512], P(None, 'px', 'py'), may hold values from -12 to 12
- coefficient: float32 [8, 256, 512], P(None, 'px', 'py'), may hold values from 0.25 to 4
- strip_rows: int32 [4], replicated, may hold values from 1 to 40, 64 in all
Outputs:
- solution: float32 [8, 256, 512], P(None, 'px', 'py')
The draws below stay inside these ranges and needn't reach their ends.
Inputs may be any that keep to these rules, and one draw needn't show every extreme that they name: `strip_rows`: the entries sum to 64 and the largest is exactly 40.
All inputs are finite; a program needn't handle non-finite values.
Results may differ from the reference program's by a relative error of at most 0.00027.
Values sent between devices are 32-bit elements; how exact they have to be, the bound alone decides.
No kernel may reach another device: no remote copies, remote signals or barrier semaphores. Data moves between devices by JAX's collectives and lax.ppermute only.
A program may use at most 128 MiB of HBM per device.

```python
import math
import jax
import jax.numpy as jnp
import numpy as np

NZ = 8
CYCLES = 2
PRE = 2
POST = 2
COARSE_SWEEPS = 6
NX = 256
NY = 512
NX2 = 64
MOST = 40
STRIPS = 4


def draw_source(key, part):
    return 3.0 * jax.random.truncated_normal(key, -4.0, 4.0, (NZ, NX, NY), jnp.float32)


def block_levels(own_key, shape, split, smallest, top_value):
    factor_of, own = 1.0, jax.random.fold_in(own_key, 6)
    for axis_at, blocks in split:
        draws = jnp.exp(jax.random.uniform(jax.random.fold_in(own, axis_at), (blocks,), jnp.float32, smallest / len(split), top_value / len(split)))
        factor_of = factor_of * jnp.repeat(draws, shape[axis_at] // blocks).reshape([-1 if axis == axis_at else 1 for axis in range(len(shape))])
    return factor_of


def profile(count, total, most, skew):
    loads = [(1 << 20) // math.isqrt(grade ** skew) + 1 for grade in range(2, count + 1)]
    surplus, holding = total - most - (count - 1), [1] * (count - 1)
    while surplus > 0:
        movable = [i for i in range(count - 1) if holding[i] < most]
        mass, budget = sum([loads[i] for i in movable]), surplus
        for i in movable:
            addition = min(most - holding[i], max(1, budget * loads[i] // mass), surplus)
            holding[i] = holding[i] + addition
            surplus = surplus - addition
    return np.array([most] + holding)


def uneven(own_key, amount, total, bound, skew):
    if amount == 2:
        one = jax.random.randint(own_key, (), max(1, total - bound), min(bound, total - 1) + 1)
        return jnp.stack([one, total - one])
    lengths = jnp.asarray(profile(amount, total, bound, skew), jnp.int32)
    couples = (amount - 1) // 2
    source_of, sink = lengths[1:1 + 2 * couples:2], lengths[2:2 + 2 * couples:2]
    room = jnp.minimum(source_of - 1, bound - sink)
    passed = jax.random.randint(jax.random.fold_in(own_key, 1), (couples,), 0, 1 << 20) % (room + 1)
    lengths = lengths.at[1:1 + 2 * couples:2].set(source_of - passed).at[2:2 + 2 * couples:2].set(sink + passed)
    return lengths[jax.random.permutation(jax.random.fold_in(own_key, 2), amount)]


def setup_inputs(seed: int = 0) -> dict:
    keys = jax.random.split(jax.random.key(seed), 4)
    source = draw_source(jax.random.fold_in(keys[3], 71), 0)
    coefficient = jnp.clip(jnp.exp(math.log(4.0) - 2.7725887 * jax.random.uniform(keys[1], (NZ, NX, NY), jnp.float32) ** block_levels(keys[1], (NZ, NX, NY), ((1, 8), (2, 4)), -0.2, 0.2)), 0.25, 4.0)
    strip_rows = uneven(keys[2], STRIPS, NX2, MOST, 2).astype(jnp.int32)
    return dict(source=source, coefficient=coefficient, strip_rows=strip_rows)


relaxation = 0.8
z_coupling = 0.25


def pad_plain(values):
    return jnp.pad(values, ((0, 0), (1, 1), (1, 1)))


def face_arrays(conduct, z_factor):
    padded = pad_plain(conduct)
    face_west = 0.5 * (conduct + padded[:, :-2, 1:-1])
    face_east = 0.5 * (conduct + padded[:, 2:, 1:-1])
    face_south = 0.5 * (conduct + padded[:, 1:-1, :-2])
    face_north = 0.5 * (conduct + padded[:, 1:-1, 2:])
    vertical = z_factor * 0.5 * (conduct[:-1] + conduct[1:])
    zero_layer = jnp.zeros_like(conduct[:1])
    face_down = jnp.concatenate([zero_layer, vertical], axis=0)
    face_up = jnp.concatenate([vertical, zero_layer], axis=0)
    diagonal = face_west + face_east + face_south + face_north + face_down + face_up
    return [face_west, face_east, face_south, face_north, face_down, face_up, diagonal]


def update(values, values_pad, faces, source_term):
    face_west, face_east, face_south, face_north, face_down, face_up, diagonal, inverse = faces
    zero_layer = jnp.zeros_like(values[:1])
    value_down = jnp.concatenate([zero_layer, values[:-1]], axis=0)
    value_up = jnp.concatenate([values[1:], zero_layer], axis=0)
    beside = (face_west * values_pad[:, :-2, 1:-1] + face_east * values_pad[:, 2:, 1:-1]
              + face_south * values_pad[:, 1:-1, :-2] + face_north * values_pad[:, 1:-1, 2:]
              + face_down * value_down + face_up * value_up)
    return source_term - diagonal * values + beside


def relax_sweep(values, values_pad, faces, source_term):
    return values + relaxation * faces[7] * update(values, values_pad, faces, source_term)


def smooth(values, source_term, faces, count):
    for sweep_index in range(count):
        values = relax_sweep(values, pad_plain(values), faces, source_term)
    return values


def coarsen(values):
    layers, row_count, col_count = values.shape
    return 0.25 * values.reshape(layers, row_count // 2, 2, col_count // 2, 2).sum(axis=(2, 4))


def restrict(values):
    layers, row_count, col_count = values.shape
    return values.reshape(layers, row_count // 2, 2, col_count // 2, 2).sum(axis=(2, 4))


def prolong(values):
    return jnp.repeat(jnp.repeat(values, 2, axis=1), 2, axis=2)


def strip_ids(strip_rows, rows_global):
    ends = jnp.cumsum(strip_rows)
    return jnp.sum((rows_global[:, None] >= ends[None, :]).astype(jnp.int32), axis=1)


def level_faces(conduct, z_factor):
    faces = face_arrays(conduct, z_factor)
    faces.append(1.0 / faces[6])
    return faces


def reference(source, coefficient, strip_rows):
    mid_conduct = coarsen(coefficient)
    low_conduct = coarsen(mid_conduct)
    fine_faces = level_faces(coefficient, z_coupling)
    mid_faces = level_faces(mid_conduct, 4.0 * z_coupling)
    low_faces = face_arrays(low_conduct, 16.0 * z_coupling)
    row_ids = strip_ids(strip_rows, jnp.arange(NX2, dtype=jnp.int32))
    same_next = (row_ids[:-1] == row_ids[1:]).astype(jnp.float32)
    zero_one = jnp.zeros((1,), jnp.float32)
    keep_west = jnp.concatenate([zero_one, same_next])
    keep_east = jnp.concatenate([same_next, zero_one])
    low_faces[0] = low_faces[0] * keep_west[None, :, None]
    low_faces[1] = low_faces[1] * keep_east[None, :, None]
    low_faces.append(1.0 / low_faces[6])
    onehot = (row_ids[:, None] == jnp.arange(STRIPS, dtype=jnp.int32)[None, :]).astype(jnp.float32)
    diag_rows = jnp.sum(low_faces[6], axis=(0, 2))
    diag_total = jnp.sum(onehot * diag_rows[:, None], axis=0)
    solution = jnp.zeros_like(source)
    for cycle_index in range(CYCLES):
        solution = smooth(solution, source, fine_faces, PRE)
        mid_source = restrict(update(solution, pad_plain(solution), fine_faces, source))
        middle = smooth(jnp.zeros_like(mid_source), mid_source, mid_faces, PRE)
        low_source = restrict(update(middle, pad_plain(middle), mid_faces, mid_source))
        correction = smooth(jnp.zeros_like(low_source), low_source, low_faces, COARSE_SWEEPS)
        left_over = update(correction, pad_plain(correction), low_faces, low_source)
        res_rows = jnp.sum(left_over, axis=(0, 2))
        res_total = jnp.sum(onehot * res_rows[:, None], axis=0)
        shift_strip = res_total / diag_total
        shift_rows = jnp.sum(onehot * shift_strip[None, :], axis=1)
        correction = correction + shift_rows[None, :, None]
        middle = smooth(middle + prolong(correction), mid_source, mid_faces, POST)
        solution = smooth(solution + prolong(middle), source, fine_faces, POST)
    return solution
```

```python
import functools

import jax
import jax.numpy as jnp
from jax import lax
from jax.experimental import pallas as pl
from jax.experimental.pallas import tpu as pltpu
from jax.sharding import PartitionSpec as P

CYCLES = 2
COARSE_SWEEPS = 6
relaxation = 0.8
z_coupling = 0.25

HALO = 24
SIDE = 32
PAD = 8
LANES = 128
VMEM = pl.BlockSpec(memory_space=pltpu.VMEM)
SMEM = pl.BlockSpec(memory_space=pltpu.SMEM)
F32 = jnp.float32


def shifted(values, amount, axis):
    return pltpu.roll(values, amount % values.shape[axis], axis)


def lane_of(values):
    return lax.broadcasted_iota(jnp.int32, values.shape, values.ndim - 1)


def rows_loop(low, high, chunk, body):
    chunk = min(chunk, high - low)
    count = -(-(high - low) // chunk)

    def step(index, carry):
        body(jnp.minimum(low + index * chunk, high - chunk), chunk)
        return carry

    lax.fori_loop(0, count, step, 0)


def pair_sum_lanes(values, step):
    first = (lane_of(values) // step) % 2 == 0
    return values + jnp.where(first, shifted(values, -step, 2), shifted(values, step, 2))


def pair_sum_rows(values):
    count = values.shape[0] // 2
    pairs = values.reshape((count, 2) + values.shape[1:])
    return pairs[:, 0] + pairs[:, 1]


W, E, S, N, D, U, BACK, INV = range(8)


def make_coefficients(k_ref, co, low, high, z_factor, step, chunk):
    def body(at, size):
        k = k_ref[pl.ds(at, size)]
        layer = lax.broadcasted_iota(jnp.int32, k.shape, 1)
        west = 0.5 * (k + k_ref[pl.ds(at - 1, size)])
        east = 0.5 * (k + k_ref[pl.ds(at + 1, size)])
        south = 0.5 * (k + shifted(k, step, 2))
        north = 0.5 * (k + shifted(k, -step, 2))
        half = 0.5 * z_factor
        down = jnp.where(layer == 0, 0.0, half * (k + shifted(k, 1, 1)))
        up = jnp.where(layer == k.shape[1] - 1, 0.0, half * (k + shifted(k, -1, 1)))
        diagonal = west + east + south + north + down + up
        inside = k > 0.0
        inverse = jnp.where(inside, relaxation / jnp.where(inside, diagonal, 1.0), 0.0)
        for which, face in zip((W, E, S, N, D, U), (west, east, south, north, down, up)):
            co[which, pl.ds(at, size)] = inverse * face
        co[BACK, pl.ds(at, size)] = (1.0 / relaxation) * diagonal
        co[INV, pl.ds(at, size)] = inverse

    rows_loop(low, high, chunk, body)


def swept(v_ref, co, g_ref, at, size, step):
    here = pl.ds(at, size)
    v = v_ref[here]
    total = g_ref[here] + (1.0 - relaxation) * v
    total = total + co[W, here] * v_ref[pl.ds(at - 1, size)]
    total = total + co[E, here] * v_ref[pl.ds(at + 1, size)]
    total = total + co[S, here] * shifted(v, step, 2)
    total = total + co[N, here] * shifted(v, -step, 2)
    total = total + co[D, here] * shifted(v, 1, 1)
    total = total + co[U, here] * shifted(v, -1, 1)
    return v, total


def sweep(v_ref, out_ref, co, g_ref, low, high, step, chunk):
    def body(at, size):
        out_ref[pl.ds(at, size)] = swept(v_ref, co, g_ref, at, size, step)[1]

    rows_loop(low, high, chunk, body)


def restricted(v_ref, co, g_ref, at, size, step):
    v, new = swept(v_ref, co, g_ref, 2 * at, 2 * size, step)
    left_over = co[BACK, pl.ds(2 * at, 2 * size)] * (new - v)
    return pair_sum_lanes(pair_sum_rows(left_over), step)


def coarse_rows(values):
    own = values[:, :, :LANES]
    left = jnp.concatenate(
        [jnp.concatenate([own[4 * p + g] for g in range(4)], axis=1) for p in range(2)], axis=0
    )
    row = lax.broadcasted_iota(jnp.int32, (4 * LANES, LANES), 0)
    col = lax.broadcasted_iota(jnp.int32, (4 * LANES, LANES), 1)
    place = (row // LANES) * (LANES // 4) + (row % LANES) // 4
    pick = jnp.where((row % 4 == 0) & (col == place), 1.0, 0.0).astype(F32)
    packed = lax.dot_general(
        left, pick, (((1,), (0,)), ((), ())), precision=lax.Precision.HIGHEST, preferred_element_type=F32
    )
    layers = own.shape[1]
    return packed[:layers], packed[layers:]


def assemble_kernel(rows, even_ref, source, coefficient, recv_a, recv_b, ext_s, ext_k, send_a, send_b):
    even_x, even_y = even_ref[0] == 0, even_ref[1] == 0
    layers = ext_s.shape[1]
    for which, (own, ext) in enumerate(((source, ext_s), (coefficient, ext_k))):
        for r in range(HALO):
            pick = pl.ds(which * layers * HALO + r, layers, stride=HALO)
            a, b = recv_a[pick, :], recv_b[pick, :]
            ext[r] = jnp.where(even_x, b, a)
            ext[HALO + rows + r] = jnp.where(even_x, a, b)
        for r in range(rows):
            ext[HALO + r] = own[pl.ds(r, layers, stride=rows), :]
    half = send_a.shape[0]

    def body(at, size):
        parts = [e[pl.ds(at + h * half, size)] for e in (ext_s, ext_k) for h in range(2)]
        group = lane_of(parts[0]) // SIDE
        first, last = parts[0], shifted(parts[0], SIDE, 2)
        for g in range(1, 4):
            first = jnp.where(group == g, shifted(parts[g], g * SIDE, 2), first)
            last = jnp.where(group == g, shifted(parts[g], (g + 1) * SIDE, 2), last)
        send_a[pl.ds(at, size)] = jnp.where(even_y, last, first)
        send_b[pl.ds(at, size)] = jnp.where(even_y, first, last)

    rows_loop(0, half, 8, body)


def descend_kernel(
    rows, even_ref, ext_s, ext_k, recv_a, recv_b, fine_u, fine_g, fine_co, mid_v, mid_g, mid_co, packed, s, k, k1
):
    even_y = even_ref[1] == 0
    total = rows + 2 * HALO
    half = total // 2

    def widen(at, size):
        a, b = recv_a[pl.ds(at, size)], recv_b[pl.ds(at, size)]
        right, left = jnp.where(even_y, a, b), jnp.where(even_y, b, a)
        lane = lane_of(right)
        for which, (ext, wide) in enumerate(((ext_s, s), (ext_k, k))):
            for h in range(2):
                group = 2 * which + h
                beside = jnp.where(
                    lane < SIDE,
                    shifted(right, -group * SIDE, 2),
                    jnp.where(lane >= LANES - SIDE, shifted(left, -(group + 1) * SIDE, 2), 0.0),
                )
                wide[pl.ds(at + h * half, size), :, pl.ds(0, LANES)] = ext[pl.ds(at + h * half, size)]
                wide[pl.ds(at + h * half, size), :, pl.ds(LANES, LANES)] = beside

    rows_loop(0, half, 4, widen)

    def coarser(at, size):
        k1[pl.ds(at, size)] = 0.25 * pair_sum_lanes(pair_sum_rows(k[pl.ds(2 * at, 2 * size)]), 1)

    rows_loop(0, half, 4, coarser)
    h0, h1 = HALO, HALO // 2
    m = rows // 2
    make_coefficients(k, fine_co, h0 - 22, h0 + rows + 22, z_coupling, 1, 2)
    make_coefficients(k1, mid_co, h1 - 10, h1 + m + 10, 4.0 * z_coupling, 2, 2)

    def scale(at, size):
        fine_g[pl.ds(at, size)] = fine_co[INV, pl.ds(at, size)] * s[pl.ds(at, size)]

    rows_loop(h0 - 22, h0 + rows + 22, 8, scale)
    descend(rows, fine_g, fine_u, fine_g, fine_co, mid_v, mid_g, mid_co, 10, packed)
    k2 = 0.25 * pair_sum_lanes(pair_sum_rows(k1[pl.ds(h1, m)]), 2)
    packed[2], packed[3] = coarse_rows(k2)


def descend(rows, fine_first, fine_u, fine_g, fine_co, mid_v, mid_g, mid_co, reach, packed):
    h0, h1 = HALO, HALO // 2
    m = rows // 2
    sweep(fine_first, fine_u, fine_co, fine_g, h0 - 2 * reach - 1, h0 + rows + 2 * reach + 1, 1, 8)

    def down(at, size):
        total = restricted(fine_u, fine_co, fine_g, at, size, 1)
        mid_g[pl.ds(at, size)] = mid_co[INV, pl.ds(at, size)] * total

    rows_loop(h1 - reach, h1 + m + reach, 4, down)
    sweep(mid_g, mid_v, mid_co, mid_g, h1 - reach + 1, h1 + m + reach - 1, 2, 8)
    low = restricted(mid_v, mid_co, mid_g, h1 // 2, m // 2, 2)
    packed[0], packed[1] = coarse_rows(low)


def unpack(gathered, base, target, first, npx, npy, block):
    per = 4
    width = LANES // per

    def body(ix, carry):
        for p in range(block // per):
            for q in range(npy // per):
                parts = [gathered[ix * npy + per * q + j, base + p] for j in range(per)]
                group = lane_of(parts[0]) // width
                for g in range(per):
                    row = shifted(parts[0], -g * width, 1)
                    for j in range(1, per):
                        row = jnp.where(group == j, shifted(parts[j], (j - g) * width, 1), row)
                    target[first + ix * block + per * p + g, :, pl.ds(q * LANES, LANES)] = row
        return carry

    lax.fori_loop(0, npx, body, 0)


def coarse_coefficients(rows2, strips_ref, k2, co, count):
    layers, width = k2.shape[1], k2.shape[2]

    def body(index, start):
        end = start + strips_ref[index]

        def row(r, carry):
            k = k2[r]
            layer = lax.broadcasted_iota(jnp.int32, k.shape, 0)
            lane = lax.broadcasted_iota(jnp.int32, k.shape, 1)
            west = 0.5 * (k + k2[r - 1])
            east = 0.5 * (k + k2[r + 1])
            open_s, open_n = lane > 0, lane < width - 1
            south = 0.5 * (k + jnp.where(open_s, shifted(k, 1, 1), 0.0))
            north = 0.5 * (k + jnp.where(open_n, shifted(k, -1, 1), 0.0))
            half = 0.5 * 16.0 * z_coupling
            down = jnp.where(layer == 0, 0.0, half * (k + shifted(k, 1, 0)))
            up = jnp.where(layer == layers - 1, 0.0, half * (k + shifted(k, -1, 0)))
            diagonal = west + east + south + north + down + up
            inverse = relaxation / diagonal
            co[W, r] = jnp.where(r > start, inverse * west, 0.0)
            co[E, r] = jnp.where(r < end - 1, inverse * east, 0.0)
            co[S, r] = jnp.where(open_s, inverse * south, 0.0)
            co[N, r] = jnp.where(open_n, inverse * north, 0.0)
            co[D, r] = inverse * down
            co[U, r] = inverse * up
            co[BACK, r] = (1.0 / relaxation) * diagonal
            co[INV, r] = inverse
            return carry

        lax.fori_loop(start, end, row, 0)
        return end

    lax.fori_loop(0, count, body, PAD)


def coarse_solve(rows2, strips_ref, count, co, g, a, b):
    zero = jnp.zeros(g.shape[1:], F32)
    for ref in (g, a, b):
        ref[PAD - 1] = zero
        ref[PAD + rows2] = zero
    for r in range(PAD - 1):
        b[r] = zero
        b[PAD + rows2 + 1 + r] = zero
    at = g
    for index in range(COARSE_SWEEPS - 1):
        to = b if index % 2 == 0 else a
        sweep(at, to, co, g, PAD, PAD + rows2, 1, 8)
        at = to

    def left(first, size):
        v, new = swept(b, co, g, first, size, 1)
        a[pl.ds(first, size)] = co[BACK, pl.ds(first, size)] * (new - v)

    rows_loop(PAD, PAD + rows2, 8, left)

    def strip(index, start):
        end = start + strips_ref[index]

        def add(r, sums):
            return sums[0] + a[r], sums[1] + co[BACK, r]

        over, diagonal = lax.fori_loop(start, end, add, (zero, zero))
        over = jnp.sum(jnp.sum(over, axis=1, keepdims=True), axis=0, keepdims=True)
        diagonal = jnp.sum(jnp.sum(diagonal, axis=1, keepdims=True), axis=0, keepdims=True)
        shift = jnp.broadcast_to(over / (relaxation * diagonal), zero.shape)

        def apply(r, carry):
            b[r] = b[r] + shift
            return carry

        lax.fori_loop(start, end, apply, 0)
        return end

    lax.fori_loop(0, count, strip, PAD)


def correct(rows, place_ref, e2, mid_v, target, reach):
    h1, m = HALO // 2, rows // 2
    low = -(-reach // 2)
    block = rows // 4
    width = e2.shape[2]
    span = block + 2 * low
    x_at, y_at = place_ref[2], place_ref[3]
    window = e2[pl.ds(x_at * block + PAD - low, span)]
    row = lax.broadcasted_iota(jnp.int32, (width, 2 * LANES), 0)
    col = lax.broadcasted_iota(jnp.int32, (width, 2 * LANES), 1)
    offset = jnp.where(col >= 2 * LANES - SIDE, col - 2 * LANES, col)
    cell = (offset + LANES) // 4 - LANES // 4 + y_at * (LANES // 4)
    pick = jnp.where((row == cell) & ((col < LANES + SIDE) | (col >= 2 * LANES - SIDE)), 1.0, 0.0).astype(F32)
    spread = lax.dot_general(
        window.reshape(span * window.shape[1], width),
        pick,
        (((1,), (0,)), ((), ())),
        precision=lax.Precision.HIGHEST,
        preferred_element_type=F32,
    ).reshape(span, window.shape[1], 2 * LANES)
    for at in range(h1 - reach, h1 + m + reach):
        target[at] = mid_v[at] + spread[at // 2 - h1 // 2 + low]


def ascend(rows, reach, mid_a, mid_b, mid_co, mid_g, fine_u, fine_t, fine_co, fine_g, last_ref):
    h0, h1 = HALO, HALO // 2
    m = rows // 2
    sweep(mid_a, mid_b, mid_co, mid_g, h1 - reach + 1, h1 + m + reach - 1, 2, 8)
    sweep(mid_b, mid_a, mid_co, mid_g, h1 - reach + 2, h1 + m + reach - 2, 2, 8)
    edge = 2 * (reach - 2) - 1

    def add(at, size):
        fine = fine_u[pl.ds(2 * at, 2 * size)]
        both = fine.reshape((size, 2) + fine.shape[1:]) + mid_a[pl.ds(at, size)][:, None]
        fine_u[pl.ds(2 * at, 2 * size)] = both.reshape(fine.shape)

    for at in range(h1 - reach + 2, h1 + m + reach - 2):
        add(at, 1)
    sweep(fine_u, fine_t, fine_co, fine_g, h0 - edge + 0, h0 + rows + edge, 1, 8)
    sweep(fine_t, last_ref, fine_co, fine_g, h0 - edge + 1, h0 + rows + edge - 1, 1, 8)


def middle_kernel(
    rows, npx, npy, place_ref, strips_ref, gathered, fine_u, fine_g, fine_co, mid_v, mid_g, mid_co,
    fine_out, mid_v_out, mid_g_out, packed, low_co,
    k2, g2, a2, b2, va, vb, fa, fb,
):
    block = rows // 4
    rows2 = npx * block
    count = strips_ref.shape[0]
    k2[PAD - 1] = jnp.zeros(k2.shape[1:], F32)
    k2[PAD + rows2] = jnp.zeros(k2.shape[1:], F32)
    unpack(gathered, 2, k2, PAD, npx, npy, block)
    coarse_coefficients(rows2, strips_ref, k2, low_co, count)
    solve(rows2, strips_ref, count, gathered, g2, a2, b2, low_co, npx, npy, block)
    correct(rows, place_ref, b2, mid_v, va, 9)

    def copy(at, size):
        fa[pl.ds(at, size)] = fine_u[pl.ds(at, size)]

    rows_loop(HALO - 14, HALO + rows + 14, 8, copy)
    ascend(rows, 9, va, vb, mid_co, mid_g, fa, fb, fine_co, fine_g, fa)
    sweep(fa, fb, fine_co, fine_g, HALO - 10, HALO + rows + 10, 1, 8)
    descend(rows, fb, fine_out, fine_g, fine_co, mid_v_out, mid_g_out, mid_co, 4, packed)


def solve(rows2, strips_ref, count, gathered, g2, a2, b2, low_co, npx, npy, block):
    unpack(gathered, 0, g2, PAD, npx, npy, block)

    def scale(at, size):
        g2[pl.ds(at, size)] = g2[pl.ds(at, size)] * low_co[INV, pl.ds(at, size)]

    rows_loop(PAD, PAD + rows2, 8, scale)
    coarse_solve(rows2, strips_ref, count, low_co, g2, a2, b2)


def last_kernel(
    rows, npx, npy, place_ref, strips_ref, gathered, fine_u, fine_g, fine_co, mid_v, mid_g, mid_co, low_co,
    out, g2, a2, b2, va, vb, fa, fb,
):
    block = rows // 4
    rows2 = npx * block
    count = strips_ref.shape[0]
    solve(rows2, strips_ref, count, gathered, g2, a2, b2, low_co, npx, npy, block)
    correct(rows, place_ref, b2, mid_v, va, 3)

    def copy(at, size):
        fa[pl.ds(at, size)] = fine_u[pl.ds(at, size)]

    rows_loop(HALO - 2, HALO + rows + 2, 8, copy)
    ascend(rows, 3, va, vb, mid_co, mid_g, fa, fb, fine_co, fine_g, fa)
    layers = fa.shape[1]
    for r in range(rows):
        out[pl.ds(r, layers, stride=rows), :] = fa[HALO + r, :, pl.ds(0, LANES)]


def neighbour_swaps(axis, send_a, send_b):
    count = lax.axis_size(axis)
    a = [(i, i ^ 1) for i in range(count)]
    b = [(i, ((i + 1) ^ 1) - 1) for i in range(1, count - 1)]
    return lax.ppermute(send_a, axis, a), lax.ppermute(send_b, axis, b)


def arr(*shape):
    return jax.ShapeDtypeStruct(shape, F32)


def shards(source, coefficient, strip_rows):
    npx, npy = lax.axis_size("px"), lax.axis_size("py")
    layers, rows, _ = source.shape
    total, mids = rows + 2 * HALO, (rows + 2 * HALO) // 2
    rows2, width2 = npx * rows // 4, npy * LANES // 4
    px, py = lax.axis_index("px"), lax.axis_index("py")
    place = jnp.stack([px % 2, py % 2, px, py]).astype(jnp.int32)
    even = px % 2 == 0

    def cut(first):
        return jnp.stack(
            [lax.dynamic_slice_in_dim(array, first, HALO, 1) for array in (source, coefficient)]
        )

    send_a = cut(jnp.where(even, rows - HALO, 0))
    send_b = cut(jnp.where(even, 0, rows - HALO))
    recv_a, recv_b = neighbour_swaps("px", send_a, send_b)
    params = pltpu.CompilerParams(vmem_limit_bytes=44 * 1024 * 1024)
    ext_s, ext_k, send_a, send_b = pl.pallas_call(
        functools.partial(assemble_kernel, rows),
        out_shape=(arr(total, layers, LANES),) * 2 + (arr(mids, layers, LANES),) * 2,
        in_specs=[SMEM] + [VMEM] * 4,
        out_specs=(VMEM,) * 4,
        compiler_params=params,
        name="assemble",
    )(
        place,
        source.reshape(layers * rows, LANES),
        coefficient.reshape(layers * rows, LANES),
        recv_a.reshape(2 * layers * HALO, LANES),
        recv_b.reshape(2 * layers * HALO, LANES),
    )
    recv_a, recv_b = neighbour_swaps("py", send_a, send_b)
    fine, mid = arr(total, layers, 2 * LANES), arr(mids, layers, 2 * LANES)
    fine_cos, mid_cos = arr(8, *fine.shape), arr(8, *mid.shape)

    def scratch(*like):
        return [pltpu.VMEM(item.shape, F32) for item in like]

    fine_u, fine_g, fine_co, mid_v, mid_g, mid_co, packed = pl.pallas_call(
        functools.partial(descend_kernel, rows),
        out_shape=(fine, fine, fine_cos, mid, mid, mid_cos, arr(4, layers, LANES)),
        in_specs=[SMEM] + [VMEM] * 4,
        out_specs=(VMEM,) * 7,
        scratch_shapes=scratch(fine, fine, mid),
        compiler_params=params,
        name="descend",
    )(place, ext_s, ext_k, recv_a, recv_b)

    def gather(block):
        every = jnp.broadcast_to(block[None], (npx * npy,) + block.shape)
        return lax.all_to_all(every, ("px", "py"), 0, 0, tiled=True)

    low = arr(rows2 + 2 * PAD, layers, width2)
    low_cos = arr(8, *low.shape)
    fine_u, mid_v, mid_g, packed, low_co = pl.pallas_call(
        functools.partial(middle_kernel, rows, npx, npy),
        out_shape=(fine, mid, mid, arr(2, layers, LANES), low_cos),
        in_specs=[SMEM] * 2 + [VMEM] * 7,
        out_specs=(VMEM,) * 5,
        scratch_shapes=scratch(low, low, low, low, mid, mid, fine, fine),
        compiler_params=params,
        name="middle",
    )(place, strip_rows, gather(packed), fine_u, fine_g, fine_co, mid_v, mid_g, mid_co)
    out = pl.pallas_call(
        functools.partial(last_kernel, rows, npx, npy),
        out_shape=arr(layers * rows, LANES),
        in_specs=[SMEM] * 2 + [VMEM] * 8,
        out_specs=VMEM,
        scratch_shapes=scratch(low, low, low, mid, mid, fine, fine),
        compiler_params=params,
        name="last",
    )(place, strip_rows, gather(packed), fine_u, fine_g, fine_co, mid_v, mid_g, mid_co, low_co)
    return out.reshape(source.shape)


def solution(mesh):
    placed = (P(None, "px", "py"), P(None, "px", "py"), P())
    return jax.shard_map(
        shards, mesh=mesh, in_specs=placed, out_specs=P(None, "px", "py"), check_vma=False
    )
```

```python
import functools

import jax
import jax.numpy as jnp
from jax import lax
from jax.experimental import pallas as pl
from jax.experimental.pallas import tpu as pltpu
from jax.sharding import PartitionSpec as P

COARSE_SWEEPS = 6
relaxation = 0.8
z_coupling = 0.25

HALO = 24
SIDE = 32
PAD = 8
LANES = 128
HALF = LANES // 2
SLOT = SIDE // 2
VMEM = pl.BlockSpec(memory_space=pltpu.VMEM)
SMEM = pl.BlockSpec(memory_space=pltpu.SMEM)
F32 = jnp.float32


def shifted(values, amount, axis):
    return pltpu.roll(values, amount % values.shape[axis], axis)


def iota_of(values, axis):
    return lax.broadcasted_iota(jnp.int32, values.shape, axis % values.ndim)


def rows_loop(low, high, chunk, body):
    chunk = min(chunk, high - low)
    count = -(-(high - low) // chunk)
    chunk = -(-(high - low) // count)

    def step(index, carry):
        body(jnp.minimum(low + index * chunk, high - chunk), chunk)
        return carry

    if count == 1:
        body(low, chunk)
    else:
        lax.fori_loop(0, count, step, 0)


def pair_sum_rows(values):
    count = values.shape[0] // 2
    pairs = values.reshape((count, 2) + values.shape[1:])
    return pairs[:, 0] + pairs[:, 1]


def pair_sum_lanes(values):
    return values + jnp.where(iota_of(values, -1) % 2 == 0, shifted(values, -1, 2), shifted(values, 1, 2))


def exact_dot(left, right):
    return lax.dot_general(
        left, right, (((1,), (0,)), ((), ())), precision=lax.Precision.HIGHEST, preferred_element_type=F32
    )


def one_hot(shape, place):
    row = lax.broadcasted_iota(jnp.int32, shape, 0)
    col = lax.broadcasted_iota(jnp.int32, shape, 1)
    return jnp.where(place(row, col), 1.0, 0.0).astype(F32)


W, E, S, N, D, U, BACK, INV = range(8)


def weights(k, west, east, south, north, z_factor):
    layer = iota_of(k, -2)
    west, east, south, north = (0.5 * (k + other) for other in (west, east, south, north))
    half = 0.5 * z_factor
    axis = k.ndim - 2
    down = jnp.where(layer == 0, 0.0, half * (k + shifted(k, 1, axis)))
    up = jnp.where(layer == k.shape[axis] - 1, 0.0, half * (k + shifted(k, -1, axis)))
    diagonal = west + east + south + north + down + up
    inside = k > 0.0
    inverse = jnp.where(inside, relaxation / jnp.where(inside, diagonal, 1.0), 0.0)
    scaled = [inverse * face for face in (west, east, south, north, down, up)]
    return scaled + [(1.0 / relaxation) * diagonal, inverse]


def fine_coefficients(k_ref, s_ref, co, g_ref, low, high, chunk):
    def body(at, size):
        here, before, after = pl.ds(at, size), pl.ds(at - 1, size), pl.ds(at + 1, size)
        k = [k_ref[here, s] for s in range(2)]
        sides = ((shifted(k[1], 1, 2), k[1]), (k[0], shifted(k[0], -1, 2)))
        for s in range(2):
            found = weights(k[s], k_ref[before, s], k_ref[after, s], *sides[s], z_coupling)
            for which in range(INV):
                co[which, here, s] = found[which]
            g_ref[here, s] = found[INV] * s_ref[here, s]

    rows_loop(low, high, chunk, body)


def mid_coefficients(k_ref, co, low, high, chunk):
    def body(at, size):
        here = pl.ds(at, size)
        k = k_ref[here]
        found = weights(
            k, k_ref[pl.ds(at - 1, size)], k_ref[pl.ds(at + 1, size)], shifted(k, 1, 2), shifted(k, -1, 2),
            4.0 * z_coupling,
        )
        for which in range(INV + 1):
            co[which, here] = found[which]

    rows_loop(low, high, chunk, body)


def swept_fine(v_ref, co, g_ref, at, size):
    here, before, after = pl.ds(at, size), pl.ds(at - 1, size), pl.ds(at + 1, size)
    v = [v_ref[here, s] for s in range(2)]
    sides = ((shifted(v[1], 1, 2), v[1]), (v[0], shifted(v[0], -1, 2)))
    new = []
    for s in range(2):
        total = g_ref[here, s] + (1.0 - relaxation) * v[s]
        total = total + co[W, here, s] * v_ref[before, s]
        total = total + co[E, here, s] * v_ref[after, s]
        total = total + co[D, here, s] * shifted(v[s], 1, 1)
        total = total + co[U, here, s] * shifted(v[s], -1, 1)
        total = total + co[S, here, s] * sides[s][0]
        total = total + co[N, here, s] * sides[s][1]
        new.append(total)
    return v, new


def swept(v_ref, co, g_ref, at, size):
    here = pl.ds(at, size)
    v = v_ref[here]
    total = g_ref[here] + (1.0 - relaxation) * v
    total = total + co[W, here] * v_ref[pl.ds(at - 1, size)]
    total = total + co[E, here] * v_ref[pl.ds(at + 1, size)]
    total = total + co[D, here] * shifted(v, 1, 1)
    total = total + co[U, here] * shifted(v, -1, 1)
    total = total + co[S, here] * shifted(v, 1, 2)
    total = total + co[N, here] * shifted(v, -1, 2)
    return v, total


def sweep_fine(v_ref, out_ref, co, g_ref, low, high):
    def body(at, size):
        new = swept_fine(v_ref, co, g_ref, at, size)[1]
        for s in range(2):
            out_ref[pl.ds(at, size), s] = new[s]

    rows_loop(low, high, FINE_CHUNK, body)


def sweep(v_ref, out_ref, co, g_ref, low, high):
    def body(at, size):
        out_ref[pl.ds(at, size)] = swept(v_ref, co, g_ref, at, size)[1]

    rows_loop(low, high, CHUNK, body)


FINE_CHUNK = 16
CHUNK = 32


def coarse_rows(values):
    per = LANES // (HALF // 2)
    count = values.shape[0] // per
    left = jnp.concatenate(
        [jnp.concatenate([values[per * p + g] for g in range(per)], axis=1) for p in range(count)], axis=0
    )

    def place(row, col):
        lane = row % LANES
        return (lane < HALF) & (lane % 2 == 0) & (col == (row // LANES) * (HALF // 2) + lane // 2)

    packed = exact_dot(left, one_hot((per * LANES, LANES), place))
    layers = values.shape[1]
    return [packed[p * layers : (p + 1) * layers] for p in range(count)]


def cut_kernel(rows, place_ref, source, coefficient, own, send_a, send_b):
    layers = own.shape[2]
    pick = [pl.ds(r, layers, stride=rows) for r in range(rows)]
    left = jnp.concatenate(
        [jnp.concatenate([source[at, :], coefficient[at, :]], axis=1) for at in pick], axis=0
    )

    def place(row, col):
        y = row % LANES
        return col == (row // LANES) * LANES + (y % 2) * HALF + y // 2

    sorted_y = exact_dot(left, one_hot((2 * LANES, 2 * LANES), place))
    for which in range(2):
        part = sorted_y[:, which * LANES : (which + 1) * LANES]
        own[:, which] = part.reshape(rows, layers, LANES)
    even_x = place_ref[0] == 0
    send_a[...] = own[pl.ds(jnp.where(even_x, rows - HALO, 0), HALO)]
    send_b[...] = own[pl.ds(jnp.where(even_x, 0, rows - HALO), HALO)]


RIGHT_SLOT = (0, 2, 1, 3)
LEFT_SLOT = (3, 5, 4, 6)


def pack_kernel(rows, place_ref, own, recv_a, recv_b, ext, send_a, send_b):
    even_x, even_y = place_ref[0] == 0, place_ref[1] == 0
    half = send_a.shape[0]
    ext[pl.ds(HALO, rows)] = own[...]
    a, b = recv_a[...], recv_b[...]
    ext[pl.ds(0, HALO)] = jnp.where(even_x, b, a)
    ext[pl.ds(HALO + rows, HALO)] = jnp.where(even_x, a, b)

    def body(at, size):
        parts = [ext[pl.ds(at + h * half, size), which] for which in range(2) for h in range(2)]
        slot = (iota_of(parts[0], 2) // SLOT) % 4
        first = last = None
        for g in range(4):
            right = shifted(parts[g], RIGHT_SLOT[g] * SLOT, 2)
            left = shifted(parts[g], (LEFT_SLOT[g] - 3) * SLOT, 2)
            first = right if g == 0 else jnp.where(slot == RIGHT_SLOT[g] % 4, right, first)
            last = left if g == 0 else jnp.where(slot == LEFT_SLOT[g] % 4, left, last)
        send_a[pl.ds(at, size)] = jnp.where(even_y, last, first)
        send_b[pl.ds(at, size)] = jnp.where(even_y, first, last)

    rows_loop(0, half, 8, body)


def descend_kernel(
    rows, place_ref, ext, recv_a, recv_b, fine_u, fine_g, fine_co, mid_v, mid_g, mid_co, packed, s_ref, k_ref, k1
):
    even_y = place_ref[1] == 0
    half = recv_a.shape[0]
    h0, h1, m = HALO, HALO // 2, rows // 2

    def widen(at, size):
        a, b = recv_a[pl.ds(at, size)], recv_b[pl.ds(at, size)]
        right, left = jnp.where(even_y, a, b), jnp.where(even_y, b, a)
        lane = iota_of(right, 2)
        odd_slot = (lane // SLOT) % 2 == 1
        merged = (jnp.where(odd_slot, left, right), jnp.where(odd_slot, right, left))
        for which, wide in enumerate((s_ref, k_ref)):
            for h in range(2):
                here = pl.ds(at + h * half, size)
                slot = RIGHT_SLOT[2 * which + h]
                inner = ext[here, which]
                wide[here, 0] = jnp.where(lane < HALF, inner, shifted(merged[which], HALF - slot * SLOT, 2))
                wide[here, 1] = jnp.where(lane < HALF, shifted(inner, HALF, 2), shifted(merged[which], -slot * SLOT, 2))

    rows_loop(0, half, 8, widen)

    def coarser(at, size):
        here = pl.ds(2 * at, 2 * size)
        k1[pl.ds(at, size)] = 0.25 * pair_sum_rows(k_ref[here, 0] + k_ref[here, 1])

    rows_loop(0, half, 20, coarser)
    fine_coefficients(k_ref, s_ref, fine_co, fine_g, h0 - 22, h0 + rows + 22, 8)
    mid_coefficients(k1, mid_co, h1 - 10, h1 + m + 10, 12)
    descend(rows, fine_g, fine_u, fine_g, fine_co, mid_v, mid_g, mid_co, 10, packed)
    k2 = 0.25 * pair_sum_lanes(pair_sum_rows(k1[pl.ds(h1, m)]))
    packed[2], packed[3] = coarse_rows(k2)


def descend(rows, fine_first, fine_u, fine_g, fine_co, mid_v, mid_g, mid_co, reach, packed):
    h0, h1, m = HALO, HALO // 2, rows // 2
    sweep_fine(fine_first, fine_u, fine_co, fine_g, h0 - 2 * reach - 1, h0 + rows + 2 * reach + 1)

    def down(at, size):
        v, new = swept_fine(fine_u, fine_co, fine_g, 2 * at, 2 * size)
        here = pl.ds(2 * at, 2 * size)
        left = fine_co[BACK, here, 0] * (new[0] - v[0]) + fine_co[BACK, here, 1] * (new[1] - v[1])
        mid_g[pl.ds(at, size)] = mid_co[INV, pl.ds(at, size)] * pair_sum_rows(left)

    rows_loop(h1 - reach, h1 + m + reach, FINE_CHUNK // 2, down)
    sweep(mid_g, mid_v, mid_co, mid_g, h1 - reach + 1, h1 + m + reach - 1)
    v, new = swept(mid_v, mid_co, mid_g, h1, m)
    left = mid_co[BACK, pl.ds(h1, m)] * (new - v)
    packed[0], packed[1] = coarse_rows(pair_sum_lanes(pair_sum_rows(left)))


def unpack(gathered, base, target, scale, npx, npy, block):
    per = 4
    width = LANES // per
    group_of = 4 if npx % 4 == 0 else 1

    def body(step, carry):
        for i in range(group_of):
            ix = step * group_of + i
            for p in range(block // per):
                for q in range(npy // per):
                    parts = [gathered[ix * npy + per * q + j, base + p] for j in range(per)]
                    group = iota_of(parts[0], 1) // width
                    for g in range(per):
                        row = shifted(parts[0], -g * width, 1)
                        for j in range(1, per):
                            row = jnp.where(group == j, shifted(parts[j], (j - g) * width, 1), row)
                        at = PAD + ix * block + per * p + g
                        lanes = pl.ds(q * LANES, LANES)
                        if scale is not None:
                            row = row * scale[INV, at, :, lanes]
                        target[at, :, lanes] = row
        return carry

    lax.fori_loop(0, npx // group_of, body, 0)


def coarse_coefficients(rows2, strips_ref, k2, co, sums):
    width = k2.shape[2]

    def body(at, size):
        k = k2[pl.ds(at, size)]
        lane = iota_of(k, 2)
        open_s, open_n = lane > 0, lane < width - 1
        found = weights(
            k, k2[pl.ds(at - 1, size)], k2[pl.ds(at + 1, size)],
            jnp.where(open_s, shifted(k, 1, 2), 0.0), jnp.where(open_n, shifted(k, -1, 2), 0.0), 16.0 * z_coupling,
        )
        found[S] = jnp.where(open_s, found[S], 0.0)
        found[N] = jnp.where(open_n, found[N], 0.0)
        for which in range(INV + 1):
            co[which, pl.ds(at, size)] = found[which]

    rows_loop(PAD, PAD + rows2, 16, body)
    zero = jnp.zeros(k2.shape[1:], F32)

    def strip(index, start):
        end = start + strips_ref[index]
        co[W, start] = zero
        co[E, end - 1] = zero
        sums[index] = lax.fori_loop(start, end, lambda r, total: total + co[BACK, r], zero)
        return end

    lax.fori_loop(0, strips_ref.shape[0], strip, PAD)
    total = jnp.sum(jnp.sum(sums[...], axis=2, keepdims=True), axis=1, keepdims=True)
    sums[...] = jnp.broadcast_to(relaxation * total, sums.shape)


def coarse_solve(rows, rows2, place_ref, strips_ref, co, sums, g, a, b, over, reach):
    zero = jnp.zeros(g.shape[1:], F32)
    for ref in (g, a, b):
        ref[PAD - 1] = zero
        ref[PAD + rows2] = zero
    for r in range(PAD - 1):
        b[r] = zero
        b[PAD + rows2 + 1 + r] = zero
    at = g
    for index in range(COARSE_SWEEPS - 1):
        to = b if index % 2 == 0 else a
        sweep(at, to, co, g, PAD, PAD + rows2)
        at = to

    def left(first, size):
        v, new = swept(b, co, g, first, size)
        a[pl.ds(first, size)] = co[BACK, pl.ds(first, size)] * (new - v)

    rows_loop(PAD, PAD + rows2, CHUNK, left)
    count = strips_ref.shape[0]

    def strip(index, start):
        end = start + strips_ref[index]
        over[index] = lax.fori_loop(start, end, lambda r, total: total + a[r], zero)
        return end

    lax.fori_loop(0, count, strip, PAD)
    total = jnp.sum(jnp.sum(over[...], axis=2, keepdims=True), axis=1, keepdims=True)
    over[...] = total / sums[...]
    block = rows // 4
    first = PAD + place_ref[2] * block - reach
    final = first + block + 2 * reach

    def shift(index, start):
        end = start + strips_ref[index]
        amount = over[index]

        def row(r, carry):
            b[r] = b[r] + amount
            return carry

        lax.fori_loop(jnp.maximum(start, first), jnp.minimum(end, final), row, 0)
        return end

    lax.fori_loop(0, count, shift, PAD)


def correct(rows, place_ref, e2, mid_v, target, reach):
    h1, m = HALO // 2, rows // 2
    low = -(-reach // 2)
    block = rows // 4
    layers, width = e2.shape[1:]
    span = block + 2 * low
    window = e2[pl.ds(place_ref[2] * block + PAD - low, span)]
    first = place_ref[3] * (HALF // 2)

    def place(row, col):
        from_own = jnp.where(col >= LANES - SLOT, col - LANES, col)
        used = (col < HALF + SLOT) | (col >= LANES - SLOT)
        return used & (row == (from_own + LANES) // 2 - HALF + first)

    spread = exact_dot(window.reshape(span * layers, width), one_hot((width, LANES), place))
    spread = spread.reshape(span, layers, LANES)
    wide = jnp.broadcast_to(spread[:, None], (span, 2, layers, LANES)).reshape(2 * span, layers, LANES)
    start = (h1 - reach) - 2 * (h1 // 2 - low)
    here = pl.ds(h1 - reach, m + 2 * reach)
    target[here] = mid_v[here] + wide[start : start + m + 2 * reach]


def ascend(rows, reach, fine_reach, mid_a, mid_b, mid_co, mid_g, fine_u, fine_a, fine_b, fine_co, fine_g):
    h0, h1, m = HALO, HALO // 2, rows // 2
    sweep(mid_a, mid_b, mid_co, mid_g, h1 - reach + 1, h1 + m + reach - 1)
    sweep(mid_b, mid_a, mid_co, mid_g, h1 - reach + 2, h1 + m + reach - 2)

    def add(at, size):
        fine = fine_u[pl.ds(2 * at, 2 * size)]
        both = fine.reshape((size, 2) + fine.shape[1:]) + mid_a[pl.ds(at, size)][:, None, None]
        fine_a[pl.ds(2 * at, 2 * size)] = both.reshape(fine.shape)

    rows_loop(h1 - reach + 2, h1 + m + reach - 2, 10, add)
    sweep_fine(fine_a, fine_b, fine_co, fine_g, h0 - fine_reach - 1, h0 + rows + fine_reach + 1)
    sweep_fine(fine_b, fine_a, fine_co, fine_g, h0 - fine_reach, h0 + rows + fine_reach)


def middle_kernel(
    rows, npx, npy, place_ref, strips_ref, gathered, fine_u, fine_g, fine_co, mid_v, mid_g, mid_co,
    fine_out, mid_v_out, mid_g_out, packed, low_co, sums,
    k2, g2, a2, b2, over, va, vb, fa, fb,
):
    block = rows // 4
    rows2 = npx * block
    zero = jnp.zeros(k2.shape[1:], F32)
    k2[PAD - 1] = zero
    k2[PAD + rows2] = zero
    unpack(gathered, 2, k2, None, npx, npy, block)
    coarse_coefficients(rows2, strips_ref, k2, low_co, sums)
    unpack(gathered, 0, g2, low_co, npx, npy, block)
    coarse_solve(rows, rows2, place_ref, strips_ref, low_co, sums, g2, a2, b2, over, 5)
    correct(rows, place_ref, b2, mid_v, va, 9)
    ascend(rows, 9, 11, va, vb, mid_co, mid_g, fine_u, fa, fb, fine_co, fine_g)
    sweep_fine(fa, fb, fine_co, fine_g, HALO - 10, HALO + rows + 10)
    descend(rows, fb, fine_out, fine_g, fine_co, mid_v_out, mid_g_out, mid_co, 4, packed)


def last_kernel(
    rows, npx, npy, place_ref, strips_ref, gathered, fine_u, fine_g, fine_co, mid_v, mid_g, mid_co, low_co, sums,
    out, g2, a2, b2, over, va, vb, fa, fb,
):
    block = rows // 4
    rows2 = npx * block
    unpack(gathered, 0, g2, low_co, npx, npy, block)
    coarse_solve(rows, rows2, place_ref, strips_ref, low_co, sums, g2, a2, b2, over, 2)
    correct(rows, place_ref, b2, mid_v, va, 3)
    ascend(rows, 3, 0, va, vb, mid_co, mid_g, fine_u, fa, fb, fine_co, fine_g)
    layers = fa.shape[2]
    here = pl.ds(HALO, rows)
    even, odd = fa[here, 0], fa[here, 1]
    both = jnp.where(iota_of(even, 2) < HALF, even, shifted(odd, HALF, 2))

    def place(row, col):
        return col == 2 * (row % HALF) + row // HALF

    natural = exact_dot(both.reshape(rows * layers, LANES), one_hot((LANES, LANES), place))
    for r in range(rows):
        out[pl.ds(r, layers, stride=rows), :] = natural[r * layers : (r + 1) * layers]


def neighbour_swaps(axis, send_a, send_b):
    count = lax.axis_size(axis)
    a = [(i, i ^ 1) for i in range(count)]
    b = [(i, ((i + 1) ^ 1) - 1) for i in range(1, count - 1)]
    return lax.ppermute(send_a, axis, a), lax.ppermute(send_b, axis, b)


def arr(*shape):
    return jax.ShapeDtypeStruct(shape, F32)


def shards(source, coefficient, strip_rows):
    npx, npy = lax.axis_size("px"), lax.axis_size("py")
    layers, rows, _ = source.shape
    total, mids = rows + 2 * HALO, (rows + 2 * HALO) // 2
    rows2, width2 = npx * rows // 4, npy * LANES // 4
    px, py = lax.axis_index("px"), lax.axis_index("py")
    place = jnp.stack([px % 2, py % 2, px, py]).astype(jnp.int32)
    fine, mid = arr(total, 2, layers, LANES), arr(mids, layers, LANES)
    low, strip_sums = arr(rows2 + 2 * PAD, layers, width2), arr(strip_rows.shape[0], layers, width2)
    fine_cos, mid_cos, low_cos = (arr(n, *item.shape) for n, item in ((7, fine), (8, mid), (8, low)))
    halo = arr(HALO, 2, layers, LANES)
    columns = arr(mids, layers, LANES)
    room = min(48, 12 + 24 * rows2 * layers * width2 * 4 // 2**20)

    def call(body, name, smem, vmem, out_shape, scratch):
        return pl.pallas_call(
            functools.partial(body, rows),
            out_shape=out_shape,
            in_specs=[SMEM] * smem + [VMEM] * vmem,
            out_specs=jax.tree.map(lambda _: VMEM, out_shape),
            scratch_shapes=[pltpu.VMEM(item.shape, F32) for item in scratch],
            compiler_params=pltpu.CompilerParams(vmem_limit_bytes=room * 2**20),
            name=name,
        )

    own, send_a, send_b = call(cut_kernel, "cut", 1, 2, (arr(rows, 2, layers, LANES), halo, halo), ())(
        place, source.reshape(layers * rows, LANES), coefficient.reshape(layers * rows, LANES)
    )
    recv_a, recv_b = neighbour_swaps("px", send_a, send_b)
    ext, send_a, send_b = call(pack_kernel, "pack", 1, 3, (arr(total, 2, layers, LANES), columns, columns), ())(
        place, own, recv_a, recv_b
    )
    recv_a, recv_b = neighbour_swaps("py", send_a, send_b)
    fine_u, fine_g, fine_co, mid_v, mid_g, mid_co, packed = call(
        descend_kernel, "descend", 1, 3, (fine, fine, fine_cos, mid, mid, mid_cos, arr(4, layers, LANES)),
        (fine, fine, mid),
    )(place, ext, recv_a, recv_b)

    def gather(block):
        every = jnp.broadcast_to(block[None], (npx * npy,) + block.shape)
        return lax.all_to_all(every, ("px", "py"), 0, 0, tiled=True)

    def sized(body):
        return lambda rows, *refs: body(rows, npx, npy, *refs)

    fine_u, mid_v, mid_g, packed, low_co, sums = call(
        sized(middle_kernel), "middle", 2, 7, (fine, mid, mid, arr(2, layers, LANES), low_cos, strip_sums),
        (low, low, low, low, strip_sums, mid, mid, fine, fine),
    )(place, strip_rows, gather(packed), fine_u, fine_g, fine_co, mid_v, mid_g, mid_co)
    out = call(
        sized(last_kernel), "last", 2, 9, arr(layers * rows, LANES),
        (low, low, low, strip_sums, mid, mid, fine, fine),
    )(place, strip_rows, gather(packed), fine_u, fine_g, fine_co, mid_v, mid_g, mid_co, low_co, sums)
    return out.reshape(source.shape)


def solution(mesh):
    placed = (P(None, "px", "py"), P(None, "px", "py"), P())
    return jax.shard_map(
        shards, mesh=mesh, in_specs=placed, out_specs=P(None, "px", "py"), check_vma=False
    )
```

```python
import functools

import jax
import jax.numpy as jnp
from jax import lax
from jax.experimental import pallas as pl
from jax.experimental.pallas import tpu as pltpu
from jax.sharding import PartitionSpec as P

COARSE_SWEEPS = 6
relaxation = 0.8
z_coupling = 0.25

HALO = 24
SIDE = 32
PAD = 8
LANES = 128
HALF = LANES // 2
SLOT = SIDE // 2
VMEM = pl.BlockSpec(memory_space=pltpu.VMEM)
SMEM = pl.BlockSpec(memory_space=pltpu.SMEM)
F32 = jnp.float32


def shifted(values, amount, axis):
    return pltpu.roll(values, amount % values.shape[axis], axis)


def iota_of(values, axis):
    return lax.broadcasted_iota(jnp.int32, values.shape, axis % values.ndim)


def rows_loop(low, high, chunk, body):
    chunk = min(chunk, high - low)
    count = -(-(high - low) // chunk)
    chunk = -(-(high - low) // count)

    def step(index, carry):
        body(jnp.minimum(low + index * chunk, high - chunk), chunk)
        return carry

    if count == 1:
        body(low, chunk)
    else:
        lax.fori_loop(0, count, step, 0)


def pair_sum_rows(values):
    count = values.shape[0] // 2
    pairs = values.reshape((count, 2) + values.shape[1:])
    return pairs[:, 0] + pairs[:, 1]


def pair_sum_lanes(values):
    return values + jnp.where(iota_of(values, -1) % 2 == 0, shifted(values, -1, 2), shifted(values, 1, 2))


def exact_dot(left, right):
    return lax.dot_general(
        left, right, (((1,), (0,)), ((), ())), precision=lax.Precision.HIGHEST, preferred_element_type=F32
    )


def one_hot(shape, place):
    row = lax.broadcasted_iota(jnp.int32, shape, 0)
    col = lax.broadcasted_iota(jnp.int32, shape, 1)
    return jnp.where(place(row, col), 1.0, 0.0).astype(F32)


W, E, S, N, D, U, BACK, INV = range(8)


def weights(k, west, east, south, north, z_factor):
    layer = iota_of(k, -2)
    west, east, south, north = (0.5 * (k + other) for other in (west, east, south, north))
    half = 0.5 * z_factor
    axis = k.ndim - 2
    down = jnp.where(layer == 0, 0.0, half * (k + shifted(k, 1, axis)))
    up = jnp.where(layer == k.shape[axis] - 1, 0.0, half * (k + shifted(k, -1, axis)))
    diagonal = west + east + south + north + down + up
    inside = k > 0.0
    inverse = jnp.where(inside, relaxation / jnp.where(inside, diagonal, 1.0), 0.0)
    scaled = [inverse * face for face in (west, east, south, north, down, up)]
    return scaled + [(1.0 / relaxation) * diagonal, inverse]


def fine_coefficients(k_ref, s_ref, co, g_ref, low, high, chunk):
    def body(at, size):
        here, before, after = pl.ds(at, size), pl.ds(at - 1, size), pl.ds(at + 1, size)
        k = [k_ref[here, s] for s in range(2)]
        sides = ((shifted(k[1], 1, 2), k[1]), (k[0], shifted(k[0], -1, 2)))
        for s in range(2):
            found = weights(k[s], k_ref[before, s], k_ref[after, s], *sides[s], z_coupling)
            for which in range(INV):
                co[which, here, s] = found[which]
            g_ref[here, s] = found[INV] * s_ref[here, s]

    rows_loop(low, high, chunk, body)


def mid_coefficients(k_ref, co, low, high, chunk):
    def body(at, size):
        here = pl.ds(at, size)
        k = k_ref[here]
        found = weights(
            k, k_ref[pl.ds(at - 1, size)], k_ref[pl.ds(at + 1, size)], shifted(k, 1, 2), shifted(k, -1, 2),
            4.0 * z_coupling,
        )
        for which in range(INV + 1):
            co[which, here] = found[which]

    rows_loop(low, high, chunk, body)


def swept_fine(v_ref, co, g_ref, at, size):
    here, before, after = pl.ds(at, size), pl.ds(at - 1, size), pl.ds(at + 1, size)
    v = [v_ref[here, s] for s in range(2)]
    sides = ((shifted(v[1], 1, 2), v[1]), (v[0], shifted(v[0], -1, 2)))
    new = []
    for s in range(2):
        total = g_ref[here, s] + (1.0 - relaxation) * v[s]
        total = total + co[W, here, s] * v_ref[before, s]
        total = total + co[E, here, s] * v_ref[after, s]
        total = total + co[D, here, s] * shifted(v[s], 1, 1)
        total = total + co[U, here, s] * shifted(v[s], -1, 1)
        total = total + co[S, here, s] * sides[s][0]
        total = total + co[N, here, s] * sides[s][1]
        new.append(total)
    return v, new


def swept(v_ref, co, g_ref, at, size):
    here = pl.ds(at, size)
    v = v_ref[here]
    total = g_ref[here] + (1.0 - relaxation) * v
    total = total + co[W, here] * v_ref[pl.ds(at - 1, size)]
    total = total + co[E, here] * v_ref[pl.ds(at + 1, size)]
    total = total + co[D, here] * shifted(v, 1, 1)
    total = total + co[U, here] * shifted(v, -1, 1)
    total = total + co[S, here] * shifted(v, 1, 2)
    total = total + co[N, here] * shifted(v, -1, 2)
    return v, total


def sweep_fine(v_ref, out_ref, co, g_ref, low, high):
    def body(at, size):
        new = swept_fine(v_ref, co, g_ref, at, size)[1]
        for s in range(2):
            out_ref[pl.ds(at, size), s] = new[s]

    rows_loop(low, high, FINE_CHUNK, body)


def sweep(v_ref, out_ref, co, g_ref, low, high):
    def body(at, size):
        out_ref[pl.ds(at, size)] = swept(v_ref, co, g_ref, at, size)[1]

    rows_loop(low, high, CHUNK, body)


FINE_CHUNK = 16
CHUNK = 32


def coarse_rows(values):
    per = LANES // (HALF // 2)
    count = values.shape[0] // per
    left = jnp.concatenate(
        [jnp.concatenate([values[per * p + g] for g in range(per)], axis=1) for p in range(count)], axis=0
    )

    def place(row, col):
        lane = row % LANES
        return (lane < HALF) & (lane % 2 == 0) & (col == (row // LANES) * (HALF // 2) + lane // 2)

    packed = exact_dot(left, one_hot((per * LANES, LANES), place))
    layers = values.shape[1]
    return [packed[p * layers : (p + 1) * layers] for p in range(count)]


def cut_kernel(rows, place_ref, source_far, coefficient_far, own, send_a, send_b, source, coefficient, arrived):
    layers = own.shape[2]
    copies = [
        pltpu.make_async_copy(far, near, arrived.at[i])
        for i, (far, near) in enumerate(((source_far, source), (coefficient_far, coefficient)))
    ]
    for copy in copies:
        copy.start()
    for copy in copies:
        copy.wait()
    pick = [pl.ds(r, layers, stride=rows) for r in range(rows)]
    left = jnp.concatenate(
        [jnp.concatenate([source[at, :], coefficient[at, :]], axis=1) for at in pick], axis=0
    )

    def place(row, col):
        y = row % LANES
        return col == (row // LANES) * LANES + (y % 2) * HALF + y // 2

    sorted_y = exact_dot(left, one_hot((2 * LANES, 2 * LANES), place))
    for which in range(2):
        part = sorted_y[:, which * LANES : (which + 1) * LANES]
        own[:, which] = part.reshape(rows, layers, LANES)
    even_x = place_ref[0] == 0
    send_a[...] = own[pl.ds(jnp.where(even_x, rows - HALO, 0), HALO)]
    send_b[...] = own[pl.ds(jnp.where(even_x, 0, rows - HALO), HALO)]


RIGHT_SLOT = (0, 2, 1, 3)
LEFT_SLOT = (3, 5, 4, 6)


def pack_kernel(rows, place_ref, own, recv_a, recv_b, ext, send_a, send_b):
    even_x, even_y = place_ref[0] == 0, place_ref[1] == 0
    half = send_a.shape[0]
    ext[pl.ds(HALO, rows)] = own[...]
    a, b = recv_a[...], recv_b[...]
    ext[pl.ds(0, HALO)] = jnp.where(even_x, b, a)
    ext[pl.ds(HALO + rows, HALO)] = jnp.where(even_x, a, b)

    def body(at, size):
        parts = [ext[pl.ds(at + h * half, size), which] for which in range(2) for h in range(2)]
        slot = (iota_of(parts[0], 2) // SLOT) % 4
        first = last = None
        for g in range(4):
            right = shifted(parts[g], RIGHT_SLOT[g] * SLOT, 2)
            left = shifted(parts[g], (LEFT_SLOT[g] - 3) * SLOT, 2)
            first = right if g == 0 else jnp.where(slot == RIGHT_SLOT[g] % 4, right, first)
            last = left if g == 0 else jnp.where(slot == LEFT_SLOT[g] % 4, left, last)
        send_a[pl.ds(at, size)] = jnp.where(even_y, last, first)
        send_b[pl.ds(at, size)] = jnp.where(even_y, first, last)

    rows_loop(0, half, 8, body)


def descend_kernel(
    rows, place_ref, ext, recv_a, recv_b, fine_u, fine_g, fine_co, mid_v, mid_g, mid_co, packed, s_ref, k_ref, k1
):
    even_y = place_ref[1] == 0
    half = recv_a.shape[0]
    h0, h1, m = HALO, HALO // 2, rows // 2

    def widen(at, size):
        a, b = recv_a[pl.ds(at, size)], recv_b[pl.ds(at, size)]
        right, left = jnp.where(even_y, a, b), jnp.where(even_y, b, a)
        lane = iota_of(right, 2)
        odd_slot = (lane // SLOT) % 2 == 1
        merged = (jnp.where(odd_slot, left, right), jnp.where(odd_slot, right, left))
        for which, wide in enumerate((s_ref, k_ref)):
            for h in range(2):
                here = pl.ds(at + h * half, size)
                slot = RIGHT_SLOT[2 * which + h]
                inner = ext[here, which]
                wide[here, 0] = jnp.where(lane < HALF, inner, shifted(merged[which], HALF - slot * SLOT, 2))
                wide[here, 1] = jnp.where(lane < HALF, shifted(inner, HALF, 2), shifted(merged[which], -slot * SLOT, 2))

    rows_loop(0, half, 8, widen)

    def coarser(at, size):
        here = pl.ds(2 * at, 2 * size)
        k1[pl.ds(at, size)] = 0.25 * pair_sum_rows(k_ref[here, 0] + k_ref[here, 1])

    rows_loop(0, half, 20, coarser)
    fine_coefficients(k_ref, s_ref, fine_co, fine_g, h0 - 22, h0 + rows + 22, 8)
    mid_coefficients(k1, mid_co, h1 - 10, h1 + m + 10, 12)
    descend(rows, fine_g, fine_u, fine_g, fine_co, mid_v, mid_g, mid_co, 10, packed)
    k2 = 0.25 * pair_sum_lanes(pair_sum_rows(k1[pl.ds(h1, m)]))
    for p, part in enumerate(coarse_rows(k2)):
        packed[p, 1] = part


def descend(rows, fine_first, fine_u, fine_g, fine_co, mid_v, mid_g, mid_co, reach, packed):
    h0, h1, m = HALO, HALO // 2, rows // 2
    sweep_fine(fine_first, fine_u, fine_co, fine_g, h0 - 2 * reach - 1, h0 + rows + 2 * reach + 1)

    def down(at, size):
        v, new = swept_fine(fine_u, fine_co, fine_g, 2 * at, 2 * size)
        here = pl.ds(2 * at, 2 * size)
        left = fine_co[BACK, here, 0] * (new[0] - v[0]) + fine_co[BACK, here, 1] * (new[1] - v[1])
        mid_g[pl.ds(at, size)] = mid_co[INV, pl.ds(at, size)] * pair_sum_rows(left)

    rows_loop(h1 - reach, h1 + m + reach, FINE_CHUNK // 2, down)
    sweep(mid_g, mid_v, mid_co, mid_g, h1 - reach + 1, h1 + m + reach - 1)
    v, new = swept(mid_v, mid_co, mid_g, h1, m)
    left = mid_co[BACK, pl.ds(h1, m)] * (new - v)
    for p, part in enumerate(coarse_rows(pair_sum_lanes(pair_sum_rows(left)))):
        packed[p, 0] = part


def unpack(place_ref, mine, other, which, target, scale, npx, npy, block):
    even_x = place_ref[0] == 0
    per = 4
    width = LANES // per
    group_of = 4 if npx % 4 == 0 else 1

    def body(step, carry):
        for i in range(group_of):
            ix = step * group_of + i
            for p in range(block // per):
                for q in range(npy // per):
                    devices = [ix * npy + per * q + j for j in range(per)]
                    here = even_x if p == 0 else jnp.logical_not(even_x)
                    parts = [jnp.where(here, mine[i, which], other[i, which]) for i in devices]
                    group = iota_of(parts[0], 1) // width
                    for g in range(per):
                        row = shifted(parts[0], -g * width, 1)
                        for j in range(1, per):
                            row = jnp.where(group == j, shifted(parts[j], (j - g) * width, 1), row)
                        at = PAD + ix * block + per * p + g
                        lanes = pl.ds(q * LANES, LANES)
                        if scale is not None:
                            row = row * scale[INV, at, :, lanes]
                        target[at, :, lanes] = row
        return carry

    lax.fori_loop(0, npx // group_of, body, 0)


def coarse_coefficients(rows2, strips_ref, k2, co, sums):
    width = k2.shape[2]

    def body(at, size):
        k = k2[pl.ds(at, size)]
        lane = iota_of(k, 2)
        open_s, open_n = lane > 0, lane < width - 1
        found = weights(
            k, k2[pl.ds(at - 1, size)], k2[pl.ds(at + 1, size)],
            jnp.where(open_s, shifted(k, 1, 2), 0.0), jnp.where(open_n, shifted(k, -1, 2), 0.0), 16.0 * z_coupling,
        )
        found[S] = jnp.where(open_s, found[S], 0.0)
        found[N] = jnp.where(open_n, found[N], 0.0)
        for which in range(INV + 1):
            co[which, pl.ds(at, size)] = found[which]

    rows_loop(PAD, PAD + rows2, 16, body)
    zero = jnp.zeros(k2.shape[1:], F32)

    def strip(index, start):
        end = start + strips_ref[index]
        co[W, start] = zero
        co[E, end - 1] = zero
        sums[index] = lax.fori_loop(start, end, lambda r, total: total + co[BACK, r], zero)
        return end

    lax.fori_loop(0, strips_ref.shape[0], strip, PAD)
    total = jnp.sum(jnp.sum(sums[...], axis=2, keepdims=True), axis=1, keepdims=True)
    sums[...] = jnp.broadcast_to(relaxation * total, sums.shape)


def coarse_solve(rows, rows2, place_ref, strips_ref, co, sums, g, a, b, over, reach):
    zero = jnp.zeros(g.shape[1:], F32)
    for ref in (g, a, b):
        ref[PAD - 1] = zero
        ref[PAD + rows2] = zero
    for r in range(PAD - 1):
        b[r] = zero
        b[PAD + rows2 + 1 + r] = zero
    at = g
    for index in range(COARSE_SWEEPS - 1):
        to = b if index % 2 == 0 else a
        sweep(at, to, co, g, PAD, PAD + rows2)
        at = to

    def left(first, size):
        v, new = swept(b, co, g, first, size)
        a[pl.ds(first, size)] = co[BACK, pl.ds(first, size)] * (new - v)

    rows_loop(PAD, PAD + rows2, CHUNK, left)
    count = strips_ref.shape[0]

    def strip(index, start):
        end = start + strips_ref[index]
        over[index] = lax.fori_loop(start, end, lambda r, total: total + a[r], zero)
        return end

    lax.fori_loop(0, count, strip, PAD)
    total = jnp.sum(jnp.sum(over[...], axis=2, keepdims=True), axis=1, keepdims=True)
    over[...] = total / sums[...]
    block = rows // 4
    first = PAD + place_ref[2] * block - reach
    final = first + block + 2 * reach

    def shift(index, start):
        end = start + strips_ref[index]
        amount = over[index]

        def row(r, carry):
            b[r] = b[r] + amount
            return carry

        lax.fori_loop(jnp.maximum(start, first), jnp.minimum(end, final), row, 0)
        return end

    lax.fori_loop(0, count, shift, PAD)


def correct(rows, place_ref, e2, mid_v, target, reach):
    h1, m = HALO // 2, rows // 2
    low = -(-reach // 2)
    block = rows // 4
    layers, width = e2.shape[1:]
    span = block + 2 * low
    window = e2[pl.ds(place_ref[2] * block + PAD - low, span)]
    first = place_ref[3] * (HALF // 2)

    def place(row, col):
        from_own = jnp.where(col >= LANES - SLOT, col - LANES, col)
        used = (col < HALF + SLOT) | (col >= LANES - SLOT)
        return used & (row == (from_own + LANES) // 2 - HALF + first)

    spread = exact_dot(window.reshape(span * layers, width), one_hot((width, LANES), place))
    spread = spread.reshape(span, layers, LANES)
    wide = jnp.broadcast_to(spread[:, None], (span, 2, layers, LANES)).reshape(2 * span, layers, LANES)
    start = (h1 - reach) - 2 * (h1 // 2 - low)
    here = pl.ds(h1 - reach, m + 2 * reach)
    target[here] = mid_v[here] + wide[start : start + m + 2 * reach]


def ascend(rows, reach, fine_reach, mid_a, mid_b, mid_co, mid_g, fine_u, fine_a, fine_b, fine_co, fine_g):
    h0, h1, m = HALO, HALO // 2, rows // 2
    sweep(mid_a, mid_b, mid_co, mid_g, h1 - reach + 1, h1 + m + reach - 1)
    sweep(mid_b, mid_a, mid_co, mid_g, h1 - reach + 2, h1 + m + reach - 2)

    def add(at, size):
        fine = fine_u[pl.ds(2 * at, 2 * size)]
        both = fine.reshape((size, 2) + fine.shape[1:]) + mid_a[pl.ds(at, size)][:, None, None]
        fine_a[pl.ds(2 * at, 2 * size)] = both.reshape(fine.shape)

    rows_loop(h1 - reach + 2, h1 + m + reach - 2, 10, add)
    sweep_fine(fine_a, fine_b, fine_co, fine_g, h0 - fine_reach - 1, h0 + rows + fine_reach + 1)
    sweep_fine(fine_b, fine_a, fine_co, fine_g, h0 - fine_reach, h0 + rows + fine_reach)


def middle_kernel(
    rows, npx, npy, place_ref, strips_ref, mine, other, fine_u, fine_g, fine_co, mid_v, mid_g, mid_co,
    fine_out, mid_v_out, mid_g_out, packed, low_co, sums,
    k2, g2, a2, b2, over, va, vb, fa, fb,
):
    block = rows // 4
    rows2 = npx * block
    zero = jnp.zeros(k2.shape[1:], F32)
    k2[PAD - 1] = zero
    k2[PAD + rows2] = zero
    unpack(place_ref, mine, other, 1, k2, None, npx, npy, block)
    coarse_coefficients(rows2, strips_ref, k2, low_co, sums)
    unpack(place_ref, mine, other, 0, g2, low_co, npx, npy, block)
    coarse_solve(rows, rows2, place_ref, strips_ref, low_co, sums, g2, a2, b2, over, 5)
    correct(rows, place_ref, b2, mid_v, va, 9)
    ascend(rows, 9, 11, va, vb, mid_co, mid_g, fine_u, fa, fb, fine_co, fine_g)
    sweep_fine(fa, fb, fine_co, fine_g, HALO - 10, HALO + rows + 10)
    descend(rows, fb, fine_out, fine_g, fine_co, mid_v_out, mid_g_out, mid_co, 4, packed)


def last_kernel(
    rows, npx, npy, place_ref, strips_ref, mine, other, fine_u, fine_g, fine_co, mid_v, mid_g, mid_co, low_co, sums,
    out, g2, a2, b2, over, va, vb, fa, fb,
):
    block = rows // 4
    rows2 = npx * block
    unpack(place_ref, mine, other, 0, g2, low_co, npx, npy, block)
    coarse_solve(rows, rows2, place_ref, strips_ref, low_co, sums, g2, a2, b2, over, 2)
    correct(rows, place_ref, b2, mid_v, va, 3)
    ascend(rows, 3, 0, va, vb, mid_co, mid_g, fine_u, fa, fb, fine_co, fine_g)
    layers = fa.shape[2]
    here = pl.ds(HALO, rows)
    even, odd = fa[here, 0], fa[here, 1]
    both = jnp.where(iota_of(even, 2) < HALF, even, shifted(odd, HALF, 2))

    def place(row, col):
        return col == 2 * (row % HALF) + row // HALF

    natural = exact_dot(both.reshape(rows * layers, LANES), one_hot((LANES, LANES), place))
    for r in range(rows):
        out[pl.ds(r, layers, stride=rows), :] = natural[r * layers : (r + 1) * layers]


def neighbour_swaps(axis, send_a, send_b):
    count = lax.axis_size(axis)
    a = [(i, i ^ 1) for i in range(count)]
    b = [(i, ((i + 1) ^ 1) - 1) for i in range(1, count - 1)]
    return lax.ppermute(send_a, axis, a), lax.ppermute(send_b, axis, b)


def arr(*shape):
    return jax.ShapeDtypeStruct(shape, F32)


def shards(source, coefficient, strip_rows):
    npx, npy = lax.axis_size("px"), lax.axis_size("py")
    layers, rows, _ = source.shape
    total, mids = rows + 2 * HALO, (rows + 2 * HALO) // 2
    rows2, width2 = npx * rows // 4, npy * LANES // 4
    px, py = lax.axis_index("px"), lax.axis_index("py")
    place = jnp.stack([px % 2, py % 2, px, py]).astype(jnp.int32)
    fine, mid = arr(total, 2, layers, LANES), arr(mids, layers, LANES)
    low, strip_sums = arr(rows2 + 2 * PAD, layers, width2), arr(strip_rows.shape[0], layers, width2)
    fine_cos, mid_cos, low_cos = (arr(n, *item.shape) for n, item in ((7, fine), (8, mid), (8, low)))
    halo = arr(HALO, 2, layers, LANES)
    columns = arr(mids, layers, LANES)
    room = min(48, 12 + 24 * rows2 * layers * width2 * 4 // 2**20)

    def call(body, name, smem, vmem, out_shape, scratch, where=VMEM, semaphores=()):
        return pl.pallas_call(
            functools.partial(body, rows),
            out_shape=out_shape,
            in_specs=[SMEM] * smem + [where] * vmem,
            out_specs=jax.tree.map(lambda _: VMEM, out_shape),
            scratch_shapes=[pltpu.VMEM(item.shape, F32) for item in scratch] + list(semaphores),
            compiler_params=pltpu.CompilerParams(vmem_limit_bytes=room * 2**20),
            name=name,
        )

    flat = arr(layers * rows, LANES)
    own, send_a, send_b = call(
        cut_kernel, "cut", 1, 2, (arr(rows, 2, layers, LANES), halo, halo), (flat, flat),
        pl.BlockSpec(memory_space=pl.ANY), (pltpu.SemaphoreType.DMA((2,)),),
    )(place, source.reshape(flat.shape), coefficient.reshape(flat.shape))
    recv_a, recv_b = neighbour_swaps("px", send_a, send_b)
    ext, send_a, send_b = call(pack_kernel, "pack", 1, 3, (arr(total, 2, layers, LANES), columns, columns), ())(
        place, own, recv_a, recv_b
    )
    recv_a, recv_b = neighbour_swaps("py", send_a, send_b)
    fine_u, fine_g, fine_co, mid_v, mid_g, mid_co, packed = call(
        descend_kernel, "descend", 1, 3, (fine, fine, fine_cos, mid, mid, mid_cos, arr(2, 2, layers, LANES)),
        (fine, fine, mid),
    )(place, ext, recv_a, recv_b)

    def gather(block):
        shape = (npx // 2, 2, npy) + block.shape[1:]
        every = jnp.broadcast_to(block[None, :, None], shape).reshape((npx * npy,) + block.shape[1:])
        half = lax.all_to_all(every, ("px", "py"), 0, 0, tiled=True)
        return half, lax.ppermute(half, "px", [(i, i ^ 1) for i in range(npx)])

    def sized(body):
        return lambda rows, *refs: body(rows, npx, npy, *refs)

    fine_u, mid_v, mid_g, packed, low_co, sums = call(
        sized(middle_kernel), "middle", 2, 8, (fine, mid, mid, arr(2, 1, layers, LANES), low_cos, strip_sums),
        (low, low, low, low, strip_sums, mid, mid, fine, fine),
    )(place, strip_rows, *gather(packed), fine_u, fine_g, fine_co, mid_v, mid_g, mid_co)
    out = call(
        sized(last_kernel), "last", 2, 10, arr(layers * rows, LANES),
        (low, low, low, strip_sums, mid, mid, fine, fine),
    )(place, strip_rows, *gather(packed), fine_u, fine_g, fine_co, mid_v, mid_g, mid_co, low_co, sums)
    return out.reshape(source.shape)


def solution(mesh):
    placed = (P(None, "px", "py"), P(None, "px", "py"), P())
    return jax.shard_map(
        shards, mesh=mesh, in_specs=placed, out_specs=P(None, "px", "py"), check_vma=False
    )
```

```python
import functools

import jax
import jax.numpy as jnp
from jax import lax
from jax.experimental import pallas as pl
from jax.experimental.pallas import tpu as pltpu
from jax.sharding import PartitionSpec as P

COARSE_SWEEPS = 6
relaxation = 0.8
z_coupling = 0.25

HALO = 24
SIDE = 32
PAD = 8
LANES = 128
HALF = LANES // 2
SLOT = SIDE // 2
VMEM = pl.BlockSpec(memory_space=pltpu.VMEM)
SMEM = pl.BlockSpec(memory_space=pltpu.SMEM)
F32 = jnp.float32


def shifted(values, amount, axis):
    return pltpu.roll(values, amount % values.shape[axis], axis)


def iota_of(values, axis):
    return lax.broadcasted_iota(jnp.int32, values.shape, axis % values.ndim)


def rows_loop(low, high, chunk, body):
    chunk = min(chunk, high - low)
    count = -(-(high - low) // chunk)
    chunk = -(-(high - low) // count)

    def step(index, carry):
        body(jnp.minimum(low + index * chunk, high - chunk), chunk)
        return carry

    if count == 1:
        body(low, chunk)
    else:
        lax.fori_loop(0, count, step, 0)


def pair_sum_rows(values):
    count = values.shape[0] // 2
    pairs = values.reshape((count, 2) + values.shape[1:])
    return pairs[:, 0] + pairs[:, 1]


def pair_sum_lanes(values):
    return values + jnp.where(iota_of(values, -1) % 2 == 0, shifted(values, -1, 2), shifted(values, 1, 2))


def exact_dot(left, right):
    return lax.dot_general(
        left, right, (((1,), (0,)), ((), ())), precision=lax.Precision.HIGHEST, preferred_element_type=F32
    )


def one_hot(shape, place):
    row = lax.broadcasted_iota(jnp.int32, shape, 0)
    col = lax.broadcasted_iota(jnp.int32, shape, 1)
    return jnp.where(place(row, col), 1.0, 0.0).astype(F32)


W, E, S, N, D, U, BACK, INV = range(8)


def weights(k, west, east, south, north, z_factor):
    layer = iota_of(k, -2)
    west, east, south, north = (0.5 * (k + other) for other in (west, east, south, north))
    half = 0.5 * z_factor
    axis = k.ndim - 2
    down = jnp.where(layer == 0, 0.0, half * (k + shifted(k, 1, axis)))
    up = jnp.where(layer == k.shape[axis] - 1, 0.0, half * (k + shifted(k, -1, axis)))
    diagonal = west + east + south + north + down + up
    inside = k > 0.0
    inverse = jnp.where(inside, relaxation / jnp.where(inside, diagonal, 1.0), 0.0)
    scaled = [inverse * face for face in (west, east, south, north, down, up)]
    return scaled + [(1.0 / relaxation) * diagonal, inverse]


def fine_coefficients(k_ref, s_ref, co, g_ref, low, high, chunk):
    def body(at, size):
        here, before, after = pl.ds(at, size), pl.ds(at - 1, size), pl.ds(at + 1, size)
        k = [k_ref[here, s] for s in range(2)]
        sides = ((shifted(k[1], 1, 2), k[1]), (k[0], shifted(k[0], -1, 2)))
        for s in range(2):
            found = weights(k[s], k_ref[before, s], k_ref[after, s], *sides[s], z_coupling)
            for which in range(INV):
                co[which, here, s] = found[which]
            g_ref[here, s] = found[INV] * s_ref[here, s]

    rows_loop(low, high, chunk, body)


def mid_coefficients(k_ref, co, low, high, chunk):
    def body(at, size):
        here = pl.ds(at, size)
        k = k_ref[here]
        found = weights(
            k, k_ref[pl.ds(at - 1, size)], k_ref[pl.ds(at + 1, size)], shifted(k, 1, 2), shifted(k, -1, 2),
            4.0 * z_coupling,
        )
        for which in range(INV + 1):
            co[which, here] = found[which]

    rows_loop(low, high, chunk, body)


def swept_fine(v_ref, co, g_ref, at, size):
    here, before, after = pl.ds(at, size), pl.ds(at - 1, size), pl.ds(at + 1, size)
    v = [v_ref[here, s] for s in range(2)]
    sides = ((shifted(v[1], 1, 2), v[1]), (v[0], shifted(v[0], -1, 2)))
    new = []
    for s in range(2):
        total = g_ref[here, s] + (1.0 - relaxation) * v[s]
        total = total + co[W, here, s] * v_ref[before, s]
        total = total + co[E, here, s] * v_ref[after, s]
        total = total + co[D, here, s] * shifted(v[s], 1, 1)
        total = total + co[U, here, s] * shifted(v[s], -1, 1)
        total = total + co[S, here, s] * sides[s][0]
        total = total + co[N, here, s] * sides[s][1]
        new.append(total)
    return v, new


def swept(v_ref, co, g_ref, at, size):
    here = pl.ds(at, size)
    v = v_ref[here]
    total = g_ref[here] + (1.0 - relaxation) * v
    total = total + co[W, here] * v_ref[pl.ds(at - 1, size)]
    total = total + co[E, here] * v_ref[pl.ds(at + 1, size)]
    total = total + co[D, here] * shifted(v, 1, 1)
    total = total + co[U, here] * shifted(v, -1, 1)
    total = total + co[S, here] * shifted(v, 1, 2)
    total = total + co[N, here] * shifted(v, -1, 2)
    return v, total


def sweep_fine(v_ref, out_ref, co, g_ref, low, high):
    def body(at, size):
        new = swept_fine(v_ref, co, g_ref, at, size)[1]
        for s in range(2):
            out_ref[pl.ds(at, size), s] = new[s]

    rows_loop(low, high, FINE_CHUNK, body)


def sweep(v_ref, out_ref, co, g_ref, low, high):
    def body(at, size):
        out_ref[pl.ds(at, size)] = swept(v_ref, co, g_ref, at, size)[1]

    rows_loop(low, high, CHUNK, body)


FINE_CHUNK = 20
CHUNK = 64


def coarse_rows(values):
    per = LANES // (HALF // 2)
    count = values.shape[0] // per
    left = jnp.concatenate(
        [jnp.concatenate([values[per * p + g] for g in range(per)], axis=1) for p in range(count)], axis=0
    )

    def place(row, col):
        lane = row % LANES
        return (lane < HALF) & (lane % 2 == 0) & (col == (row // LANES) * (HALF // 2) + lane // 2)

    packed = exact_dot(left, one_hot((per * LANES, LANES), place))
    layers = values.shape[1]
    return [packed[p * layers : (p + 1) * layers] for p in range(count)]


def cut_kernel(rows, place_ref, source_far, coefficient_far, own, send_a, send_b, source, coefficient, arrived):
    layers = own.shape[2]
    copies = [
        pltpu.make_async_copy(far, near, arrived.at[i])
        for i, (far, near) in enumerate(((source_far, source), (coefficient_far, coefficient)))
    ]
    for copy in copies:
        copy.start()
    for copy in copies:
        copy.wait()
    pick = [pl.ds(r, layers, stride=rows) for r in range(rows)]
    left = jnp.concatenate(
        [jnp.concatenate([source[at, :], coefficient[at, :]], axis=1) for at in pick], axis=0
    )

    def place(row, col):
        y = row % LANES
        return col == (row // LANES) * LANES + (y % 2) * HALF + y // 2

    sorted_y = exact_dot(left, one_hot((2 * LANES, 2 * LANES), place))
    for which in range(2):
        part = sorted_y[:, which * LANES : (which + 1) * LANES]
        own[:, which] = part.reshape(rows, layers, LANES)
    even_x = place_ref[0] == 0
    send_a[...] = own[pl.ds(jnp.where(even_x, rows - HALO, 0), HALO)]
    send_b[...] = own[pl.ds(jnp.where(even_x, 0, rows - HALO), HALO)]


RIGHT_SLOT = (0, 2, 1, 3)
LEFT_SLOT = (3, 5, 4, 6)


def pack_kernel(rows, place_ref, own, recv_a, recv_b, ext, send_a, send_b):
    even_x, even_y = place_ref[0] == 0, place_ref[1] == 0
    half = send_a.shape[0]
    ext[pl.ds(HALO, rows)] = own[...]
    a, b = recv_a[...], jnp.where(place_ref[4] != 0, recv_b[...], 0.0)
    ext[pl.ds(0, HALO)] = jnp.where(even_x, b, a)
    ext[pl.ds(HALO + rows, HALO)] = jnp.where(even_x, a, b)

    def body(at, size):
        parts = [ext[pl.ds(at + h * half, size), which] for which in range(2) for h in range(2)]
        slot = (iota_of(parts[0], 2) // SLOT) % 4
        first = last = None
        for g in range(4):
            right = shifted(parts[g], RIGHT_SLOT[g] * SLOT, 2)
            left = shifted(parts[g], (LEFT_SLOT[g] - 3) * SLOT, 2)
            first = right if g == 0 else jnp.where(slot == RIGHT_SLOT[g] % 4, right, first)
            last = left if g == 0 else jnp.where(slot == LEFT_SLOT[g] % 4, left, last)
        send_a[pl.ds(at, size)] = jnp.where(even_y, last, first)
        send_b[pl.ds(at, size)] = jnp.where(even_y, first, last)

    rows_loop(0, half, 8, body)


def descend_kernel(
    rows, place_ref, ext, recv_a, recv_b, fine_u, fine_g, fine_co, mid_v, mid_g, mid_co, packed, s_ref, k_ref, k1
):
    even_y = place_ref[1] == 0
    half = recv_a.shape[0]
    h0, h1, m = HALO, HALO // 2, rows // 2

    def widen(at, size):
        a, b = recv_a[pl.ds(at, size)], jnp.where(place_ref[5] != 0, recv_b[pl.ds(at, size)], 0.0)
        right, left = jnp.where(even_y, a, b), jnp.where(even_y, b, a)
        lane = iota_of(right, 2)
        odd_slot = (lane // SLOT) % 2 == 1
        merged = (jnp.where(odd_slot, left, right), jnp.where(odd_slot, right, left))
        for which, wide in enumerate((s_ref, k_ref)):
            for h in range(2):
                here = pl.ds(at + h * half, size)
                slot = RIGHT_SLOT[2 * which + h]
                inner = ext[here, which]
                wide[here, 0] = jnp.where(lane < HALF, inner, shifted(merged[which], HALF - slot * SLOT, 2))
                wide[here, 1] = jnp.where(lane < HALF, shifted(inner, HALF, 2), shifted(merged[which], -slot * SLOT, 2))

    rows_loop(0, half, 8, widen)

    def coarser(at, size):
        here = pl.ds(2 * at, 2 * size)
        k1[pl.ds(at, size)] = 0.25 * pair_sum_rows(k_ref[here, 0] + k_ref[here, 1])

    rows_loop(0, half, 20, coarser)
    fine_coefficients(k_ref, s_ref, fine_co, fine_g, h0 - 22, h0 + rows + 22, 8)
    mid_coefficients(k1, mid_co, h1 - 10, h1 + m + 10, 12)
    descend(rows, fine_g, fine_u, fine_g, fine_co, mid_v, mid_g, mid_co, 10, packed)
    k2 = 0.25 * pair_sum_lanes(pair_sum_rows(k1[pl.ds(h1, m)]))
    for p, part in enumerate(coarse_rows(k2)):
        packed[p, 1] = part


def descend(rows, fine_first, fine_u, fine_g, fine_co, mid_v, mid_g, mid_co, reach, packed):
    h0, h1, m = HALO, HALO // 2, rows // 2
    sweep_fine(fine_first, fine_u, fine_co, fine_g, h0 - 2 * reach - 1, h0 + rows + 2 * reach + 1)

    def down(at, size):
        v, new = swept_fine(fine_u, fine_co, fine_g, 2 * at, 2 * size)
        here = pl.ds(2 * at, 2 * size)
        left = fine_co[BACK, here, 0] * (new[0] - v[0]) + fine_co[BACK, here, 1] * (new[1] - v[1])
        mid_g[pl.ds(at, size)] = mid_co[INV, pl.ds(at, size)] * pair_sum_rows(left)

    rows_loop(h1 - reach, h1 + m + reach, FINE_CHUNK // 2, down)
    sweep(mid_g, mid_v, mid_co, mid_g, h1 - reach + 1, h1 + m + reach - 1)
    v, new = swept(mid_v, mid_co, mid_g, h1, m)
    left = mid_co[BACK, pl.ds(h1, m)] * (new - v)
    for p, part in enumerate(coarse_rows(pair_sum_lanes(pair_sum_rows(left)))):
        packed[p, 0] = part


def unpack(place_ref, mine, other, which, target, scale, npx, npy, block):
    even_x = place_ref[0] == 0
    per = 4
    width = LANES // per
    group_of = 4 if npx % 4 == 0 else 1

    def body(step, carry):
        for i in range(group_of):
            ix = step * group_of + i
            for p in range(block // per):
                for q in range(npy // per):
                    devices = [ix * npy + per * q + j for j in range(per)]
                    here = even_x if p == 0 else jnp.logical_not(even_x)
                    parts = [jnp.where(here, mine[i, which], other[i, which]) for i in devices]
                    group = iota_of(parts[0], 1) // width
                    for g in range(per):
                        row = shifted(parts[0], -g * width, 1)
                        for j in range(1, per):
                            row = jnp.where(group == j, shifted(parts[j], (j - g) * width, 1), row)
                        at = PAD + ix * block + per * p + g
                        lanes = pl.ds(q * LANES, LANES)
                        if scale is not None:
                            row = row * scale[INV, at, :, lanes]
                        target[at, :, lanes] = row
        return carry

    lax.fori_loop(0, npx // group_of, body, 0)


def coarse_coefficients(rows2, strips_ref, k2, co, sums):
    width = k2.shape[2]

    def body(at, size):
        k = k2[pl.ds(at, size)]
        lane = iota_of(k, 2)
        open_s, open_n = lane > 0, lane < width - 1
        found = weights(
            k, k2[pl.ds(at - 1, size)], k2[pl.ds(at + 1, size)],
            jnp.where(open_s, shifted(k, 1, 2), 0.0), jnp.where(open_n, shifted(k, -1, 2), 0.0), 16.0 * z_coupling,
        )
        found[S] = jnp.where(open_s, found[S], 0.0)
        found[N] = jnp.where(open_n, found[N], 0.0)
        for which in range(INV + 1):
            co[which, pl.ds(at, size)] = found[which]

    rows_loop(PAD, PAD + rows2, 16, body)
    zero = jnp.zeros(k2.shape[1:], F32)

    def strip(index, start):
        end = start + strips_ref[index]
        co[W, start] = zero
        co[E, end - 1] = zero
        sums[index] = lax.fori_loop(start, end, lambda r, total: total + co[BACK, r], zero)
        return end

    lax.fori_loop(0, strips_ref.shape[0], strip, PAD)
    total = jnp.sum(jnp.sum(sums[...], axis=2, keepdims=True), axis=1, keepdims=True)
    sums[...] = jnp.broadcast_to(relaxation * total, sums.shape)


def coarse_solve(rows, rows2, place_ref, strips_ref, co, sums, g, a, b, over, reach):
    zero = jnp.zeros(g.shape[1:], F32)
    for ref in (g, a, b):
        ref[PAD - 1] = zero
        ref[PAD + rows2] = zero
    for r in range(PAD - 1):
        b[r] = zero
        b[PAD + rows2 + 1 + r] = zero
    at = g
    for index in range(COARSE_SWEEPS - 1):
        to = b if index % 2 == 0 else a
        sweep(at, to, co, g, PAD, PAD + rows2)
        at = to

    def left(first, size):
        v, new = swept(b, co, g, first, size)
        a[pl.ds(first, size)] = co[BACK, pl.ds(first, size)] * (new - v)

    rows_loop(PAD, PAD + rows2, CHUNK, left)
    count = strips_ref.shape[0]

    def strip(index, start):
        end = start + strips_ref[index]
        over[index] = lax.fori_loop(start, end, lambda r, total: total + a[r], zero)
        return end

    lax.fori_loop(0, count, strip, PAD)
    total = jnp.sum(jnp.sum(over[...], axis=2, keepdims=True), axis=1, keepdims=True)
    over[...] = total / sums[...]
    block = rows // 4
    first = PAD + place_ref[2] * block - reach
    final = first + block + 2 * reach

    def shift(index, start):
        end = start + strips_ref[index]
        amount = over[index]

        def row(r, carry):
            b[r] = b[r] + amount
            return carry

        lax.fori_loop(jnp.maximum(start, first), jnp.minimum(end, final), row, 0)
        return end

    lax.fori_loop(0, count, shift, PAD)


def correct(rows, place_ref, e2, mid_v, target, reach):
    h1, m = HALO // 2, rows // 2
    low = -(-reach // 2)
    block = rows // 4
    layers, width = e2.shape[1:]
    span = block + 2 * low
    window = e2[pl.ds(place_ref[2] * block + PAD - low, span)]
    first = place_ref[3] * (HALF // 2)

    def place(row, col):
        from_own = jnp.where(col >= LANES - SLOT, col - LANES, col)
        used = (col < HALF + SLOT) | (col >= LANES - SLOT)
        return used & (row == (from_own + LANES) // 2 - HALF + first)

    spread = exact_dot(window.reshape(span * layers, width), one_hot((width, LANES), place))
    spread = spread.reshape(span, layers, LANES)
    wide = jnp.broadcast_to(spread[:, None], (span, 2, layers, LANES)).reshape(2 * span, layers, LANES)
    start = (h1 - reach) - 2 * (h1 // 2 - low)
    here = pl.ds(h1 - reach, m + 2 * reach)
    target[here] = mid_v[here] + wide[start : start + m + 2 * reach]


def ascend(rows, reach, fine_reach, mid_a, mid_b, mid_co, mid_g, fine_u, fine_a, fine_b, fine_co, fine_g):
    h0, h1, m = HALO, HALO // 2, rows // 2
    sweep(mid_a, mid_b, mid_co, mid_g, h1 - reach + 1, h1 + m + reach - 1)
    sweep(mid_b, mid_a, mid_co, mid_g, h1 - reach + 2, h1 + m + reach - 2)

    def add(at, size):
        fine = fine_u[pl.ds(2 * at, 2 * size)]
        both = fine.reshape((size, 2) + fine.shape[1:]) + mid_a[pl.ds(at, size)][:, None, None]
        fine_a[pl.ds(2 * at, 2 * size)] = both.reshape(fine.shape)

    rows_loop(h1 - reach + 2, h1 + m + reach - 2, 10, add)
    sweep_fine(fine_a, fine_b, fine_co, fine_g, h0 - fine_reach - 1, h0 + rows + fine_reach + 1)
    sweep_fine(fine_b, fine_a, fine_co, fine_g, h0 - fine_reach, h0 + rows + fine_reach)


def middle_kernel(
    rows, npx, npy, place_ref, strips_ref, mine, other, fine_u, fine_g, fine_co, mid_v, mid_g, mid_co,
    fine_out, mid_v_out, mid_g_out, packed, low_co, sums,
    k2, g2, a2, b2, over, va, vb, fa, fb,
):
    block = rows // 4
    rows2 = npx * block
    zero = jnp.zeros(k2.shape[1:], F32)
    k2[PAD - 1] = zero
    k2[PAD + rows2] = zero
    unpack(place_ref, mine, other, 1, k2, None, npx, npy, block)
    coarse_coefficients(rows2, strips_ref, k2, low_co, sums)
    unpack(place_ref, mine, other, 0, g2, low_co, npx, npy, block)
    coarse_solve(rows, rows2, place_ref, strips_ref, low_co, sums, g2, a2, b2, over, 5)
    correct(rows, place_ref, b2, mid_v, va, 9)
    ascend(rows, 9, 11, va, vb, mid_co, mid_g, fine_u, fa, fb, fine_co, fine_g)
    sweep_fine(fa, fb, fine_co, fine_g, HALO - 10, HALO + rows + 10)
    descend(rows, fb, fine_out, fine_g, fine_co, mid_v_out, mid_g_out, mid_co, 4, packed)


def last_kernel(
    rows, npx, npy, place_ref, strips_ref, mine, other, fine_u, fine_g, fine_co, mid_v, mid_g, mid_co, low_co, sums,
    out, g2, a2, b2, over, va, vb, fa, fb,
):
    block = rows // 4
    rows2 = npx * block
    unpack(place_ref, mine, other, 0, g2, low_co, npx, npy, block)
    coarse_solve(rows, rows2, place_ref, strips_ref, low_co, sums, g2, a2, b2, over, 2)
    correct(rows, place_ref, b2, mid_v, va, 3)
    ascend(rows, 3, 0, va, vb, mid_co, mid_g, fine_u, fa, fb, fine_co, fine_g)
    layers = fa.shape[2]
    here = pl.ds(HALO, rows)
    even, odd = fa[here, 0], fa[here, 1]
    both = jnp.where(iota_of(even, 2) < HALF, even, shifted(odd, HALF, 2))

    def place(row, col):
        return col == 2 * (row % HALF) + row // HALF

    natural = exact_dot(both.reshape(rows * layers, LANES), one_hot((LANES, LANES), place))
    for r in range(rows):
        out[pl.ds(r, layers, stride=rows), :] = natural[r * layers : (r + 1) * layers]


def neighbour_swaps(along_x, send_a, send_b):
    npx, npy = lax.axis_size("px"), lax.axis_size("py")

    def swap_with(partner):
        pairs = [(x * npy + y, partner(x, y)) for x in range(npx) for y in range(npy)]
        return [(here, x * npy + y) for here, (x, y) in pairs]

    def beside(i):
        return ((i + 1) ^ 1) - 1

    if along_x:
        a = swap_with(lambda x, y: (x ^ 1, y))
        b = swap_with(lambda x, y: (beside(x), y) if 0 < x < npx - 1 else (x, y ^ 1))
    else:
        a = swap_with(lambda x, y: (x, y ^ 1))
        b = swap_with(lambda x, y: (x, beside(y)) if 0 < y < npy - 1 else (x ^ 1, y))
    recv_b = lax.ppermute(send_b, ("px", "py"), b)
    return lax.ppermute(send_a, ("px", "py"), a), recv_b


def arr(*shape):
    return jax.ShapeDtypeStruct(shape, F32)


def shards(source, coefficient, strip_rows):
    npx, npy = lax.axis_size("px"), lax.axis_size("py")
    layers, rows, _ = source.shape
    total, mids = rows + 2 * HALO, (rows + 2 * HALO) // 2
    rows2, width2 = npx * rows // 4, npy * LANES // 4
    px, py = lax.axis_index("px"), lax.axis_index("py")
    inner_x, inner_y = ((i > 0) & (i < n - 1) for i, n in ((px, npx), (py, npy)))
    place = jnp.stack([px % 2, py % 2, px, py, inner_x, inner_y]).astype(jnp.int32)
    fine, mid = arr(total, 2, layers, LANES), arr(mids, layers, LANES)
    low, strip_sums = arr(rows2 + 2 * PAD, layers, width2), arr(strip_rows.shape[0], layers, width2)
    fine_cos, mid_cos, low_cos = (arr(n, *item.shape) for n, item in ((7, fine), (8, mid), (8, low)))
    halo = arr(HALO, 2, layers, LANES)
    columns = arr(mids, layers, LANES)
    room = min(48, 12 + 24 * rows2 * layers * width2 * 4 // 2**20)

    def call(body, name, smem, vmem, out_shape, scratch, where=VMEM, semaphores=()):
        return pl.pallas_call(
            functools.partial(body, rows),
            out_shape=out_shape,
            in_specs=[SMEM] * smem + [where] * vmem,
            out_specs=jax.tree.map(lambda _: VMEM, out_shape),
            scratch_shapes=[pltpu.VMEM(item.shape, F32) for item in scratch] + list(semaphores),
            compiler_params=pltpu.CompilerParams(vmem_limit_bytes=room * 2**20),
            name=name,
        )

    flat = arr(layers * rows, LANES)
    own, send_a, send_b = call(
        cut_kernel, "cut", 1, 2, (arr(rows, 2, layers, LANES), halo, halo), (flat, flat),
        pl.BlockSpec(memory_space=pltpu.HBM), (pltpu.SemaphoreType.DMA((2,)),),
    )(place, source.reshape(flat.shape), coefficient.reshape(flat.shape))
    recv_a, recv_b = neighbour_swaps(True, send_a, send_b)
    ext, send_a, send_b = call(pack_kernel, "pack", 1, 3, (arr(total, 2, layers, LANES), columns, columns), ())(
        place, own, recv_a, recv_b
    )
    recv_a, recv_b = neighbour_swaps(False, send_a, send_b)
    fine_u, fine_g, fine_co, mid_v, mid_g, mid_co, packed = call(
        descend_kernel, "descend", 1, 3, (fine, fine, fine_cos, mid, mid, mid_cos, arr(2, 2, layers, LANES)),
        (fine, fine, mid),
    )(place, ext, recv_a, recv_b)

    def gather(block):
        shape = (npx // 2, 2, npy) + block.shape[1:]
        every = jnp.broadcast_to(block[None, :, None], shape).reshape((npx * npy,) + block.shape[1:])
        half = lax.all_to_all(every, ("px", "py"), 0, 0, tiled=True)
        return half, lax.ppermute(half, "px", [(i, i ^ 1) for i in range(npx)])

    def sized(body):
        return lambda rows, *refs: body(rows, npx, npy, *refs)

    fine_u, mid_v, mid_g, packed, low_co, sums = call(
        sized(middle_kernel), "middle", 2, 8, (fine, mid, mid, arr(2, 1, layers, LANES), low_cos, strip_sums),
        (low, low, low, low, strip_sums, mid, mid, fine, fine),
    )(place, strip_rows, *gather(packed), fine_u, fine_g, fine_co, mid_v, mid_g, mid_co)
    out = call(
        sized(last_kernel), "last", 2, 10, arr(layers * rows, LANES),
        (low, low, low, strip_sums, mid, mid, fine, fine),
    )(place, strip_rows, *gather(packed), fine_u, fine_g, fine_co, mid_v, mid_g, mid_co, low_co, sums)
    return out.reshape(source.shape)


def solution(mesh):
    placed = (P(None, "px", "py"), P(None, "px", "py"), P())
    return jax.shard_map(
        shards, mesh=mesh, in_specs=placed, out_specs=P(None, "px", "py"), check_vma=False
    )
```

```python
import functools

import jax
import jax.numpy as jnp
from jax import lax
from jax.experimental import pallas as pl
from jax.experimental.pallas import tpu as pltpu
from jax.sharding import PartitionSpec as P

COARSE_SWEEPS = 6
relaxation = 0.8
z_coupling = 0.25

HALO = 24
SIDE = 32
PAD = 8
LANES = 128
HALF = LANES // 2
SLOT = SIDE // 2
VMEM = pl.BlockSpec(memory_space=pltpu.VMEM)
SMEM = pl.BlockSpec(memory_space=pltpu.SMEM)
F32 = jnp.float32


def shifted(values, amount, axis):
    return pltpu.roll(values, amount % values.shape[axis], axis)


def iota_of(values, axis):
    return lax.broadcasted_iota(jnp.int32, values.shape, axis % values.ndim)


def rows_loop(low, high, chunk, body):
    chunk = min(chunk, high - low)
    count = -(-(high - low) // chunk)
    chunk = -(-(high - low) // count)

    def step(index, carry):
        body(jnp.minimum(low + index * chunk, high - chunk), chunk)
        return carry

    if count == 1:
        body(low, chunk)
    else:
        lax.fori_loop(0, count, step, 0)


def pair_sum_rows(values):
    count = values.shape[0] // 2
    pairs = values.reshape((count, 2) + values.shape[1:])
    return pairs[:, 0] + pairs[:, 1]


def pair_sum_lanes(values):
    return values + jnp.where(iota_of(values, -1) % 2 == 0, shifted(values, -1, 2), shifted(values, 1, 2))


def exact_dot(left, right):
    return lax.dot_general(
        left, right, (((1,), (0,)), ((), ())), precision=lax.Precision.HIGHEST, preferred_element_type=F32
    )


def one_hot(shape, place):
    row = lax.broadcasted_iota(jnp.int32, shape, 0)
    col = lax.broadcasted_iota(jnp.int32, shape, 1)
    return jnp.where(place(row, col), 1.0, 0.0).astype(F32)


W, E, S, N, D, U, BACK, INV = range(8)


def weights(k, west, east, south, north, z_factor):
    layer = iota_of(k, -2)
    west, east, south, north = (0.5 * (k + other) for other in (west, east, south, north))
    half = 0.5 * z_factor
    axis = k.ndim - 2
    down = jnp.where(layer == 0, 0.0, half * (k + shifted(k, 1, axis)))
    up = jnp.where(layer == k.shape[axis] - 1, 0.0, half * (k + shifted(k, -1, axis)))
    diagonal = west + east + south + north + down + up
    inside = k > 0.0
    inverse = jnp.where(inside, relaxation / jnp.where(inside, diagonal, 1.0), 0.0)
    scaled = [inverse * face for face in (west, east, south, north, down, up)]
    return scaled + [(1.0 / relaxation) * diagonal, inverse]


def fine_coefficients(k_ref, s_ref, co, g_ref, low, high, chunk):
    def body(at, size):
        here, before, after = pl.ds(at, size), pl.ds(at - 1, size), pl.ds(at + 1, size)
        k = [k_ref[here, s] for s in range(2)]
        sides = ((shifted(k[1], 1, 2), k[1]), (k[0], shifted(k[0], -1, 2)))
        for s in range(2):
            found = weights(k[s], k_ref[before, s], k_ref[after, s], *sides[s], z_coupling)
            for which in range(INV):
                co[which, here, s] = found[which]
            g_ref[here, s] = found[INV] * s_ref[here, s]

    rows_loop(low, high, chunk, body)


def mid_coefficients(k_ref, co, low, high, chunk):
    def body(at, size):
        here = pl.ds(at, size)
        k = k_ref[here]
        found = weights(
            k, k_ref[pl.ds(at - 1, size)], k_ref[pl.ds(at + 1, size)], shifted(k, 1, 2), shifted(k, -1, 2),
            4.0 * z_coupling,
        )
        for which in range(INV + 1):
            co[which, here] = found[which]

    rows_loop(low, high, chunk, body)


def swept_fine(v_ref, co, g_ref, at, size):
    here, before, after = pl.ds(at, size), pl.ds(at - 1, size), pl.ds(at + 1, size)
    v = [v_ref[here, s] for s in range(2)]
    sides = ((shifted(v[1], 1, 2), v[1]), (v[0], shifted(v[0], -1, 2)))
    new = []
    for s in range(2):
        total = g_ref[here, s] + (1.0 - relaxation) * v[s]
        total = total + co[W, here, s] * v_ref[before, s]
        total = total + co[E, here, s] * v_ref[after, s]
        total = total + co[D, here, s] * shifted(v[s], 1, 1)
        total = total + co[U, here, s] * shifted(v[s], -1, 1)
        total = total + co[S, here, s] * sides[s][0]
        total = total + co[N, here, s] * sides[s][1]
        new.append(total)
    return v, new


def swept(v_ref, co, g_ref, at, size):
    here = pl.ds(at, size)
    v = v_ref[here]
    total = g_ref[here] + (1.0 - relaxation) * v
    total = total + co[W, here] * v_ref[pl.ds(at - 1, size)]
    total = total + co[E, here] * v_ref[pl.ds(at + 1, size)]
    total = total + co[D, here] * shifted(v, 1, 1)
    total = total + co[U, here] * shifted(v, -1, 1)
    total = total + co[S, here] * shifted(v, 1, 2)
    total = total + co[N, here] * shifted(v, -1, 2)
    return v, total


def sweep_fine(v_ref, out_ref, co, g_ref, low, high):
    def body(at, size):
        new = swept_fine(v_ref, co, g_ref, at, size)[1]
        for s in range(2):
            out_ref[pl.ds(at, size), s] = new[s]

    rows_loop(low, high, FINE_CHUNK, body)


def sweep(v_ref, out_ref, co, g_ref, low, high):
    def body(at, size):
        out_ref[pl.ds(at, size)] = swept(v_ref, co, g_ref, at, size)[1]

    rows_loop(low, high, CHUNK, body)


FINE_CHUNK = 20
CHUNK = 64
DOWN_CHUNK = 10
PACK_CHUNK = 40
WIDEN_CHUNK = 40
FINE_SET = 19
MID_SET = 18
LOW_SET = 32
ADD_CHUNK = 15


def coarse_rows(values, place_ref):
    per = LANES // (HALF // 2)
    turn = place_ref[3] % per
    count = values.shape[0] // per
    left = jnp.concatenate(
        [jnp.concatenate([values[per * p + g] for g in range(per)], axis=1) for p in range(count)], axis=0
    )

    def place(row, col):
        lane = row % LANES
        quarter = (row // LANES + turn) % per
        return (lane < HALF) & (lane % 2 == 0) & (col == quarter * (HALF // 2) + lane // 2)

    packed = exact_dot(left, one_hot((per * LANES, LANES), place))
    layers = values.shape[1]
    return [packed[p * layers : (p + 1) * layers] for p in range(count)]


def cut_kernel(rows, place_ref, both, own, send_a, send_b):
    layers = own.shape[2]
    pick = [[pl.ds(which * layers * rows + r, layers, stride=rows) for which in range(2)] for r in range(rows)]
    left = jnp.concatenate(
        [jnp.concatenate([both[at, :] for at in pair], axis=1) for pair in pick], axis=0
    )

    def place(row, col):
        y = row % LANES
        return col == (row // LANES) * LANES + (y % 2) * HALF + y // 2

    sorted_y = exact_dot(left, one_hot((2 * LANES, 2 * LANES), place))
    for which in range(2):
        part = sorted_y[:, which * LANES : (which + 1) * LANES]
        own[:, which] = part.reshape(rows, layers, LANES)
    even_x = place_ref[0] == 0
    send_a[...] = own[pl.ds(jnp.where(even_x, rows - HALO, 0), HALO)]
    send_b[...] = own[pl.ds(jnp.where(even_x, 0, rows - HALO), HALO)]


RIGHT_SLOT = (0, 2, 1, 3)
LEFT_SLOT = (3, 5, 4, 6)


def pack_kernel(rows, place_ref, own, recv_a, recv_b, ext, send_a, send_b):
    even_x, even_y = place_ref[0] == 0, place_ref[1] == 0
    half = send_a.shape[0]
    ext[pl.ds(HALO, rows)] = own[...]
    a, b = recv_a[...], jnp.where(place_ref[4] != 0, recv_b[...], 0.0)
    ext[pl.ds(0, HALO)] = jnp.where(even_x, b, a)
    ext[pl.ds(HALO + rows, HALO)] = jnp.where(even_x, a, b)

    def body(at, size):
        parts = [ext[pl.ds(at + h * half, size), which] for which in range(2) for h in range(2)]
        slot = (iota_of(parts[0], 2) // SLOT) % 4
        first = last = None
        for g in range(4):
            right = shifted(parts[g], RIGHT_SLOT[g] * SLOT, 2)
            left = shifted(parts[g], (LEFT_SLOT[g] - 3) * SLOT, 2)
            first = right if g == 0 else jnp.where(slot == RIGHT_SLOT[g] % 4, right, first)
            last = left if g == 0 else jnp.where(slot == LEFT_SLOT[g] % 4, left, last)
        send_a[pl.ds(at, size)] = jnp.where(even_y, last, first)
        send_b[pl.ds(at, size)] = jnp.where(even_y, first, last)

    rows_loop(0, half, PACK_CHUNK, body)


def descend_kernel(
    rows, place_ref, ext, recv_a, recv_b, fine_u, fine_g, fine_co, mid_v, mid_g, mid_co, packed, s_ref, k_ref, k1
):
    even_y = place_ref[1] == 0
    half = recv_a.shape[0]
    h0, h1, m = HALO, HALO // 2, rows // 2

    def widen(at, size):
        a, b = recv_a[pl.ds(at, size)], jnp.where(place_ref[5] != 0, recv_b[pl.ds(at, size)], 0.0)
        right, left = jnp.where(even_y, a, b), jnp.where(even_y, b, a)
        lane = iota_of(right, 2)
        odd_slot = (lane // SLOT) % 2 == 1
        merged = (jnp.where(odd_slot, left, right), jnp.where(odd_slot, right, left))
        for which, wide in enumerate((s_ref, k_ref)):
            for h in range(2):
                here = pl.ds(at + h * half, size)
                slot = RIGHT_SLOT[2 * which + h]
                inner = ext[here, which]
                wide[here, 0] = jnp.where(lane < HALF, inner, shifted(merged[which], HALF - slot * SLOT, 2))
                wide[here, 1] = jnp.where(lane < HALF, shifted(inner, HALF, 2), shifted(merged[which], -slot * SLOT, 2))

    rows_loop(0, half, WIDEN_CHUNK, widen)

    def coarser(at, size):
        here = pl.ds(2 * at, 2 * size)
        k1[pl.ds(at, size)] = 0.25 * pair_sum_rows(k_ref[here, 0] + k_ref[here, 1])

    rows_loop(0, half, 20, coarser)
    fine_coefficients(k_ref, s_ref, fine_co, fine_g, h0 - 22, h0 + rows + 22, FINE_SET)
    mid_coefficients(k1, mid_co, h1 - 10, h1 + m + 10, MID_SET)
    descend(rows, place_ref, fine_g, fine_u, fine_g, fine_co, mid_v, mid_g, mid_co, 10, packed)
    k2 = 0.25 * pair_sum_lanes(pair_sum_rows(k1[pl.ds(h1, m)]))
    for p, part in enumerate(coarse_rows(k2, place_ref)):
        packed[p, 1] = part


def descend(rows, place_ref, fine_first, fine_u, fine_g, fine_co, mid_v, mid_g, mid_co, reach, packed):
    h0, h1, m = HALO, HALO // 2, rows // 2
    sweep_fine(fine_first, fine_u, fine_co, fine_g, h0 - 2 * reach - 1, h0 + rows + 2 * reach + 1)

    def down(at, size):
        v, new = swept_fine(fine_u, fine_co, fine_g, 2 * at, 2 * size)
        here = pl.ds(2 * at, 2 * size)
        left = fine_co[BACK, here, 0] * (new[0] - v[0]) + fine_co[BACK, here, 1] * (new[1] - v[1])
        mid_g[pl.ds(at, size)] = mid_co[INV, pl.ds(at, size)] * pair_sum_rows(left)

    rows_loop(h1 - reach, h1 + m + reach, DOWN_CHUNK, down)
    sweep(mid_g, mid_v, mid_co, mid_g, h1 - reach + 1, h1 + m + reach - 1)
    v, new = swept(mid_v, mid_co, mid_g, h1, m)
    left = mid_co[BACK, pl.ds(h1, m)] * (new - v)
    for p, part in enumerate(coarse_rows(pair_sum_lanes(pair_sum_rows(left)), place_ref)):
        packed[p, 0] = part


def unpack(place_ref, mine, other, which, target, scale, npx, npy, block):
    even_x = place_ref[0] == 0
    per = 4
    width = LANES // per
    group_of = 4 if npx % 4 == 0 else 1

    def body(step, carry):
        for i in range(group_of):
            ix = step * group_of + i
            for p in range(block // per):
                for q in range(npy // per):
                    devices = [ix * npy + per * q + j for j in range(per)]
                    here = even_x if p == 0 else jnp.logical_not(even_x)
                    parts = [jnp.where(here, mine[i, which], other[i, which]) for i in devices]
                    group = iota_of(parts[0], 1) // width
                    for g in range(per):
                        row = parts[-g % per]
                        for quarter in range(1, per):
                            row = jnp.where(group == quarter, parts[(quarter - g) % per], row)
                        row = shifted(row, -g * width, 1)
                        at = PAD + ix * block + per * p + g
                        lanes = pl.ds(q * LANES, LANES)
                        if scale is not None:
                            row = row * scale[INV, at, :, lanes]
                        target[at, :, lanes] = row
        return carry

    lax.fori_loop(0, npx // group_of, body, 0)


def coarse_coefficients(rows2, strips_ref, k2, co, sums):
    width = k2.shape[2]

    def body(at, size):
        k = k2[pl.ds(at, size)]
        lane = iota_of(k, 2)
        open_s, open_n = lane > 0, lane < width - 1
        found = weights(
            k, k2[pl.ds(at - 1, size)], k2[pl.ds(at + 1, size)],
            jnp.where(open_s, shifted(k, 1, 2), 0.0), jnp.where(open_n, shifted(k, -1, 2), 0.0), 16.0 * z_coupling,
        )
        found[S] = jnp.where(open_s, found[S], 0.0)
        found[N] = jnp.where(open_n, found[N], 0.0)
        for which in range(INV + 1):
            co[which, pl.ds(at, size)] = found[which]

    rows_loop(PAD, PAD + rows2, LOW_SET, body)
    zero = jnp.zeros(k2.shape[1:], F32)
    for start, end in strips(strips_ref):
        co[W, PAD + start] = zero
        co[E, PAD + end - 1] = zero
    sums[...] = 1.0 / (relaxation * strip_sums(co.at[BACK], strips_ref, rows2, sums))


def strips(strips_ref):
    ends = [0]
    for index in range(strips_ref.shape[0]):
        ends.append(ends[-1] + strips_ref[index])
    return list(zip(ends[:-1], ends[1:]))


def strip_sums(values, strips_ref, rows2, scratch):
    whole = values[pl.ds(PAD, rows2)]
    row = iota_of(whole, 0)
    for index, (start, end) in enumerate(strips(strips_ref)):
        scratch[index] = jnp.sum(jnp.where((row >= start) & (row < end), whole, 0.0), axis=0)
    total = jnp.sum(jnp.sum(scratch[...], axis=2, keepdims=True), axis=1, keepdims=True)
    return jnp.broadcast_to(total, scratch.shape)


def coarse_solve(rows2, strips_ref, co, sums, g, a, b, over):
    zero = jnp.zeros(g.shape[1:], F32)
    for ref in (g, a, b):
        ref[PAD - 1] = zero
        ref[PAD + rows2] = zero
    for r in range(PAD - 1):
        b[r] = zero
        b[PAD + rows2 + 1 + r] = zero
    at = g
    for index in range(COARSE_SWEEPS - 1):
        to = b if index % 2 == 0 else a
        sweep(at, to, co, g, PAD, PAD + rows2)
        at = to

    def left(first, size):
        v, new = swept(b, co, g, first, size)
        a[pl.ds(first, size)] = co[BACK, pl.ds(first, size)] * (new - v)

    rows_loop(PAD, PAD + rows2, CHUNK, left)
    over[...] = sums[...] * strip_sums(a, strips_ref, rows2, over)


def correct(rows, place_ref, strips_ref, e2, over, mid_v, target, reach):
    h1, m = HALO // 2, rows // 2
    low = -(-reach // 2)
    block = rows // 4
    layers, width = e2.shape[1:]
    span = block + 2 * low
    first_row = place_ref[2] * block - low
    window = e2[pl.ds(first_row + PAD, span)]
    row = iota_of(window, 0) + first_row
    for index, (start, end) in enumerate(strips(strips_ref)):
        window = window + jnp.where((row >= start) & (row < end), over[index][None], 0.0)
    first = place_ref[3] * (HALF // 2)

    def place(row, col):
        from_own = jnp.where(col >= LANES - SLOT, col - LANES, col)
        used = (col < HALF + SLOT) | (col >= LANES - SLOT)
        return used & (row == (from_own + LANES) // 2 - HALF + first)

    spread = exact_dot(window.reshape(span * layers, width), one_hot((width, LANES), place))
    spread = spread.reshape(span, layers, LANES)
    wide = jnp.broadcast_to(spread[:, None], (span, 2, layers, LANES)).reshape(2 * span, layers, LANES)
    start = (h1 - reach) - 2 * (h1 // 2 - low)
    here = pl.ds(h1 - reach, m + 2 * reach)
    target[here] = mid_v[here] + wide[start : start + m + 2 * reach]


def ascend(rows, reach, fine_reach, mid_a, mid_b, mid_co, mid_g, fine_u, fine_a, fine_b, fine_co, fine_g):
    h0, h1, m = HALO, HALO // 2, rows // 2
    sweep(mid_a, mid_b, mid_co, mid_g, h1 - reach + 1, h1 + m + reach - 1)
    sweep(mid_b, mid_a, mid_co, mid_g, h1 - reach + 2, h1 + m + reach - 2)

    def add(at, size):
        fine = fine_u[pl.ds(2 * at, 2 * size)]
        both = fine.reshape((size, 2) + fine.shape[1:]) + mid_a[pl.ds(at, size)][:, None, None]
        fine_a[pl.ds(2 * at, 2 * size)] = both.reshape(fine.shape)

    rows_loop(h1 - reach + 2, h1 + m + reach - 2, ADD_CHUNK, add)
    sweep_fine(fine_a, fine_b, fine_co, fine_g, h0 - fine_reach - 1, h0 + rows + fine_reach + 1)
    sweep_fine(fine_b, fine_a, fine_co, fine_g, h0 - fine_reach, h0 + rows + fine_reach)


def middle_kernel(
    rows, npx, npy, place_ref, strips_ref, mine, other, fine_u, fine_g, fine_co, mid_v, mid_g, mid_co,
    fine_out, mid_v_out, mid_g_out, packed, low_co, sums,
    k2, g2, a2, b2, over, va, vb, fa, fb,
):
    block = rows // 4
    rows2 = npx * block
    zero = jnp.zeros(k2.shape[1:], F32)
    k2[PAD - 1] = zero
    k2[PAD + rows2] = zero
    unpack(place_ref, mine, other, 1, k2, None, npx, npy, block)
    coarse_coefficients(rows2, strips_ref, k2, low_co, sums)
    unpack(place_ref, mine, other, 0, g2, low_co, npx, npy, block)
    coarse_solve(rows2, strips_ref, low_co, sums, g2, a2, b2, over)
    correct(rows, place_ref, strips_ref, b2, over, mid_v, va, 9)
    ascend(rows, 9, 11, va, vb, mid_co, mid_g, fine_u, fa, fb, fine_co, fine_g)
    sweep_fine(fa, fb, fine_co, fine_g, HALO - 10, HALO + rows + 10)
    descend(rows, place_ref, fb, fine_out, fine_g, fine_co, mid_v_out, mid_g_out, mid_co, 4, packed)


def last_kernel(
    rows, npx, npy, place_ref, strips_ref, mine, other, fine_u, fine_g, fine_co, mid_v, mid_g, mid_co, low_co, sums,
    out, g2, a2, b2, over, va, vb, fa, fb,
):
    block = rows // 4
    rows2 = npx * block
    unpack(place_ref, mine, other, 0, g2, low_co, npx, npy, block)
    coarse_solve(rows2, strips_ref, low_co, sums, g2, a2, b2, over)
    correct(rows, place_ref, strips_ref, b2, over, mid_v, va, 3)
    ascend(rows, 3, 0, va, vb, mid_co, mid_g, fine_u, fa, fb, fine_co, fine_g)
    layers = fa.shape[2]
    here = pl.ds(HALO, rows)
    even, odd = fa[here, 0], fa[here, 1]
    both = jnp.where(iota_of(even, 2) < HALF, even, shifted(odd, HALF, 2))

    def place(row, col):
        return col == 2 * (row % HALF) + row // HALF

    natural = exact_dot(both.reshape(rows * layers, LANES), one_hot((LANES, LANES), place))
    for r in range(rows):
        out[pl.ds(r, layers, stride=rows), :] = natural[r * layers : (r + 1) * layers]


def neighbour_swaps(along_x, send_a, send_b):
    npx, npy = lax.axis_size("px"), lax.axis_size("py")

    def swap_with(partner):
        pairs = [(x * npy + y, partner(x, y)) for x in range(npx) for y in range(npy)]
        return [(here, x * npy + y) for here, (x, y) in pairs]

    def beside(i):
        return ((i + 1) ^ 1) - 1

    if along_x:
        a = swap_with(lambda x, y: (x ^ 1, y))
        b = swap_with(lambda x, y: (beside(x), y) if 0 < x < npx - 1 else (x, y ^ 1))
    else:
        a = swap_with(lambda x, y: (x, y ^ 1))
        b = swap_with(lambda x, y: (x, beside(y)) if 0 < y < npy - 1 else (x ^ 1, y))
    recv_b = lax.ppermute(send_b, ("px", "py"), b)
    return lax.ppermute(send_a, ("px", "py"), a), recv_b


def arr(*shape):
    return jax.ShapeDtypeStruct(shape, F32)


def shards(source, coefficient, strip_rows):
    npx, npy = lax.axis_size("px"), lax.axis_size("py")
    layers, rows, _ = source.shape
    total, mids = rows + 2 * HALO, (rows + 2 * HALO) // 2
    rows2, width2 = npx * rows // 4, npy * LANES // 4
    px, py = lax.axis_index("px"), lax.axis_index("py")
    inner_x, inner_y = ((i > 0) & (i < n - 1) for i, n in ((px, npx), (py, npy)))
    place = jnp.stack([px % 2, py % 2, px, py, inner_x, inner_y]).astype(jnp.int32)
    fine, mid = arr(total, 2, layers, LANES), arr(mids, layers, LANES)
    low, strip_sums = arr(rows2 + 2 * PAD, layers, width2), arr(strip_rows.shape[0], layers, width2)
    fine_cos, mid_cos, low_cos = (arr(n, *item.shape) for n, item in ((7, fine), (8, mid), (8, low)))
    halo = arr(HALO, 2, layers, LANES)
    columns = arr(mids, layers, LANES)
    room = min(48, 12 + 24 * rows2 * layers * width2 * 4 // 2**20)

    def call(body, name, smem, vmem, out_shape, scratch):
        return pl.pallas_call(
            functools.partial(body, rows),
            out_shape=out_shape,
            in_specs=[SMEM] * smem + [VMEM] * vmem,
            out_specs=jax.tree.map(lambda _: VMEM, out_shape),
            scratch_shapes=[pltpu.VMEM(item.shape, F32) for item in scratch],
            compiler_params=pltpu.CompilerParams(vmem_limit_bytes=room * 2**20),
            name=name,
        )

    both = jnp.stack([source, coefficient]).reshape(2 * layers * rows, LANES)
    own, send_a, send_b = call(cut_kernel, "cut", 1, 1, (arr(rows, 2, layers, LANES), halo, halo), ())(place, both)
    recv_a, recv_b = neighbour_swaps(True, send_a, send_b)
    ext, send_a, send_b = call(pack_kernel, "pack", 1, 3, (arr(total, 2, layers, LANES), columns, columns), ())(
        place, own, recv_a, recv_b
    )
    recv_a, recv_b = neighbour_swaps(False, send_a, send_b)
    fine_u, fine_g, fine_co, mid_v, mid_g, mid_co, packed = call(
        descend_kernel, "descend", 1, 3, (fine, fine, fine_cos, mid, mid, mid_cos, arr(2, 2, layers, LANES)),
        (fine, fine, mid),
    )(place, ext, recv_a, recv_b)

    def gather(block):
        shape = (npx // 2, 2, npy) + block.shape[1:]
        every = jnp.broadcast_to(block[None, :, None], shape).reshape((npx * npy,) + block.shape[1:])
        half = lax.all_to_all(every, ("px", "py"), 0, 0, tiled=True)
        return half, lax.ppermute(half, "px", [(i, i ^ 1) for i in range(npx)])

    def sized(body):
        return lambda rows, *refs: body(rows, npx, npy, *refs)

    fine_u, mid_v, mid_g, packed, low_co, sums = call(
        sized(middle_kernel), "middle", 2, 8, (fine, mid, mid, arr(2, 1, layers, LANES), low_cos, strip_sums),
        (low, low, low, low, strip_sums, mid, mid, fine, fine),
    )(place, strip_rows, *gather(packed), fine_u, fine_g, fine_co, mid_v, mid_g, mid_co)
    out = call(
        sized(last_kernel), "last", 2, 10, arr(layers * rows, LANES),
        (low, low, low, strip_sums, mid, mid, fine, fine),
    )(place, strip_rows, *gather(packed), fine_u, fine_g, fine_co, mid_v, mid_g, mid_co, low_co, sums)
    return out.reshape(source.shape)


def solution(mesh):
    placed = (P(None, "px", "py"), P(None, "px", "py"), P())
    return jax.shard_map(
        shards, mesh=mesh, in_specs=placed, out_specs=P(None, "px", "py"), check_vma=False
    )
```

```python
import functools

import jax
import jax.numpy as jnp
from jax import lax
from jax.experimental import pallas as pl
from jax.experimental.pallas import tpu as pltpu
from jax.sharding import PartitionSpec as P

COARSE_SWEEPS = 6
relaxation = 0.8
z_coupling = 0.25

HALO = 24
SIDE = 32
PAD = 8
LANES = 128
HALF = LANES // 2
SLOT = SIDE // 2
VMEM = pl.BlockSpec(memory_space=pltpu.VMEM)
SMEM = pl.BlockSpec(memory_space=pltpu.SMEM)
F32 = jnp.float32


def shifted(values, amount, axis):
    return pltpu.roll(values, amount % values.shape[axis], axis)


def iota_of(values, axis):
    return lax.broadcasted_iota(jnp.int32, values.shape, axis % values.ndim)


def rows_loop(low, high, chunk, body):
    chunk = min(chunk, high - low)
    count = -(-(high - low) // chunk)
    chunk = -(-(high - low) // count)

    def step(index, carry):
        body(jnp.minimum(low + index * chunk, high - chunk), chunk)
        return carry

    if count == 1:
        body(low, chunk)
    else:
        lax.fori_loop(0, count, step, 0)


def pair_sum_rows(values):
    count = values.shape[0] // 2
    pairs = values.reshape((count, 2) + values.shape[1:])
    return pairs[:, 0] + pairs[:, 1]


def pair_sum_lanes(values):
    return values + jnp.where(iota_of(values, -1) % 2 == 0, shifted(values, -1, 2), shifted(values, 1, 2))


def exact_dot(left, right):
    total = None
    for last in (False, False, True):
        part = left.astype(jnp.bfloat16)
        term = lax.dot_general(part, right, (((1,), (0,)), ((), ())), preferred_element_type=F32)
        total = term if total is None else total + term
        if not last:
            left = left - part.astype(F32)
    return total


def one_hot(shape, place):
    row = lax.broadcasted_iota(jnp.int32, shape, 0)
    col = lax.broadcasted_iota(jnp.int32, shape, 1)
    return jnp.where(place(row, col), 1.0, 0.0).astype(jnp.bfloat16)


W, E, S, N, D, U, BACK, INV = range(8)


def weights(k, west, east, south, north, z_factor):
    layer = iota_of(k, -2)
    west, east, south, north = (0.5 * (k + other) for other in (west, east, south, north))
    half = 0.5 * z_factor
    axis = k.ndim - 2
    down = jnp.where(layer == 0, 0.0, half * (k + shifted(k, 1, axis)))
    up = jnp.where(layer == k.shape[axis] - 1, 0.0, half * (k + shifted(k, -1, axis)))
    diagonal = west + east + south + north + down + up
    inside = k > 0.0
    inverse = jnp.where(inside, relaxation / jnp.where(inside, diagonal, 1.0), 0.0)
    scaled = [inverse * face for face in (west, east, south, north, down, up)]
    return scaled + [(1.0 / relaxation) * diagonal, inverse]


def fine_coefficients(k_ref, s_ref, co, g_ref, low, high, chunk):
    def body(at, size):
        here, before, after = pl.ds(at, size), pl.ds(at - 1, size), pl.ds(at + 1, size)
        k = [k_ref[here, s] for s in range(2)]
        sides = ((shifted(k[1], 1, 2), k[1]), (k[0], shifted(k[0], -1, 2)))
        for s in range(2):
            found = weights(k[s], k_ref[before, s], k_ref[after, s], *sides[s], z_coupling)
            for which in range(INV):
                co[which, here, s] = found[which]
            g_ref[here, s] = found[INV] * s_ref[here, s]

    rows_loop(low, high, chunk, body)


def mid_coefficients(k_ref, co, low, high, chunk):
    def body(at, size):
        here = pl.ds(at, size)
        k = k_ref[here]
        found = weights(
            k, k_ref[pl.ds(at - 1, size)], k_ref[pl.ds(at + 1, size)], shifted(k, 1, 2), shifted(k, -1, 2),
            4.0 * z_coupling,
        )
        for which in range(INV + 1):
            co[which, here] = found[which]

    rows_loop(low, high, chunk, body)


def swept_fine(v_ref, co, g_ref, at, size):
    here, before, after = pl.ds(at, size), pl.ds(at - 1, size), pl.ds(at + 1, size)
    v = [v_ref[here, s] for s in range(2)]
    sides = ((shifted(v[1], 1, 2), v[1]), (v[0], shifted(v[0], -1, 2)))
    new = []
    for s in range(2):
        total = g_ref[here, s] + (1.0 - relaxation) * v[s]
        total = total + co[W, here, s] * v_ref[before, s]
        total = total + co[E, here, s] * v_ref[after, s]
        total = total + co[D, here, s] * shifted(v[s], 1, 1)
        total = total + co[U, here, s] * shifted(v[s], -1, 1)
        total = total + co[S, here, s] * sides[s][0]
        total = total + co[N, here, s] * sides[s][1]
        new.append(total)
    return v, new


def swept(v_ref, co, g_ref, at, size):
    here = pl.ds(at, size)
    v = v_ref[here]
    total = g_ref[here] + (1.0 - relaxation) * v
    total = total + co[W, here] * v_ref[pl.ds(at - 1, size)]
    total = total + co[E, here] * v_ref[pl.ds(at + 1, size)]
    total = total + co[D, here] * shifted(v, 1, 1)
    total = total + co[U, here] * shifted(v, -1, 1)
    total = total + co[S, here] * shifted(v, 1, 2)
    total = total + co[N, here] * shifted(v, -1, 2)
    return v, total


def sweep_fine(v_ref, out_ref, co, g_ref, low, high):
    def body(at, size):
        new = swept_fine(v_ref, co, g_ref, at, size)[1]
        for s in range(2):
            out_ref[pl.ds(at, size), s] = new[s]

    rows_loop(low, high, FINE_CHUNK, body)


def sweep(v_ref, out_ref, co, g_ref, low, high):
    def body(at, size):
        out_ref[pl.ds(at, size)] = swept(v_ref, co, g_ref, at, size)[1]

    rows_loop(low, high, CHUNK, body)


FINE_CHUNK = 20
CHUNK = 64
DOWN_CHUNK = 10
FINE_SET = 19
MID_SET = 18
LOW_SET = 32
ADD_CHUNK = 15


def coarse_rows(values, place_ref):
    per = LANES // (HALF // 2)
    turn = place_ref[3] % per
    count = values.shape[0] // per
    left = jnp.concatenate(
        [jnp.concatenate([values[per * p + g] for g in range(per)], axis=1) for p in range(count)], axis=0
    )

    def place(row, col):
        lane = row % LANES
        quarter = (row // LANES + turn) % per
        return (lane < HALF) & (lane % 2 == 0) & (col == quarter * (HALF // 2) + lane // 2)

    packed = exact_dot(left, one_hot((per * LANES, LANES), place))
    layers = values.shape[1]
    return [packed[p * layers : (p + 1) * layers] for p in range(count)]


RIGHT_SLOT = (0, 2, 1, 3)
LEFT_SLOT = (3, 5, 4, 6)
PAIRS = HALO // 2


def cut_kernel(rows, place_ref, both, own, xa, xb, ya, yb, aa, ab, ba, bb):
    layers = own.shape[2]
    pick = [[pl.ds(which * layers * rows + r, layers, stride=rows) for which in range(2)] for r in range(rows)]
    left = jnp.concatenate(
        [jnp.concatenate([both[at, :] for at in pair], axis=1) for pair in pick], axis=0
    )

    def place(row, col):
        y = row % LANES
        return col == (row // LANES) * LANES + (y % 2) * HALF + y // 2

    sorted_y = exact_dot(left, one_hot((2 * LANES, 2 * LANES), place))
    parts = []
    for which in range(2):
        part = sorted_y[:, which * LANES : (which + 1) * LANES].reshape(rows, layers, LANES)
        own[:, which] = part
        pairs = part.reshape(rows // 2, 2, layers, LANES)
        parts += [pairs[:, 0], pairs[:, 1]]
    even_x, even_y = place_ref[0] == 0, place_ref[1] == 0
    low, high = jnp.where(even_x, rows - HALO, 0), jnp.where(even_x, 0, rows - HALO)
    xa[...] = own[pl.ds(low, HALO)]
    xb[...] = own[pl.ds(high, HALO)]
    slot = (iota_of(parts[0], 2) // SLOT) % 4
    for g in range(4):
        right = shifted(parts[g], RIGHT_SLOT[g] * SLOT, 2)
        left = shifted(parts[g], (LEFT_SLOT[g] - 3) * SLOT, 2)
        first = right if g == 0 else jnp.where(slot == RIGHT_SLOT[g] % 4, right, first)
        last = left if g == 0 else jnp.where(slot == LEFT_SLOT[g] % 4, left, last)
    ya[...] = jnp.where(even_y, last, first)
    yb[...] = jnp.where(even_y, first, last)
    for columns, with_a, with_b in ((ya, aa, ba), (yb, ab, bb)):
        with_a[...] = columns[pl.ds(low // 2, PAIRS)]
        with_b[...] = columns[pl.ds(high // 2, PAIRS)]


def widen(rows, place_ref, own, xa, xb, ya, yb, aa, ab, ba, bb, s_ref, k_ref):
    even_x, even_y = place_ref[0] == 0, place_ref[1] == 0
    inner_x, inner_y = place_ref[4] != 0, place_ref[5] != 0
    inner_both = jnp.logical_and(inner_x, inner_y)
    xa, ya, aa = xa[...], ya[...], aa[...]
    xb, ba = (jnp.where(inner_x, ref[...], 0.0) for ref in (xb, ba))
    yb, ab = (jnp.where(inner_y, ref[...], 0.0) for ref in (yb, ab))
    bb = jnp.where(inner_both, bb[...], 0.0)
    before = [jnp.where(even_x, b, a) for a, b in ((aa, ba), (ab, bb))]
    after = [jnp.where(even_x, a, b) for a, b in ((aa, ba), (ab, bb))]
    for start, inner, (a, b) in (
        (0, jnp.where(even_x, xb, xa), before),
        (HALO, own[...], (ya, yb)),
        (HALO + rows, jnp.where(even_x, xa, xb), after),
    ):
        right, left = jnp.where(even_y, a, b), jnp.where(even_y, b, a)
        lane = iota_of(right, 2)
        odd_slot = (lane // SLOT) % 2 == 1
        merged = (jnp.where(odd_slot, left, right), jnp.where(odd_slot, right, left))
        count, layers = right.shape[:2]
        pairs = inner.reshape(count, 2, 2, layers, LANES)
        for which, wide in enumerate((s_ref, k_ref)):
            found = []
            for h in range(2):
                slot = RIGHT_SLOT[2 * which + h]
                block = pairs[:, h, which]
                found.append((
                    jnp.where(lane < HALF, block, shifted(merged[which], HALF - slot * SLOT, 2)),
                    jnp.where(lane < HALF, shifted(block, HALF, 2), shifted(merged[which], -slot * SLOT, 2)),
                ))
            for s in range(2):
                both = jnp.stack([found[0][s], found[1][s]], axis=1)
                wide[pl.ds(start, 2 * count), s] = both.reshape(2 * count, layers, LANES)


def descend_kernel(
    rows, place_ref, own, xa, xb, ya, yb, aa, ab, ba, bb,
    fine_u, fine_g, fine_co, mid_v, mid_g, mid_co, packed, s_ref, k_ref, k1,
):
    h0, h1, m = HALO, HALO // 2, rows // 2
    half = h0 + m
    widen(rows, place_ref, own, xa, xb, ya, yb, aa, ab, ba, bb, s_ref, k_ref)

    def coarser(at, size):
        here = pl.ds(2 * at, 2 * size)
        k1[pl.ds(at, size)] = 0.25 * pair_sum_rows(k_ref[here, 0] + k_ref[here, 1])

    rows_loop(0, half, 20, coarser)
    fine_coefficients(k_ref, s_ref, fine_co, fine_g, h0 - 22, h0 + rows + 22, FINE_SET)
    mid_coefficients(k1, mid_co, h1 - 10, h1 + m + 10, MID_SET)
    descend(rows, place_ref, fine_g, fine_u, fine_g, fine_co, mid_v, mid_g, mid_co, 10, packed)
    k2 = 0.25 * pair_sum_lanes(pair_sum_rows(k1[pl.ds(h1, m)]))
    for p, part in enumerate(coarse_rows(k2, place_ref)):
        packed[p, 1] = part


def descend(rows, place_ref, fine_first, fine_u, fine_g, fine_co, mid_v, mid_g, mid_co, reach, packed):
    h0, h1, m = HALO, HALO // 2, rows // 2
    sweep_fine(fine_first, fine_u, fine_co, fine_g, h0 - 2 * reach - 1, h0 + rows + 2 * reach + 1)

    def down(at, size):
        v, new = swept_fine(fine_u, fine_co, fine_g, 2 * at, 2 * size)
        here = pl.ds(2 * at, 2 * size)
        left = fine_co[BACK, here, 0] * (new[0] - v[0]) + fine_co[BACK, here, 1] * (new[1] - v[1])
        mid_g[pl.ds(at, size)] = mid_co[INV, pl.ds(at, size)] * pair_sum_rows(left)

    rows_loop(h1 - reach, h1 + m + reach, DOWN_CHUNK, down)
    sweep(mid_g, mid_v, mid_co, mid_g, h1 - reach + 1, h1 + m + reach - 1)
    v, new = swept(mid_v, mid_co, mid_g, h1, m)
    left = mid_co[BACK, pl.ds(h1, m)] * (new - v)
    for p, part in enumerate(coarse_rows(pair_sum_lanes(pair_sum_rows(left)), place_ref)):
        packed[p, 0] = part


def unpack(place_ref, mine, other, which, target, scale, npx, npy, block):
    even_x = place_ref[0] == 0
    per = 4
    width = LANES // per
    group_of = 4 if npx % 4 == 0 else 1

    def body(step, carry):
        for i in range(group_of):
            ix = step * group_of + i
            for p in range(block // per):
                for q in range(npy // per):
                    devices = [ix * npy + per * q + j for j in range(per)]
                    here = even_x if p == 0 else jnp.logical_not(even_x)
                    parts = [jnp.where(here, mine[i, which], other[i, which]) for i in devices]
                    group = iota_of(parts[0], 1) // width
                    for g in range(per):
                        row = parts[-g % per]
                        for quarter in range(1, per):
                            row = jnp.where(group == quarter, parts[(quarter - g) % per], row)
                        row = shifted(row, -g * width, 1)
                        at = PAD + ix * block + per * p + g
                        lanes = pl.ds(q * LANES, LANES)
                        if scale is not None:
                            row = row * scale[INV, at, :, lanes]
                        target[at, :, lanes] = row
        return carry

    lax.fori_loop(0, npx // group_of, body, 0)


def coarse_coefficients(rows2, strips_ref, k2, co, sums):
    width = k2.shape[2]

    def body(at, size):
        k = k2[pl.ds(at, size)]
        lane = iota_of(k, 2)
        open_s, open_n = lane > 0, lane < width - 1
        found = weights(
            k, k2[pl.ds(at - 1, size)], k2[pl.ds(at + 1, size)],
            jnp.where(open_s, shifted(k, 1, 2), 0.0), jnp.where(open_n, shifted(k, -1, 2), 0.0), 16.0 * z_coupling,
        )
        found[S] = jnp.where(open_s, found[S], 0.0)
        found[N] = jnp.where(open_n, found[N], 0.0)
        for which in range(INV + 1):
            co[which, pl.ds(at, size)] = found[which]

    rows_loop(PAD, PAD + rows2, LOW_SET, body)
    zero = jnp.zeros(k2.shape[1:], F32)
    for start, end in strips(strips_ref):
        co[W, PAD + start] = zero
        co[E, PAD + end - 1] = zero
    sums[...] = 1.0 / (relaxation * strip_sums(co.at[BACK], strips_ref, rows2, sums))


def strips(strips_ref):
    ends = [0]
    for index in range(strips_ref.shape[0]):
        ends.append(ends[-1] + strips_ref[index])
    return list(zip(ends[:-1], ends[1:]))


def strip_sums(values, strips_ref, rows2, scratch):
    whole = values[pl.ds(PAD, rows2)]
    row = iota_of(whole, 0)
    for index, (start, end) in enumerate(strips(strips_ref)):
        scratch[index] = jnp.sum(jnp.where((row >= start) & (row < end), whole, 0.0), axis=0)
    total = jnp.sum(jnp.sum(scratch[...], axis=2, keepdims=True), axis=1, keepdims=True)
    return jnp.broadcast_to(total, scratch.shape)


def coarse_solve(rows2, strips_ref, co, sums, g, a, b, over):
    zero = jnp.zeros(g.shape[1:], F32)
    for ref in (g, a, b):
        ref[PAD - 1] = zero
        ref[PAD + rows2] = zero
    for r in range(PAD - 1):
        b[r] = zero
        b[PAD + rows2 + 1 + r] = zero
    at = g
    for index in range(COARSE_SWEEPS - 1):
        to = b if index % 2 == 0 else a
        sweep(at, to, co, g, PAD, PAD + rows2)
        at = to

    def left(first, size):
        v, new = swept(b, co, g, first, size)
        a[pl.ds(first, size)] = co[BACK, pl.ds(first, size)] * (new - v)

    rows_loop(PAD, PAD + rows2, CHUNK, left)
    over[...] = sums[...] * strip_sums(a, strips_ref, rows2, over)


def correct(rows, place_ref, strips_ref, e2, over, mid_v, target, reach):
    h1, m = HALO // 2, rows // 2
    low = -(-reach // 2)
    block = rows // 4
    layers, width = e2.shape[1:]
    span = block + 2 * low
    first_row = place_ref[2] * block - low
    window = e2[pl.ds(first_row + PAD, span)]
    row = iota_of(window, 0) + first_row
    for index, (start, end) in enumerate(strips(strips_ref)):
        window = window + jnp.where((row >= start) & (row < end), over[index][None], 0.0)
    first = place_ref[3] * (HALF // 2)

    def place(row, col):
        from_own = jnp.where(col >= LANES - SLOT, col - LANES, col)
        used = (col < HALF + SLOT) | (col >= LANES - SLOT)
        return used & (row == (from_own + LANES) // 2 - HALF + first)

    spread = exact_dot(window.reshape(span * layers, width), one_hot((width, LANES), place))
    spread = spread.reshape(span, layers, LANES)
    wide = jnp.broadcast_to(spread[:, None], (span, 2, layers, LANES)).reshape(2 * span, layers, LANES)
    start = (h1 - reach) - 2 * (h1 // 2 - low)
    here = pl.ds(h1 - reach, m + 2 * reach)
    target[here] = mid_v[here] + wide[start : start + m + 2 * reach]


def ascend(rows, reach, fine_reach, mid_a, mid_b, mid_co, mid_g, fine_u, fine_a, fine_b, fine_co, fine_g):
    h0, h1, m = HALO, HALO // 2, rows // 2
    sweep(mid_a, mid_b, mid_co, mid_g, h1 - reach + 1, h1 + m + reach - 1)
    sweep(mid_b, mid_a, mid_co, mid_g, h1 - reach + 2, h1 + m + reach - 2)

    def add(at, size):
        fine = fine_u[pl.ds(2 * at, 2 * size)]
        both = fine.reshape((size, 2) + fine.shape[1:]) + mid_a[pl.ds(at, size)][:, None, None]
        fine_a[pl.ds(2 * at, 2 * size)] = both.reshape(fine.shape)

    rows_loop(h1 - reach + 2, h1 + m + reach - 2, ADD_CHUNK, add)
    sweep_fine(fine_a, fine_b, fine_co, fine_g, h0 - fine_reach - 1, h0 + rows + fine_reach + 1)
    sweep_fine(fine_b, fine_a, fine_co, fine_g, h0 - fine_reach, h0 + rows + fine_reach)


def middle_kernel(
    rows, npx, npy, place_ref, strips_ref, mine, other, fine_u, fine_g, fine_co, mid_v, mid_g, mid_co,
    fine_out, mid_v_out, mid_g_out, packed, low_co, sums,
    k2, g2, a2, b2, over, va, vb, fa, fb,
):
    block = rows // 4
    rows2 = npx * block
    zero = jnp.zeros(k2.shape[1:], F32)
    k2[PAD - 1] = zero
    k2[PAD + rows2] = zero
    unpack(place_ref, mine, other, 1, k2, None, npx, npy, block)
    coarse_coefficients(rows2, strips_ref, k2, low_co, sums)
    unpack(place_ref, mine, other, 0, g2, low_co, npx, npy, block)
    coarse_solve(rows2, strips_ref, low_co, sums, g2, a2, b2, over)
    correct(rows, place_ref, strips_ref, b2, over, mid_v, va, 9)
    ascend(rows, 9, 11, va, vb, mid_co, mid_g, fine_u, fa, fb, fine_co, fine_g)
    sweep_fine(fa, fb, fine_co, fine_g, HALO - 10, HALO + rows + 10)
    descend(rows, place_ref, fb, fine_out, fine_g, fine_co, mid_v_out, mid_g_out, mid_co, 4, packed)


def last_kernel(
    rows, npx, npy, place_ref, strips_ref, mine, other, fine_u, fine_g, fine_co, mid_v, mid_g, mid_co, low_co, sums,
    out, g2, a2, b2, over, va, vb, fa, fb,
):
    block = rows // 4
    rows2 = npx * block
    unpack(place_ref, mine, other, 0, g2, low_co, npx, npy, block)
    coarse_solve(rows2, strips_ref, low_co, sums, g2, a2, b2, over)
    correct(rows, place_ref, strips_ref, b2, over, mid_v, va, 3)
    ascend(rows, 3, 0, va, vb, mid_co, mid_g, fine_u, fa, fb, fine_co, fine_g)
    layers = fa.shape[2]
    here = pl.ds(HALO, rows)
    even, odd = fa[here, 0], fa[here, 1]
    both = jnp.where(iota_of(even, 2) < HALF, even, shifted(odd, HALF, 2))

    def place(row, col):
        return col == 2 * (row % HALF) + row // HALF

    natural = exact_dot(both.reshape(rows * layers, LANES), one_hot((LANES, LANES), place))
    for r in range(rows):
        out[pl.ds(r, layers, stride=rows), :] = natural[r * layers : (r + 1) * layers]


def neighbour_swaps(xa, xb, ya, yb, aa, ab, ba, bb):
    npx, npy = lax.axis_size("px"), lax.axis_size("py")

    def swap(block, partner):
        pairs = []
        for x in range(npx):
            for y in range(npy):
                to_x, to_y = partner(x, y, 0 < x < npx - 1, 0 < y < npy - 1)
                pairs.append((x * npy + y, to_x * npy + to_y))
        return lax.ppermute(block, ("px", "py"), pairs)

    def far(i):
        return ((i + 1) ^ 1) - 1

    def corner(x, y, inner_x, inner_y):
        if not inner_y:
            return x ^ 1, y
        return far(x) if inner_x else x, far(y)

    ya = swap(ya, lambda x, y, inner_x, inner_y: (x, y ^ 1))
    xa = swap(xa, lambda x, y, inner_x, inner_y: (x ^ 1, y))
    aa = swap(aa, lambda x, y, inner_x, inner_y: (x ^ 1, y ^ 1))
    yb = swap(yb, lambda x, y, inner_x, inner_y: (x, far(y)) if inner_y else (x ^ 1, y))
    ab = swap(ab, lambda x, y, inner_x, inner_y: (x ^ 1, far(y) if inner_y else y))
    ba = swap(ba, lambda x, y, inner_x, inner_y: (far(x) if inner_x else x, y ^ 1))
    xb = swap(xb, lambda x, y, inner_x, inner_y: (far(x), y) if inner_x else (x, y ^ 1))
    bb = swap(bb, corner)
    return xa, xb, ya, yb, aa, ab, ba, bb


def arr(*shape):
    return jax.ShapeDtypeStruct(shape, F32)


def shards(source, coefficient, strip_rows):
    npx, npy = lax.axis_size("px"), lax.axis_size("py")
    layers, rows, _ = source.shape
    total, mids = rows + 2 * HALO, (rows + 2 * HALO) // 2
    rows2, width2 = npx * rows // 4, npy * LANES // 4
    px, py = lax.axis_index("px"), lax.axis_index("py")
    inner_x, inner_y = ((i > 0) & (i < n - 1) for i, n in ((px, npx), (py, npy)))
    place = jnp.stack([px % 2, py % 2, px, py, inner_x, inner_y]).astype(jnp.int32)
    fine, mid = arr(total, 2, layers, LANES), arr(mids, layers, LANES)
    low, strip_sums = arr(rows2 + 2 * PAD, layers, width2), arr(strip_rows.shape[0], layers, width2)
    fine_cos, mid_cos, low_cos = (arr(n, *item.shape) for n, item in ((7, fine), (8, mid), (8, low)))
    halo, columns, corner = (arr(*n, layers, LANES) for n in ((HALO, 2), (rows // 2,), (PAIRS,)))
    room = min(48, 12 + 24 * rows2 * layers * width2 * 4 // 2**20)

    def call(body, name, smem, vmem, out_shape, scratch):
        return pl.pallas_call(
            functools.partial(body, rows),
            out_shape=out_shape,
            in_specs=[SMEM] * smem + [VMEM] * vmem,
            out_specs=jax.tree.map(lambda _: VMEM, out_shape),
            scratch_shapes=[pltpu.VMEM(item.shape, F32) for item in scratch],
            compiler_params=pltpu.CompilerParams(vmem_limit_bytes=room * 2**20),
            name=name,
        )

    both = jnp.stack([source, coefficient]).reshape(2 * layers * rows, LANES)
    own, *sent = call(
        cut_kernel, "cut", 1, 1, (arr(rows, 2, layers, LANES),) + (halo,) * 2 + (columns,) * 2 + (corner,) * 4, ()
    )(place, both)
    fine_u, fine_g, fine_co, mid_v, mid_g, mid_co, packed = call(
        descend_kernel, "descend", 1, 9, (fine, fine, fine_cos, mid, mid, mid_cos, arr(2, 2, layers, LANES)),
        (fine, fine, mid),
    )(place, own, *neighbour_swaps(*sent))

    def gather(block):
        shape = (npx // 2, 2, npy) + block.shape[1:]
        every = jnp.broadcast_to(block[None, :, None], shape).reshape((npx * npy,) + block.shape[1:])
        half = lax.all_to_all(every, ("px", "py"), 0, 0, tiled=True)
        return half, lax.ppermute(half, "px", [(i, i ^ 1) for i in range(npx)])

    def sized(body):
        return lambda rows, *refs: body(rows, npx, npy, *refs)

    fine_u, mid_v, mid_g, packed, low_co, sums = call(
        sized(middle_kernel), "middle", 2, 8, (fine, mid, mid, arr(2, 1, layers, LANES), low_cos, strip_sums),
        (low, low, low, low, strip_sums, mid, mid, fine, fine),
    )(place, strip_rows, *gather(packed), fine_u, fine_g, fine_co, mid_v, mid_g, mid_co)
    out = call(
        sized(last_kernel), "last", 2, 10, arr(layers * rows, LANES),
        (low, low, low, strip_sums, mid, mid, fine, fine),
    )(place, strip_rows, *gather(packed), fine_u, fine_g, fine_co, mid_v, mid_g, mid_co, low_co, sums)
    return out.reshape(source.shape)


def solution(mesh):
    placed = (P(None, "px", "py"), P(None, "px", "py"), P())
    return jax.shard_map(
        shards, mesh=mesh, in_specs=placed, out_specs=P(None, "px", "py"), check_vma=False
    )
```

```python
import functools

import jax
import jax.numpy as jnp
from jax import lax
from jax.experimental import pallas as pl
from jax.experimental.pallas import tpu as pltpu
from jax.sharding import PartitionSpec as P

COARSE_SWEEPS = 6
relaxation = 0.8
z_coupling = 0.25

HALO = 24
SIDE = 32
PAD = 8
LANES = 128
HALF = LANES // 2
SLOT = SIDE // 2
VMEM = pl.BlockSpec(memory_space=pltpu.VMEM)
SMEM = pl.BlockSpec(memory_space=pltpu.SMEM)
F32 = jnp.float32


def shifted(values, amount, axis):
    return pltpu.roll(values, amount % values.shape[axis], axis)


def iota_of(values, axis):
    return lax.broadcasted_iota(jnp.int32, values.shape, axis % values.ndim)


def rows_loop(low, high, chunk, body):
    chunk = min(chunk, high - low)
    count = -(-(high - low) // chunk)
    chunk = -(-(high - low) // count)

    def step(index, carry):
        body(jnp.minimum(low + index * chunk, high - chunk), chunk)
        return carry

    if count == 1:
        body(low, chunk)
    else:
        lax.fori_loop(0, count, step, 0)


def pair_sum_rows(values):
    count = values.shape[0] // 2
    pairs = values.reshape((count, 2) + values.shape[1:])
    return pairs[:, 0] + pairs[:, 1]


def pair_sum_lanes(values):
    return values + jnp.where(iota_of(values, -1) % 2 == 0, shifted(values, -1, 2), shifted(values, 1, 2))


def exact_dot(left, right):
    total = None
    for last in (False, False, True):
        part = left.astype(jnp.bfloat16)
        term = lax.dot_general(part, right, (((1,), (0,)), ((), ())), preferred_element_type=F32)
        total = term if total is None else total + term
        if not last:
            left = left - part.astype(F32)
    return total


def one_hot(shape, place):
    row = lax.broadcasted_iota(jnp.int32, shape, 0)
    col = lax.broadcasted_iota(jnp.int32, shape, 1)
    return jnp.where(place(row, col), 1.0, 0.0).astype(jnp.bfloat16)


W, E, S, N, D, U, BACK, INV = range(8)


def weights(k, west, east, south, north, z_factor):
    layer = iota_of(k, -2)
    west, east, south, north = (0.5 * (k + other) for other in (west, east, south, north))
    half = 0.5 * z_factor
    axis = k.ndim - 2
    down = jnp.where(layer == 0, 0.0, half * (k + shifted(k, 1, axis)))
    up = jnp.where(layer == k.shape[axis] - 1, 0.0, half * (k + shifted(k, -1, axis)))
    diagonal = west + east + south + north + down + up
    inside = k > 0.0
    inverse = jnp.where(inside, relaxation / jnp.where(inside, diagonal, 1.0), 0.0)
    scaled = [inverse * face for face in (west, east, south, north, down, up)]
    return scaled + [(1.0 / relaxation) * diagonal, inverse]


def fine_coefficients(k_ref, s_ref, co, g_ref, low, high, chunk):
    def body(at, size):
        here, before, after = pl.ds(at, size), pl.ds(at - 1, size), pl.ds(at + 1, size)
        k = [k_ref[here, s] for s in range(2)]
        sides = ((shifted(k[1], 1, 2), k[1]), (k[0], shifted(k[0], -1, 2)))
        for s in range(2):
            found = weights(k[s], k_ref[before, s], k_ref[after, s], *sides[s], z_coupling)
            for which in range(INV):
                co[which, here, s] = found[which]
            g_ref[here, s] = found[INV] * s_ref[here, s]

    rows_loop(low, high, chunk, body)


def mid_coefficients(k_ref, co, low, high, chunk):
    def body(at, size):
        here = pl.ds(at, size)
        k = k_ref[here]
        found = weights(
            k, k_ref[pl.ds(at - 1, size)], k_ref[pl.ds(at + 1, size)], shifted(k, 1, 2), shifted(k, -1, 2),
            4.0 * z_coupling,
        )
        for which in range(INV + 1):
            co[which, here] = found[which]

    rows_loop(low, high, chunk, body)


def swept_fine(v_ref, co, g_ref, at, size):
    here = pl.ds(at, size)
    around = v_ref[pl.ds(at - 1, size + 2)]
    v = [around[1:-1, s] for s in range(2)]
    sides = ((shifted(v[1], 1, 2), v[1]), (v[0], shifted(v[0], -1, 2)))
    new = []
    for s in range(2):
        total = g_ref[here, s] + (1.0 - relaxation) * v[s]
        total = total + co[W, here, s] * around[:-2, s]
        total = total + co[E, here, s] * around[2:, s]
        total = total + co[D, here, s] * shifted(v[s], 1, 1)
        total = total + co[U, here, s] * shifted(v[s], -1, 1)
        total = total + co[S, here, s] * sides[s][0]
        total = total + co[N, here, s] * sides[s][1]
        new.append(total)
    return v, new


def swept(v_ref, co, g_ref, at, size):
    here = pl.ds(at, size)
    around = v_ref[pl.ds(at - 1, size + 2)]
    v = around[1:-1]
    total = g_ref[here] + (1.0 - relaxation) * v
    total = total + co[W, here] * around[:-2]
    total = total + co[E, here] * around[2:]
    total = total + co[D, here] * shifted(v, 1, 1)
    total = total + co[U, here] * shifted(v, -1, 1)
    total = total + co[S, here] * shifted(v, 1, 2)
    total = total + co[N, here] * shifted(v, -1, 2)
    return v, total


def sweep_fine(v_ref, out_ref, co, g_ref, low, high):
    def body(at, size):
        new = swept_fine(v_ref, co, g_ref, at, size)[1]
        for s in range(2):
            out_ref[pl.ds(at, size), s] = new[s]

    rows_loop(low, high, FINE_CHUNK, body)


def sweep(v_ref, out_ref, co, g_ref, low, high):
    def body(at, size):
        out_ref[pl.ds(at, size)] = swept(v_ref, co, g_ref, at, size)[1]

    rows_loop(low, high, CHUNK, body)


FINE_CHUNK = 80
CHUNK = 64
DOWN_CHUNK = 36
FINE_SET = 19
MID_SET = 18
LOW_SET = 32
ADD_CHUNK = 15


def coarse_rows(values, place_ref):
    per = LANES // (HALF // 2)
    count, layers = values.shape[:2]
    pick = one_hot((LANES, LANES), lambda row, col: (row < HALF) & (row == 2 * col))
    cells = exact_dot(values.reshape(count * layers, LANES), pick).reshape(count // per, per, layers, LANES)
    packed = [shifted(cells[:, g], (place_ref[3] + g) % per * (HALF // 2), 2) for g in range(per)]
    return packed[0] + packed[1] + packed[2] + packed[3]


RIGHT_SLOT = (0, 2, 1, 3)
LEFT_SLOT = (3, 5, 4, 6)
PAIRS = HALO // 2


def cut_kernel(rows, place_ref, both, own, xa, xb, ya, yb, aa, ab, ba, bb):
    layers = own.shape[2]
    pick = [[pl.ds(which * layers * rows + r, layers, stride=rows) for which in range(2)] for r in range(rows)]
    left = jnp.concatenate(
        [jnp.concatenate([both[at, :] for at in pair], axis=1) for pair in pick], axis=0
    )

    def place(row, col):
        y = row % LANES
        return col == (row // LANES) * LANES + (y % 2) * HALF + y // 2

    sorted_y = exact_dot(left, one_hot((2 * LANES, 2 * LANES), place))
    parts = []
    for which in range(2):
        part = sorted_y[:, which * LANES : (which + 1) * LANES].reshape(rows, layers, LANES)
        own[:, which] = part
        pairs = part.reshape(rows // 2, 2, layers, LANES)
        parts += [pairs[:, 0], pairs[:, 1]]
    even_x, even_y = place_ref[0] == 0, place_ref[1] == 0
    low, high = jnp.where(even_x, rows - HALO, 0), jnp.where(even_x, 0, rows - HALO)
    xa[...] = own[pl.ds(low, HALO)]
    xb[...] = own[pl.ds(high, HALO)]
    slot = (iota_of(parts[0], 2) // SLOT) % 4
    for g in range(4):
        right = shifted(parts[g], RIGHT_SLOT[g] * SLOT, 2)
        left = shifted(parts[g], (LEFT_SLOT[g] - 3) * SLOT, 2)
        first = right if g == 0 else jnp.where(slot == RIGHT_SLOT[g] % 4, right, first)
        last = left if g == 0 else jnp.where(slot == LEFT_SLOT[g] % 4, left, last)
    ya[...] = jnp.where(even_y, last, first)
    yb[...] = jnp.where(even_y, first, last)
    for columns, with_a, with_b in ((ya, aa, ba), (yb, ab, bb)):
        with_a[...] = columns[pl.ds(low // 2, PAIRS)]
        with_b[...] = columns[pl.ds(high // 2, PAIRS)]


def widen(rows, place_ref, own, xa, xb, ya, yb, aa, ab, ba, bb, s_ref, k_ref):
    even_x, even_y = place_ref[0] == 0, place_ref[1] == 0
    inner_x, inner_y = place_ref[4] != 0, place_ref[5] != 0
    inner_both = jnp.logical_and(inner_x, inner_y)
    xa, ya, aa = xa[...], ya[...], aa[...]
    xb, ba = (jnp.where(inner_x, ref[...], 0.0) for ref in (xb, ba))
    yb, ab = (jnp.where(inner_y, ref[...], 0.0) for ref in (yb, ab))
    bb = jnp.where(inner_both, bb[...], 0.0)
    before = [jnp.where(even_x, b, a) for a, b in ((aa, ba), (ab, bb))]
    after = [jnp.where(even_x, a, b) for a, b in ((aa, ba), (ab, bb))]
    for start, inner, (a, b) in (
        (0, jnp.where(even_x, xb, xa), before),
        (HALO, own[...], (ya, yb)),
        (HALO + rows, jnp.where(even_x, xa, xb), after),
    ):
        right, left = jnp.where(even_y, a, b), jnp.where(even_y, b, a)
        lane = iota_of(right, 2)
        odd_slot = (lane // SLOT) % 2 == 1
        merged = (jnp.where(odd_slot, left, right), jnp.where(odd_slot, right, left))
        count, layers = right.shape[:2]
        pairs = inner.reshape(count, 2, 2, layers, LANES)
        for which, wide in enumerate((s_ref, k_ref)):
            found = []
            for h in range(2):
                slot = RIGHT_SLOT[2 * which + h]
                block = pairs[:, h, which]
                found.append((
                    jnp.where(lane < HALF, block, shifted(merged[which], HALF - slot * SLOT, 2)),
                    jnp.where(lane < HALF, shifted(block, HALF, 2), shifted(merged[which], -slot * SLOT, 2)),
                ))
            for s in range(2):
                both = jnp.stack([found[0][s], found[1][s]], axis=1)
                wide[pl.ds(start, 2 * count), s] = both.reshape(2 * count, layers, LANES)


def descend_kernel(
    rows, place_ref, own, xa, xb, ya, yb, aa, ab, ba, bb,
    fine_u, fine_g, fine_co, mid_v, mid_g, mid_co, packed, s_ref, k_ref, k1,
):
    h0, h1, m = HALO, HALO // 2, rows // 2
    half = h0 + m
    widen(rows, place_ref, own, xa, xb, ya, yb, aa, ab, ba, bb, s_ref, k_ref)

    def coarser(at, size):
        here = pl.ds(2 * at, 2 * size)
        k1[pl.ds(at, size)] = 0.25 * pair_sum_rows(k_ref[here, 0] + k_ref[here, 1])

    rows_loop(0, half, 20, coarser)
    fine_coefficients(k_ref, s_ref, fine_co, fine_g, h0 - 22, h0 + rows + 22, FINE_SET)
    mid_coefficients(k1, mid_co, h1 - 10, h1 + m + 10, MID_SET)
    descend(rows, place_ref, fine_g, fine_u, fine_g, fine_co, mid_v, mid_g, mid_co, 10, packed, k1[pl.ds(h1, m)])


def descend(rows, place_ref, fine_first, fine_u, fine_g, fine_co, mid_v, mid_g, mid_co, reach, packed, k1=None):
    h0, h1, m = HALO, HALO // 2, rows // 2
    sweep_fine(fine_first, fine_u, fine_co, fine_g, h0 - 2 * reach - 1, h0 + rows + 2 * reach + 1)

    def down(at, size):
        v, new = swept_fine(fine_u, fine_co, fine_g, 2 * at, 2 * size)
        here = pl.ds(2 * at, 2 * size)
        left = fine_co[BACK, here, 0] * (new[0] - v[0]) + fine_co[BACK, here, 1] * (new[1] - v[1])
        mid_g[pl.ds(at, size)] = mid_co[INV, pl.ds(at, size)] * pair_sum_rows(left)

    rows_loop(h1 - reach, h1 + m + reach, DOWN_CHUNK, down)
    sweep(mid_g, mid_v, mid_co, mid_g, h1 - reach + 1, h1 + m + reach - 1)
    v, new = swept(mid_v, mid_co, mid_g, h1, m)
    left = mid_co[BACK, pl.ds(h1, m)] * (new - v)
    low = left if k1 is None else jnp.concatenate([left, 0.25 * k1], axis=0)
    low = coarse_rows(pair_sum_lanes(pair_sum_rows(low)), place_ref)
    for which in range(low.shape[0] // packed.shape[0]):
        for p in range(packed.shape[0]):
            packed[p, which] = low[which * packed.shape[0] + p]


def unpack(place_ref, mine, other, which, target, scale, npx, npy, block):
    even_x = place_ref[0] == 0
    per = 4
    width = LANES // per
    group_of = 4 if npx % 4 == 0 else 1

    def body(step, carry):
        for i in range(group_of):
            ix = step * group_of + i
            for p in range(block // per):
                for q in range(npy // per):
                    devices = [ix * npy + per * q + j for j in range(per)]
                    here = even_x if p == 0 else jnp.logical_not(even_x)
                    parts = [jnp.where(here, mine[i, which], other[i, which]) for i in devices]
                    group = iota_of(parts[0], 1) // width
                    for g in range(per):
                        row = parts[-g % per]
                        for quarter in range(1, per):
                            row = jnp.where(group == quarter, parts[(quarter - g) % per], row)
                        row = shifted(row, -g * width, 1)
                        at = PAD + ix * block + per * p + g
                        lanes = pl.ds(q * LANES, LANES)
                        if scale is not None:
                            row = row * scale[INV, at, :, lanes]
                        target[at, :, lanes] = row
        return carry

    lax.fori_loop(0, npx // group_of, body, 0)


def coarse_coefficients(rows2, strips_ref, k2, co, sums):
    width = k2.shape[2]

    def body(at, size):
        k = k2[pl.ds(at, size)]
        lane = iota_of(k, 2)
        open_s, open_n = lane > 0, lane < width - 1
        found = weights(
            k, k2[pl.ds(at - 1, size)], k2[pl.ds(at + 1, size)],
            jnp.where(open_s, shifted(k, 1, 2), 0.0), jnp.where(open_n, shifted(k, -1, 2), 0.0), 16.0 * z_coupling,
        )
        found[S] = jnp.where(open_s, found[S], 0.0)
        found[N] = jnp.where(open_n, found[N], 0.0)
        for which in range(INV + 1):
            co[which, pl.ds(at, size)] = found[which]

    rows_loop(PAD, PAD + rows2, LOW_SET, body)
    zero = jnp.zeros(k2.shape[1:], F32)
    for start, end in strips(strips_ref):
        co[W, PAD + start] = zero
        co[E, PAD + end - 1] = zero
    sums[...] = 1.0 / (relaxation * strip_sums(co.at[BACK], strips_ref, rows2, sums))


def strips(strips_ref):
    ends = [0]
    for index in range(strips_ref.shape[0]):
        ends.append(ends[-1] + strips_ref[index])
    return list(zip(ends[:-1], ends[1:]))


def strip_sums(values, strips_ref, rows2, scratch):
    whole = values[pl.ds(PAD, rows2)]
    row = iota_of(whole, 0)
    for index, (start, end) in enumerate(strips(strips_ref)):
        scratch[index] = jnp.sum(jnp.where((row >= start) & (row < end), whole, 0.0), axis=0)
    total = jnp.sum(jnp.sum(scratch[...], axis=2, keepdims=True), axis=1, keepdims=True)
    return jnp.broadcast_to(total, scratch.shape)


def coarse_solve(rows2, strips_ref, co, sums, g, a, b, over):
    zero = jnp.zeros(g.shape[1:], F32)
    for ref in (g, a, b):
        ref[PAD - 1] = zero
        ref[PAD + rows2] = zero
    for r in range(PAD - 1):
        b[r] = zero
        b[PAD + rows2 + 1 + r] = zero
    at = g
    for index in range(COARSE_SWEEPS - 1):
        to = b if index % 2 == 0 else a
        sweep(at, to, co, g, PAD, PAD + rows2)
        at = to

    def left(first, size):
        v, new = swept(b, co, g, first, size)
        a[pl.ds(first, size)] = co[BACK, pl.ds(first, size)] * (new - v)

    rows_loop(PAD, PAD + rows2, CHUNK, left)
    over[...] = sums[...] * strip_sums(a, strips_ref, rows2, over)


def correct(rows, place_ref, strips_ref, e2, over, mid_v, target, reach):
    h1, m = HALO // 2, rows // 2
    low = -(-reach // 2)
    block = rows // 4
    layers, width = e2.shape[1:]
    span = block + 2 * low
    first_row = place_ref[2] * block - low
    window = e2[pl.ds(first_row + PAD, span)]
    row = iota_of(window, 0) + first_row
    for index, (start, end) in enumerate(strips(strips_ref)):
        window = window + jnp.where((row >= start) & (row < end), over[index][None], 0.0)
    first = place_ref[3] * (HALF // 2)

    def place(row, col):
        from_own = jnp.where(col >= LANES - SLOT, col - LANES, col)
        used = (col < HALF + SLOT) | (col >= LANES - SLOT)
        return used & (row == (from_own + LANES) // 2 - HALF + first)

    spread = exact_dot(window.reshape(span * layers, width), one_hot((width, LANES), place))
    spread = spread.reshape(span, layers, LANES)
    wide = jnp.broadcast_to(spread[:, None], (span, 2, layers, LANES)).reshape(2 * span, layers, LANES)
    start = (h1 - reach) - 2 * (h1 // 2 - low)
    here = pl.ds(h1 - reach, m + 2 * reach)
    target[here] = mid_v[here] + wide[start : start + m + 2 * reach]


def ascend(rows, reach, fine_reach, mid_a, mid_b, mid_co, mid_g, fine_u, fine_a, fine_b, fine_co, fine_g):
    h0, h1, m = HALO, HALO // 2, rows // 2
    sweep(mid_a, mid_b, mid_co, mid_g, h1 - reach + 1, h1 + m + reach - 1)
    sweep(mid_b, mid_a, mid_co, mid_g, h1 - reach + 2, h1 + m + reach - 2)

    def add(at, size):
        fine = fine_u[pl.ds(2 * at, 2 * size)]
        both = fine.reshape((size, 2) + fine.shape[1:]) + mid_a[pl.ds(at, size)][:, None, None]
        fine_a[pl.ds(2 * at, 2 * size)] = both.reshape(fine.shape)

    rows_loop(h1 - reach + 2, h1 + m + reach - 2, ADD_CHUNK, add)
    sweep_fine(fine_a, fine_b, fine_co, fine_g, h0 - fine_reach - 1, h0 + rows + fine_reach + 1)
    sweep_fine(fine_b, fine_a, fine_co, fine_g, h0 - fine_reach, h0 + rows + fine_reach)


def middle_kernel(
    rows, npx, npy, place_ref, strips_ref, mine, other, fine_u, fine_g, fine_co, mid_v, mid_g, mid_co,
    fine_out, mid_v_out, mid_g_out, packed, low_co, sums,
    k2, g2, a2, b2, over, va, vb, fa, fb,
):
    block = rows // 4
    rows2 = npx * block
    zero = jnp.zeros(k2.shape[1:], F32)
    k2[PAD - 1] = zero
    k2[PAD + rows2] = zero
    unpack(place_ref, mine, other, 1, k2, None, npx, npy, block)
    coarse_coefficients(rows2, strips_ref, k2, low_co, sums)
    unpack(place_ref, mine, other, 0, g2, low_co, npx, npy, block)
    coarse_solve(rows2, strips_ref, low_co, sums, g2, a2, b2, over)
    correct(rows, place_ref, strips_ref, b2, over, mid_v, va, 9)
    ascend(rows, 9, 11, va, vb, mid_co, mid_g, fine_u, fa, fb, fine_co, fine_g)
    sweep_fine(fa, fb, fine_co, fine_g, HALO - 10, HALO + rows + 10)
    descend(rows, place_ref, fb, fine_out, fine_g, fine_co, mid_v_out, mid_g_out, mid_co, 4, packed)


def last_kernel(
    rows, npx, npy, place_ref, strips_ref, mine, other, fine_u, fine_g, fine_co, mid_v, mid_g, mid_co, low_co, sums,
    out, g2, a2, b2, over, va, vb, fa, fb,
):
    block = rows // 4
    rows2 = npx * block
    unpack(place_ref, mine, other, 0, g2, low_co, npx, npy, block)
    coarse_solve(rows2, strips_ref, low_co, sums, g2, a2, b2, over)
    correct(rows, place_ref, strips_ref, b2, over, mid_v, va, 3)
    ascend(rows, 3, 0, va, vb, mid_co, mid_g, fine_u, fa, fb, fine_co, fine_g)
    layers = fa.shape[2]
    here = pl.ds(HALO, rows)
    even, odd = fa[here, 0], fa[here, 1]
    both = jnp.where(iota_of(even, 2) < HALF, even, shifted(odd, HALF, 2))

    def place(row, col):
        return col == 2 * (row % HALF) + row // HALF

    natural = exact_dot(both.reshape(rows * layers, LANES), one_hot((LANES, LANES), place))
    for r in range(rows):
        out[pl.ds(r, layers, stride=rows), :] = natural[r * layers : (r + 1) * layers]


def neighbour_swaps(xa, xb, ya, yb, aa, ab, ba, bb):
    npx, npy = lax.axis_size("px"), lax.axis_size("py")

    def swap(block, partner):
        pairs = []
        for x in range(npx):
            for y in range(npy):
                to_x, to_y = partner(x, y, 0 < x < npx - 1, 0 < y < npy - 1)
                pairs.append((x * npy + y, to_x * npy + to_y))
        return lax.ppermute(block, ("px", "py"), pairs)

    def far(i):
        return ((i + 1) ^ 1) - 1

    def corner(x, y, inner_x, inner_y):
        if not inner_y:
            return x ^ 1, y
        return far(x) if inner_x else x, far(y)

    ya = swap(ya, lambda x, y, inner_x, inner_y: (x, y ^ 1))
    xa = swap(xa, lambda x, y, inner_x, inner_y: (x ^ 1, y))
    aa = swap(aa, lambda x, y, inner_x, inner_y: (x ^ 1, y ^ 1))
    yb = swap(yb, lambda x, y, inner_x, inner_y: (x, far(y)) if inner_y else (x ^ 1, y))
    ab = swap(ab, lambda x, y, inner_x, inner_y: (x ^ 1, far(y) if inner_y else y))
    ba = swap(ba, lambda x, y, inner_x, inner_y: (far(x) if inner_x else x, y ^ 1))
    xb = swap(xb, lambda x, y, inner_x, inner_y: (far(x), y) if inner_x else (x, y ^ 1))
    bb = swap(bb, corner)
    return xa, xb, ya, yb, aa, ab, ba, bb


def arr(*shape):
    return jax.ShapeDtypeStruct(shape, F32)


def shards(source, coefficient, strip_rows):
    npx, npy = lax.axis_size("px"), lax.axis_size("py")
    layers, rows, _ = source.shape
    total, mids = rows + 2 * HALO, (rows + 2 * HALO) // 2
    rows2, width2 = npx * rows // 4, npy * LANES // 4
    px, py = lax.axis_index("px"), lax.axis_index("py")
    inner_x, inner_y = ((i > 0) & (i < n - 1) for i, n in ((px, npx), (py, npy)))
    place = jnp.stack([px % 2, py % 2, px, py, inner_x, inner_y]).astype(jnp.int32)
    fine, mid = arr(total, 2, layers, LANES), arr(mids, layers, LANES)
    low, strip_sums = arr(rows2 + 2 * PAD, layers, width2), arr(strip_rows.shape[0], layers, width2)
    fine_cos, mid_cos, low_cos = (arr(n, *item.shape) for n, item in ((7, fine), (8, mid), (8, low)))
    halo, columns, corner = (arr(*n, layers, LANES) for n in ((HALO, 2), (rows // 2,), (PAIRS,)))
    room = min(48, 12 + 24 * rows2 * layers * width2 * 4 // 2**20)

    def call(body, name, smem, vmem, out_shape, scratch):
        return pl.pallas_call(
            functools.partial(body, rows),
            out_shape=out_shape,
            in_specs=[SMEM] * smem + [VMEM] * vmem,
            out_specs=jax.tree.map(lambda _: VMEM, out_shape),
            scratch_shapes=[pltpu.VMEM(item.shape, F32) for item in scratch],
            compiler_params=pltpu.CompilerParams(vmem_limit_bytes=room * 2**20),
            name=name,
        )

    both = jnp.stack([source, coefficient]).reshape(2 * layers * rows, LANES)
    own, *sent = call(
        cut_kernel, "cut", 1, 1, (arr(rows, 2, layers, LANES),) + (halo,) * 2 + (columns,) * 2 + (corner,) * 4, ()
    )(place, both)
    fine_u, fine_g, fine_co, mid_v, mid_g, mid_co, packed = call(
        descend_kernel, "descend", 1, 9, (fine, fine, fine_cos, mid, mid, mid_cos, arr(2, 2, layers, LANES)),
        (fine, fine, mid),
    )(place, own, *neighbour_swaps(*sent))

    def gather(block):
        shape = (npx // 2, 2, npy) + block.shape[1:]
        every = jnp.broadcast_to(block[None, :, None], shape).reshape((npx * npy,) + block.shape[1:])
        half = lax.all_to_all(every, ("px", "py"), 0, 0, tiled=True)
        return half, lax.ppermute(half, "px", [(i, i ^ 1) for i in range(npx)])

    def sized(body):
        return lambda rows, *refs: body(rows, npx, npy, *refs)

    fine_u, mid_v, mid_g, packed, low_co, sums = call(
        sized(middle_kernel), "middle", 2, 8, (fine, mid, mid, arr(2, 1, layers, LANES), low_cos, strip_sums),
        (low, low, low, low, strip_sums, mid, mid, fine, fine),
    )(place, strip_rows, *gather(packed), fine_u, fine_g, fine_co, mid_v, mid_g, mid_co)
    out = call(
        sized(last_kernel), "last", 2, 10, arr(layers * rows, LANES),
        (low, low, low, strip_sums, mid, mid, fine, fine),
    )(place, strip_rows, *gather(packed), fine_u, fine_g, fine_co, mid_v, mid_g, mid_co, low_co, sums)
    return out.reshape(source.shape)


def solution(mesh):
    placed = (P(None, "px", "py"), P(None, "px", "py"), P())
    return jax.shard_map(
        shards, mesh=mesh, in_specs=placed, out_specs=P(None, "px", "py"), check_vma=False
    )
```

```python
import functools

import jax
import jax.numpy as jnp
from jax import lax
from jax.experimental import pallas as pl
from jax.experimental.pallas import tpu as pltpu
from jax.sharding import PartitionSpec as P

COARSE_SWEEPS = 6
relaxation = 0.8
z_coupling = 0.25

HALO = 24
SIDE = 32
PAD = 8
LANES = 128
HALF = LANES // 2
SLOT = SIDE // 2
VMEM = pl.BlockSpec(memory_space=pltpu.VMEM)
SMEM = pl.BlockSpec(memory_space=pltpu.SMEM)
F32 = jnp.float32


def shifted(values, amount, axis):
    return pltpu.roll(values, amount % values.shape[axis], axis)


def iota_of(values, axis):
    return lax.broadcasted_iota(jnp.int32, values.shape, axis % values.ndim)


def rows_loop(low, high, chunk, body):
    chunk = min(chunk, high - low)
    count = -(-(high - low) // chunk)
    chunk = -(-(high - low) // count)

    def step(index, carry):
        body(jnp.minimum(low + index * chunk, high - chunk), chunk)
        return carry

    if count == 1:
        body(low, chunk)
    else:
        lax.fori_loop(0, count, step, 0)


def pair_sum_rows(values):
    count = values.shape[0] // 2
    pairs = values.reshape((count, 2) + values.shape[1:])
    return pairs[:, 0] + pairs[:, 1]


def pair_sum_lanes(values):
    return values + jnp.where(iota_of(values, -1) % 2 == 0, shifted(values, -1, 2), shifted(values, 1, 2))


def exact_dot(left, right):
    total = None
    for last in (False, False, True):
        part = left.astype(jnp.bfloat16)
        term = lax.dot_general(part, right, (((1,), (0,)), ((), ())), preferred_element_type=F32)
        total = term if total is None else total + term
        if not last:
            left = left - part.astype(F32)
    return total


def one_hot(shape, place):
    row = lax.broadcasted_iota(jnp.int32, shape, 0)
    col = lax.broadcasted_iota(jnp.int32, shape, 1)
    return jnp.where(place(row, col), 1.0, 0.0).astype(jnp.bfloat16)


W, E, S, N, D, U, BACK, INV = range(8)


def weights(k, west, east, south, north, z_factor):
    layer = iota_of(k, -2)
    west, east, south, north = (k + other for other in (west, east, south, north))
    axis = k.ndim - 2
    down = jnp.where(layer == 0, 0.0, z_factor * (k + shifted(k, 1, axis)))
    up = jnp.where(layer == k.shape[axis] - 1, 0.0, z_factor * (k + shifted(k, -1, axis)))
    diagonal = west + east + south + north + down + up
    rough = pl.reciprocal(diagonal, approx=True)
    rough = rough * (2.0 - diagonal * rough)
    inverse = rough * (2.0 * relaxation - relaxation * (diagonal * rough))
    inverse = jnp.where(k > 0.0, inverse, 0.0)
    scaled = [inverse * face for face in (west, east, south, north, down, up)]
    return scaled + [(0.5 / relaxation) * diagonal, 2.0 * inverse]


def fine_coefficients(k_ref, s_ref, co, g_ref, low, high, chunk):
    def body(at, size):
        here, before, after = pl.ds(at, size), pl.ds(at - 1, size), pl.ds(at + 1, size)
        k = [k_ref[here, s] for s in range(2)]
        sides = ((shifted(k[1], 1, 2), k[1]), (k[0], shifted(k[0], -1, 2)))
        for s in range(2):
            found = weights(k[s], k_ref[before, s], k_ref[after, s], *sides[s], z_coupling)
            for which in range(INV):
                co[which, here, s] = found[which]
            g_ref[here, s] = found[INV] * s_ref[here, s]

    rows_loop(low, high, chunk, body)


def mid_coefficients(k_ref, co, low, high, chunk):
    def body(at, size):
        here = pl.ds(at, size)
        k = k_ref[here]
        found = weights(
            k, k_ref[pl.ds(at - 1, size)], k_ref[pl.ds(at + 1, size)], shifted(k, 1, 2), shifted(k, -1, 2),
            4.0 * z_coupling,
        )
        for which in range(INV + 1):
            co[which, here] = found[which]

    rows_loop(low, high, chunk, body)


def swept_fine(v_ref, co, g_ref, at, size):
    here = pl.ds(at, size)
    around = v_ref[pl.ds(at - 1, size + 2)]
    v = [around[1:-1, s] for s in range(2)]
    sides = ((shifted(v[1], 1, 2), v[1]), (v[0], shifted(v[0], -1, 2)))
    new = []
    for s in range(2):
        total = g_ref[here, s] + (1.0 - relaxation) * v[s]
        total = total + co[W, here, s] * around[:-2, s]
        total = total + co[E, here, s] * around[2:, s]
        total = total + co[D, here, s] * shifted(v[s], 1, 1)
        total = total + co[U, here, s] * shifted(v[s], -1, 1)
        total = total + co[S, here, s] * sides[s][0]
        total = total + co[N, here, s] * sides[s][1]
        new.append(total)
    return v, new


def swept(v_ref, co, g_ref, at, size):
    here = pl.ds(at, size)
    around = v_ref[pl.ds(at - 1, size + 2)]
    v = around[1:-1]
    total = g_ref[here] + (1.0 - relaxation) * v
    total = total + co[W, here] * around[:-2]
    total = total + co[E, here] * around[2:]
    total = total + co[D, here] * shifted(v, 1, 1)
    total = total + co[U, here] * shifted(v, -1, 1)
    total = total + co[S, here] * shifted(v, 1, 2)
    total = total + co[N, here] * shifted(v, -1, 2)
    return v, total


def sweep_fine(v_ref, out_ref, co, g_ref, low, high):
    def body(at, size):
        new = swept_fine(v_ref, co, g_ref, at, size)[1]
        for s in range(2):
            out_ref[pl.ds(at, size), s] = new[s]

    rows_loop(low, high, FINE_CHUNK, body)


def sweep(v_ref, out_ref, co, g_ref, low, high):
    def body(at, size):
        out_ref[pl.ds(at, size)] = swept(v_ref, co, g_ref, at, size)[1]

    rows_loop(low, high, CHUNK, body)


FINE_CHUNK = 80
CHUNK = 64
DOWN_CHUNK = 36
FINE_SET = 80
MID_SET = 40
LOW_SET = 64
ADD_CHUNK = 15


def coarse_rows(values, place_ref):
    per = LANES // (HALF // 2)
    count, layers = values.shape[:2]
    pick = one_hot((LANES, LANES), lambda row, col: (row < HALF) & (row == 2 * col))
    cells = exact_dot(values.reshape(count * layers, LANES), pick).reshape(count // per, per, layers, LANES)
    packed = [shifted(cells[:, g], (place_ref[3] + g) % per * (HALF // 2), 2) for g in range(per)]
    return packed[0] + packed[1] + packed[2] + packed[3]


RIGHT_SLOT = (0, 2, 1, 3)
LEFT_SLOT = (3, 5, 4, 6)
PAIRS = HALO // 2


def cut_kernel(rows, place_ref, both, own, xa, xb, ya, yb, ba, bb):
    layers = own.shape[2]
    pick = [[pl.ds(which * layers * rows + r, layers, stride=rows) for which in range(2)] for r in range(rows)]
    left = jnp.concatenate(
        [jnp.concatenate([both[at, :] for at in pair], axis=1) for pair in pick], axis=0
    )

    def place(row, col):
        y = row % LANES
        return col == (row // LANES) * LANES + (y % 2) * HALF + y // 2

    sorted_y = exact_dot(left, one_hot((2 * LANES, 2 * LANES), place))
    parts = []
    for which in range(2):
        part = sorted_y[:, which * LANES : (which + 1) * LANES].reshape(rows, layers, LANES)
        own[:, which] = part
        pairs = part.reshape(rows // 2, 2, layers, LANES)
        parts += [pairs[:, 0], pairs[:, 1]]
    even_x, even_y = place_ref[0] == 0, place_ref[1] == 0
    low, high = jnp.where(even_x, rows - HALO, 0), jnp.where(even_x, 0, rows - HALO)
    xa[...] = own[pl.ds(low, HALO)]
    xb[...] = own[pl.ds(high, HALO)]
    slot = (iota_of(parts[0], 2) // SLOT) % 4
    for g in range(4):
        right = shifted(parts[g], RIGHT_SLOT[g] * SLOT, 2)
        left = shifted(parts[g], (LEFT_SLOT[g] - 3) * SLOT, 2)
        first = right if g == 0 else jnp.where(slot == RIGHT_SLOT[g] % 4, right, first)
        last = left if g == 0 else jnp.where(slot == LEFT_SLOT[g] % 4, left, last)
    ya[...] = jnp.where(even_y, last, first)
    yb[...] = jnp.where(even_y, first, last)
    ba[...] = ya[pl.ds(high // 2, PAIRS)]
    bb[...] = yb[pl.ds(high // 2, PAIRS)]


def widen(rows, place_ref, own, xa, xb, ya, yb, aa, ab, ba, bb, s_ref, k_ref):
    even_x, even_y = place_ref[0] == 0, place_ref[1] == 0
    inner_x, inner_y = place_ref[4] != 0, place_ref[5] != 0
    inner_both = jnp.logical_and(inner_x, inner_y)
    beside = pl.ds(jnp.where(even_x, 0, rows // 2 - PAIRS), PAIRS)
    xa, ya, aa, ab = xa[...], ya[...], aa[beside], ab[beside]
    xb, ba = (jnp.where(inner_x, ref[...], 0.0) for ref in (xb, ba))
    yb, ab = (jnp.where(inner_y, part, 0.0) for part in (yb[...], ab))
    bb = jnp.where(inner_both, bb[...], 0.0)
    before = [jnp.where(even_x, b, a) for a, b in ((aa, ba), (ab, bb))]
    after = [jnp.where(even_x, a, b) for a, b in ((aa, ba), (ab, bb))]
    for start, inner, (a, b) in (
        (0, jnp.where(even_x, xb, xa), before),
        (HALO, own[...], (ya, yb)),
        (HALO + rows, jnp.where(even_x, xa, xb), after),
    ):
        right, left = jnp.where(even_y, a, b), jnp.where(even_y, b, a)
        lane = iota_of(right, 2)
        odd_slot = (lane // SLOT) % 2 == 1
        merged = (jnp.where(odd_slot, left, right), jnp.where(odd_slot, right, left))
        count, layers = right.shape[:2]
        pairs = inner.reshape(count, 2, 2, layers, LANES)
        for which, wide in enumerate((s_ref, k_ref)):
            found = []
            for h in range(2):
                slot = RIGHT_SLOT[2 * which + h]
                block = pairs[:, h, which]
                found.append((
                    jnp.where(lane < HALF, block, shifted(merged[which], HALF - slot * SLOT, 2)),
                    jnp.where(lane < HALF, shifted(block, HALF, 2), shifted(merged[which], -slot * SLOT, 2)),
                ))
            for s in range(2):
                both = jnp.stack([found[0][s], found[1][s]], axis=1)
                wide[pl.ds(start, 2 * count), s] = both.reshape(2 * count, layers, LANES)


def descend_kernel(
    rows, place_ref, own, xa, xb, ya, yb, aa, ab, ba, bb,
    fine_u, fine_g, fine_co, mid_v, mid_g, mid_co, packed, s_ref, k_ref, k1,
):
    h0, h1, m = HALO, HALO // 2, rows // 2
    half = h0 + m
    widen(rows, place_ref, own, xa, xb, ya, yb, aa, ab, ba, bb, s_ref, k_ref)

    def coarser(at, size):
        here = pl.ds(2 * at, 2 * size)
        k1[pl.ds(at, size)] = 0.25 * pair_sum_rows(k_ref[here, 0] + k_ref[here, 1])

    rows_loop(0, half, 20, coarser)
    fine_coefficients(k_ref, s_ref, fine_co, fine_g, h0 - 22, h0 + rows + 22, FINE_SET)
    mid_coefficients(k1, mid_co, h1 - 10, h1 + m + 10, MID_SET)
    descend(rows, place_ref, fine_g, fine_u, fine_g, fine_co, mid_v, mid_g, mid_co, 10, packed, k1[pl.ds(h1, m)])


def descend(rows, place_ref, fine_first, fine_u, fine_g, fine_co, mid_v, mid_g, mid_co, reach, packed, k1=None):
    h0, h1, m = HALO, HALO // 2, rows // 2
    sweep_fine(fine_first, fine_u, fine_co, fine_g, h0 - 2 * reach - 1, h0 + rows + 2 * reach + 1)

    def down(at, size):
        v, new = swept_fine(fine_u, fine_co, fine_g, 2 * at, 2 * size)
        here = pl.ds(2 * at, 2 * size)
        left = fine_co[BACK, here, 0] * (new[0] - v[0]) + fine_co[BACK, here, 1] * (new[1] - v[1])
        mid_g[pl.ds(at, size)] = mid_co[INV, pl.ds(at, size)] * pair_sum_rows(left)

    rows_loop(h1 - reach, h1 + m + reach, DOWN_CHUNK, down)
    sweep(mid_g, mid_v, mid_co, mid_g, h1 - reach + 1, h1 + m + reach - 1)
    v, new = swept(mid_v, mid_co, mid_g, h1, m)
    left = mid_co[BACK, pl.ds(h1, m)] * (new - v)
    low = left if k1 is None else jnp.concatenate([left, 0.25 * k1], axis=0)
    low = coarse_rows(pair_sum_lanes(pair_sum_rows(low)), place_ref)
    for which in range(low.shape[0] // packed.shape[0]):
        for p in range(packed.shape[0]):
            packed[p, which] = low[which * packed.shape[0] + p]


def unpack(place_ref, mine, other, which, target, scale, npx, npy, block):
    even_x = place_ref[0] == 0
    per = 4
    width = LANES // per
    group_of = 4 if npx % 4 == 0 else 1

    def body(step, carry):
        for i in range(group_of):
            ix = step * group_of + i
            for p in range(block // per):
                for q in range(npy // per):
                    devices = [ix * npy + per * q + j for j in range(per)]
                    here = even_x if p == 0 else jnp.logical_not(even_x)
                    parts = [jnp.where(here, mine[i, which], other[i, which]) for i in devices]
                    group = iota_of(parts[0], 1) // width
                    for g in range(per):
                        row = parts[-g % per]
                        for quarter in range(1, per):
                            row = jnp.where(group == quarter, parts[(quarter - g) % per], row)
                        row = shifted(row, -g * width, 1)
                        at = PAD + ix * block + per * p + g
                        lanes = pl.ds(q * LANES, LANES)
                        if scale is not None:
                            row = row * scale[INV, at, :, lanes]
                        target[at, :, lanes] = row
        return carry

    lax.fori_loop(0, npx // group_of, body, 0)


def coarse_coefficients(rows2, strips_ref, k2, co, sums):
    width = k2.shape[2]

    def body(at, size):
        k = k2[pl.ds(at, size)]
        lane = iota_of(k, 2)
        open_s, open_n = lane > 0, lane < width - 1
        found = weights(
            k, k2[pl.ds(at - 1, size)], k2[pl.ds(at + 1, size)],
            jnp.where(open_s, shifted(k, 1, 2), 0.0), jnp.where(open_n, shifted(k, -1, 2), 0.0), 16.0 * z_coupling,
        )
        found[S] = jnp.where(open_s, found[S], 0.0)
        found[N] = jnp.where(open_n, found[N], 0.0)
        for which in range(INV + 1):
            co[which, pl.ds(at, size)] = found[which]

    rows_loop(PAD, PAD + rows2, LOW_SET, body)
    zero = jnp.zeros(k2.shape[1:], F32)
    for start, end in strips(strips_ref):
        co[W, PAD + start] = zero
        co[E, PAD + end - 1] = zero
    sums[...] = 1.0 / (relaxation * strip_sums(co.at[BACK], strips_ref, rows2, sums))


def strips(strips_ref):
    ends = [0]
    for index in range(strips_ref.shape[0]):
        ends.append(ends[-1] + strips_ref[index])
    return list(zip(ends[:-1], ends[1:]))


def strip_sums(values, strips_ref, rows2, scratch):
    whole = values[pl.ds(PAD, rows2)]
    row = iota_of(whole, 0)
    before = 0.0
    last = scratch.shape[0] - 1
    for index, (_, end) in enumerate(strips(strips_ref)):
        until = jnp.sum(whole if index == last else jnp.where(row < end, whole, 0.0), axis=0)
        scratch[index] = until - before
        before = until
    total = jnp.sum(jnp.sum(scratch[...], axis=2, keepdims=True), axis=1, keepdims=True)
    return jnp.broadcast_to(total, scratch.shape)


def coarse_solve(rows2, strips_ref, co, sums, g, a, b, over):
    zero = jnp.zeros(g.shape[1:], F32)
    for ref in (g, a, b):
        ref[PAD - 1] = zero
        ref[PAD + rows2] = zero
    for r in range(PAD - 1):
        b[r] = zero
        b[PAD + rows2 + 1 + r] = zero
    at = g
    for index in range(COARSE_SWEEPS - 1):
        to = b if index % 2 == 0 else a
        sweep(at, to, co, g, PAD, PAD + rows2)
        at = to

    def left(first, size):
        v, new = swept(b, co, g, first, size)
        a[pl.ds(first, size)] = co[BACK, pl.ds(first, size)] * (new - v)

    rows_loop(PAD, PAD + rows2, CHUNK, left)
    over[...] = sums[...] * strip_sums(a, strips_ref, rows2, over)


def correct(rows, place_ref, strips_ref, e2, over, mid_v, target, reach):
    h1, m = HALO // 2, rows // 2
    low = -(-reach // 2)
    block = rows // 4
    layers, width = e2.shape[1:]
    span = block + 2 * low
    first_row = place_ref[2] * block - low
    window = e2[pl.ds(first_row + PAD, span)]
    row = iota_of(window, 0) + first_row
    for index, (start, end) in enumerate(strips(strips_ref)):
        window = window + jnp.where((row >= start) & (row < end), over[index][None], 0.0)
    first = place_ref[3] * (HALF // 2)

    def place(row, col):
        from_own = jnp.where(col >= LANES - SLOT, col - LANES, col)
        used = (col < HALF + SLOT) | (col >= LANES - SLOT)
        return used & (row == (from_own + LANES) // 2 - HALF + first)

    spread = exact_dot(window.reshape(span * layers, width), one_hot((width, LANES), place))
    spread = spread.reshape(span, layers, LANES)
    wide = jnp.broadcast_to(spread[:, None], (span, 2, layers, LANES)).reshape(2 * span, layers, LANES)
    start = (h1 - reach) - 2 * (h1 // 2 - low)
    here = pl.ds(h1 - reach, m + 2 * reach)
    target[here] = mid_v[here] + wide[start : start + m + 2 * reach]


def ascend(rows, reach, fine_reach, mid_a, mid_b, mid_co, mid_g, fine_u, fine_a, fine_b, fine_co, fine_g):
    h0, h1, m = HALO, HALO // 2, rows // 2
    sweep(mid_a, mid_b, mid_co, mid_g, h1 - reach + 1, h1 + m + reach - 1)
    sweep(mid_b, mid_a, mid_co, mid_g, h1 - reach + 2, h1 + m + reach - 2)

    def add(at, size):
        fine = fine_u[pl.ds(2 * at, 2 * size)]
        both = fine.reshape((size, 2) + fine.shape[1:]) + mid_a[pl.ds(at, size)][:, None, None]
        fine_a[pl.ds(2 * at, 2 * size)] = both.reshape(fine.shape)

    rows_loop(h1 - reach + 2, h1 + m + reach - 2, ADD_CHUNK, add)
    sweep_fine(fine_a, fine_b, fine_co, fine_g, h0 - fine_reach - 1, h0 + rows + fine_reach + 1)
    sweep_fine(fine_b, fine_a, fine_co, fine_g, h0 - fine_reach, h0 + rows + fine_reach)


def middle_kernel(
    rows, npx, npy, place_ref, strips_ref, mine, other, fine_u, fine_g, fine_co, mid_v, mid_g, mid_co,
    fine_out, mid_v_out, mid_g_out, packed, low_co, sums,
    k2, g2, a2, b2, over, va, vb, fa, fb,
):
    block = rows // 4
    rows2 = npx * block
    zero = jnp.zeros(k2.shape[1:], F32)
    k2[PAD - 1] = zero
    k2[PAD + rows2] = zero
    unpack(place_ref, mine, other, 1, k2, None, npx, npy, block)
    coarse_coefficients(rows2, strips_ref, k2, low_co, sums)
    unpack(place_ref, mine, other, 0, g2, low_co, npx, npy, block)
    coarse_solve(rows2, strips_ref, low_co, sums, g2, a2, b2, over)
    correct(rows, place_ref, strips_ref, b2, over, mid_v, va, 9)
    ascend(rows, 9, 11, va, vb, mid_co, mid_g, fine_u, fa, fb, fine_co, fine_g)
    sweep_fine(fa, fb, fine_co, fine_g, HALO - 10, HALO + rows + 10)
    descend(rows, place_ref, fb, fine_out, fine_g, fine_co, mid_v_out, mid_g_out, mid_co, 4, packed)


def last_kernel(
    rows, npx, npy, place_ref, strips_ref, mine, other, fine_u, fine_g, fine_co, mid_v, mid_g, mid_co, low_co, sums,
    out, g2, a2, b2, over, va, vb, fa, fb,
):
    block = rows // 4
    rows2 = npx * block
    unpack(place_ref, mine, other, 0, g2, low_co, npx, npy, block)
    coarse_solve(rows2, strips_ref, low_co, sums, g2, a2, b2, over)
    correct(rows, place_ref, strips_ref, b2, over, mid_v, va, 3)
    ascend(rows, 3, 0, va, vb, mid_co, mid_g, fine_u, fa, fb, fine_co, fine_g)
    layers = fa.shape[2]
    here = pl.ds(HALO, rows)
    even, odd = fa[here, 0], fa[here, 1]
    both = jnp.where(iota_of(even, 2) < HALF, even, shifted(odd, HALF, 2))

    def place(row, col):
        return col == 2 * (row % HALF) + row // HALF

    natural = exact_dot(both.reshape(rows * layers, LANES), one_hot((LANES, LANES), place))
    for r in range(rows):
        out[pl.ds(r, layers, stride=rows), :] = natural[r * layers : (r + 1) * layers]


def neighbour_swaps(xa, xb, ya, yb, ba, bb):
    npx, npy = lax.axis_size("px"), lax.axis_size("py")

    def swap(block, partner):
        pairs = []
        for x in range(npx):
            for y in range(npy):
                to_x, to_y = partner(x, y, 0 < x < npx - 1, 0 < y < npy - 1)
                pairs.append((x * npy + y, to_x * npy + to_y))
        return lax.ppermute(block, ("px", "py"), pairs)

    def far(i):
        return ((i + 1) ^ 1) - 1

    def corner(x, y, inner_x, inner_y):
        if not inner_y:
            return x ^ 1, y
        return far(x) if inner_x else x, far(y)

    ya = swap(ya, lambda x, y, inner_x, inner_y: (x, y ^ 1))
    xa = swap(xa, lambda x, y, inner_x, inner_y: (x ^ 1, y))
    yb = swap(yb, lambda x, y, inner_x, inner_y: (x, far(y)) if inner_y else (x ^ 1, y))
    xb = swap(xb, lambda x, y, inner_x, inner_y: (far(x), y) if inner_x else (x, y ^ 1))
    bb = swap(bb, corner)
    ba, xa = lax.optimization_barrier((ba, xa))
    ba = swap(ba, lambda x, y, inner_x, inner_y: (far(x) if inner_x else x, y ^ 1))
    aa, ab = (swap(part, lambda x, y, inner_x, inner_y: (x ^ 1, y)) for part in (ya, yb))
    return xa, xb, ya, yb, aa, ab, ba, bb


def arr(*shape):
    return jax.ShapeDtypeStruct(shape, F32)


def shards(source, coefficient, strip_rows):
    npx, npy = lax.axis_size("px"), lax.axis_size("py")
    layers, rows, _ = source.shape
    total, mids = rows + 2 * HALO, (rows + 2 * HALO) // 2
    rows2, width2 = npx * rows // 4, npy * LANES // 4
    px, py = lax.axis_index("px"), lax.axis_index("py")
    inner_x, inner_y = ((i > 0) & (i < n - 1) for i, n in ((px, npx), (py, npy)))
    place = jnp.stack([px % 2, py % 2, px, py, inner_x, inner_y]).astype(jnp.int32)
    fine, mid = arr(total, 2, layers, LANES), arr(mids, layers, LANES)
    low, strip_sums = arr(rows2 + 2 * PAD, layers, width2), arr(strip_rows.shape[0], layers, width2)
    fine_cos, mid_cos, low_cos = (arr(n, *item.shape) for n, item in ((7, fine), (8, mid), (8, low)))
    halo, columns, corner = (arr(*n, layers, LANES) for n in ((HALO, 2), (rows // 2,), (PAIRS,)))
    room = min(48, 12 + 24 * rows2 * layers * width2 * 4 // 2**20)

    def call(body, name, smem, vmem, out_shape, scratch):
        return pl.pallas_call(
            functools.partial(body, rows),
            out_shape=out_shape,
            in_specs=[SMEM] * smem + [VMEM] * vmem,
            out_specs=jax.tree.map(lambda _: VMEM, out_shape),
            scratch_shapes=[pltpu.VMEM(item.shape, F32) for item in scratch],
            compiler_params=pltpu.CompilerParams(vmem_limit_bytes=room * 2**20),
            name=name,
        )

    both = jnp.stack([source, coefficient]).reshape(2 * layers * rows, LANES)
    own, *sent = call(
        cut_kernel, "cut", 1, 1, (arr(rows, 2, layers, LANES),) + (halo,) * 2 + (columns,) * 2 + (corner,) * 2, ()
    )(place, both)
    fine_u, fine_g, fine_co, mid_v, mid_g, mid_co, packed = call(
        descend_kernel, "descend", 1, 9, (fine, fine, fine_cos, mid, mid, mid_cos, arr(2, 2, layers, LANES)),
        (fine, fine, mid),
    )(place, own, *neighbour_swaps(*sent))

    def gather(block):
        shape = (npx // 2, 2, npy) + block.shape[1:]
        every = jnp.broadcast_to(block[None, :, None], shape).reshape((npx * npy,) + block.shape[1:])
        half = lax.all_to_all(every, ("px", "py"), 0, 0, tiled=True)
        return half, lax.ppermute(half, "px", [(i, i ^ 1) for i in range(npx)])

    def sized(body):
        return lambda rows, *refs: body(rows, npx, npy, *refs)

    fine_u, mid_v, mid_g, packed, low_co, sums = call(
        sized(middle_kernel), "middle", 2, 8, (fine, mid, mid, arr(2, 1, layers, LANES), low_cos, strip_sums),
        (low, low, low, low, strip_sums, mid, mid, fine, fine),
    )(place, strip_rows, *gather(packed), fine_u, fine_g, fine_co, mid_v, mid_g, mid_co)
    out = call(
        sized(last_kernel), "last", 2, 10, arr(layers * rows, LANES),
        (low, low, low, strip_sums, mid, mid, fine, fine),
    )(place, strip_rows, *gather(packed), fine_u, fine_g, fine_co, mid_v, mid_g, mid_co, low_co, sums)
    return out.reshape(source.shape)


def solution(mesh):
    placed = (P(None, "px", "py"), P(None, "px", "py"), P())
    return jax.shard_map(
        shards, mesh=mesh, in_specs=placed, out_specs=P(None, "px", "py"), check_vma=False
    )
```

```python
import functools

import jax
import jax.numpy as jnp
from jax import lax
from jax.experimental import pallas as pl
from jax.experimental.pallas import tpu as pltpu
from jax.sharding import PartitionSpec as P

COARSE_SWEEPS = 6
relaxation = 0.8
z_coupling = 0.25

HALO = 24
SIDE = 32
PAD = 8
LANES = 128
HALF = LANES // 2
SLOT = SIDE // 2
VMEM = pl.BlockSpec(memory_space=pltpu.VMEM)
SMEM = pl.BlockSpec(memory_space=pltpu.SMEM)
F32 = jnp.float32


def shifted(values, amount, axis):
    return pltpu.roll(values, amount % values.shape[axis], axis)


def iota_of(values, axis):
    return lax.broadcasted_iota(jnp.int32, values.shape, axis % values.ndim)


def rows_loop(low, high, chunk, body):
    chunk = min(chunk, high - low)
    count = -(-(high - low) // chunk)
    chunk = -(-(high - low) // count)

    def step(index, carry):
        body(jnp.minimum(low + index * chunk, high - chunk), chunk)
        return carry

    if count == 1:
        body(low, chunk)
    else:
        lax.fori_loop(0, count, step, 0)


def pair_sum_rows(values):
    count = values.shape[0] // 2
    pairs = values.reshape((count, 2) + values.shape[1:])
    return pairs[:, 0] + pairs[:, 1]


def pair_sum_lanes(values):
    return values + jnp.where(iota_of(values, -1) % 2 == 0, shifted(values, -1, 2), shifted(values, 1, 2))


def exact_dot(left, right):
    total = None
    for last in (False, False, True):
        part = left.astype(jnp.bfloat16)
        term = lax.dot_general(part, right, (((1,), (0,)), ((), ())), preferred_element_type=F32)
        total = term if total is None else total + term
        if not last:
            left = left - part.astype(F32)
    return total


def one_hot(shape, place):
    row = lax.broadcasted_iota(jnp.int32, shape, 0)
    col = lax.broadcasted_iota(jnp.int32, shape, 1)
    return jnp.where(place(row, col), 1.0, 0.0).astype(jnp.bfloat16)


W, E, S, N, D, U, BACK, INV = range(8)


def weights(k, west, east, south, north, z_factor):
    layer = iota_of(k, -2)
    west, east, south, north = (k + other for other in (west, east, south, north))
    axis = k.ndim - 2
    down = jnp.where(layer == 0, 0.0, z_factor * (k + shifted(k, 1, axis)))
    up = jnp.where(layer == k.shape[axis] - 1, 0.0, z_factor * (k + shifted(k, -1, axis)))
    diagonal = west + east + south + north + down + up
    rough = pl.reciprocal(diagonal, approx=True)
    rough = rough * (2.0 - diagonal * rough)
    inverse = rough * (2.0 * relaxation - relaxation * (diagonal * rough))
    inverse = jnp.where(k > 0.0, inverse, 0.0)
    scaled = [inverse * face for face in (west, east, south, north, down, up)]
    return scaled + [(0.5 / relaxation) * diagonal, 2.0 * inverse]


def fine_coefficients(k_ref, s_ref, co, g_ref, low, high, chunk):
    def body(at, size):
        here, before, after = pl.ds(at, size), pl.ds(at - 1, size), pl.ds(at + 1, size)
        k = [k_ref[here, s] for s in range(2)]
        sides = ((shifted(k[1], 1, 2), k[1]), (k[0], shifted(k[0], -1, 2)))
        for s in range(2):
            found = weights(k[s], k_ref[before, s], k_ref[after, s], *sides[s], z_coupling)
            for which in range(INV):
                co[which, here, s] = found[which]
            g_ref[here, s] = found[INV] * s_ref[here, s]

    rows_loop(low, high, chunk, body)


def mid_coefficients(k_ref, co, low, high, chunk):
    def body(at, size):
        here = pl.ds(at, size)
        k = k_ref[here]
        found = weights(
            k, k_ref[pl.ds(at - 1, size)], k_ref[pl.ds(at + 1, size)], shifted(k, 1, 2), shifted(k, -1, 2),
            4.0 * z_coupling,
        )
        for which in range(INV + 1):
            co[which, here] = found[which]

    rows_loop(low, high, chunk, body)


def swept_fine(v_ref, co, g_ref, at, size):
    here = pl.ds(at, size)
    around = v_ref[pl.ds(at - 1, size + 2)]
    v = [around[1:-1, s] for s in range(2)]
    sides = ((shifted(v[1], 1, 2), v[1]), (v[0], shifted(v[0], -1, 2)))
    new = []
    for s in range(2):
        total = g_ref[here, s] + (1.0 - relaxation) * v[s]
        total = total + co[W, here, s] * around[:-2, s]
        total = total + co[E, here, s] * around[2:, s]
        total = total + co[D, here, s] * shifted(v[s], 1, 1)
        total = total + co[U, here, s] * shifted(v[s], -1, 1)
        total = total + co[S, here, s] * sides[s][0]
        total = total + co[N, here, s] * sides[s][1]
        new.append(total)
    return v, new


def swept(v_ref, co, g_ref, at, size):
    here = pl.ds(at, size)
    around = v_ref[pl.ds(at - 1, size + 2)]
    v = around[1:-1]
    total = g_ref[here] + (1.0 - relaxation) * v
    total = total + co[W, here] * around[:-2]
    total = total + co[E, here] * around[2:]
    total = total + co[D, here] * shifted(v, 1, 1)
    total = total + co[U, here] * shifted(v, -1, 1)
    total = total + co[S, here] * shifted(v, 1, 2)
    total = total + co[N, here] * shifted(v, -1, 2)
    return v, total


def sweep_fine(v_ref, out_ref, co, g_ref, low, high):
    def body(at, size):
        new = swept_fine(v_ref, co, g_ref, at, size)[1]
        for s in range(2):
            out_ref[pl.ds(at, size), s] = new[s]

    rows_loop(low, high, FINE_CHUNK, body)


def sweep(v_ref, out_ref, co, g_ref, low, high):
    def body(at, size):
        out_ref[pl.ds(at, size)] = swept(v_ref, co, g_ref, at, size)[1]

    rows_loop(low, high, CHUNK, body)


FINE_CHUNK = 80
CHUNK = 64
DOWN_CHUNK = 36
FINE_SET = 80
MID_SET = 40
LOW_SET = 64
ADD_CHUNK = 40
K1_CHUNK = 40
BLOCKS = 8


def coarse_rows(values, place_ref):
    per = LANES // (HALF // 2)
    count, layers = values.shape[:2]
    pick = one_hot((LANES, LANES), lambda row, col: (row < HALF) & (row == 2 * col))
    cells = exact_dot(values.reshape(count * layers, LANES), pick).reshape(count // per, per, layers, LANES)
    packed = [shifted(cells[:, g], (place_ref[3] + g) % per * (HALF // 2), 2) for g in range(per)]
    return packed[0] + packed[1] + packed[2] + packed[3]


RIGHT_SLOT = (0, 2, 1, 3)
LEFT_SLOT = (3, 5, 4, 6)
PAIRS = HALO // 2


def cut_kernel(rows, place_ref, both, own, xa, xb, ya, yb, ba, bb):
    layers = own.shape[2]
    pick = [[pl.ds(which * layers * rows + r, layers, stride=rows) for which in range(2)] for r in range(rows)]
    left = jnp.concatenate(
        [jnp.concatenate([both[at, :] for at in pair], axis=1) for pair in pick], axis=0
    )

    def place(row, col):
        y = row % LANES
        return col == (row // LANES) * LANES + (y % 2) * HALF + y // 2

    sorted_y = exact_dot(left, one_hot((2 * LANES, 2 * LANES), place))
    parts = []
    for which in range(2):
        part = sorted_y[:, which * LANES : (which + 1) * LANES].reshape(rows, layers, LANES)
        own[:, which] = part
        pairs = part.reshape(rows // 2, 2, layers, LANES)
        parts += [pairs[:, 0], pairs[:, 1]]
    even_x, even_y = place_ref[0] == 0, place_ref[1] == 0
    low, high = jnp.where(even_x, rows - HALO, 0), jnp.where(even_x, 0, rows - HALO)
    xa[...] = own[pl.ds(low, HALO)]
    xb[...] = own[pl.ds(high, HALO)]
    slot = (iota_of(parts[0], 2) // SLOT) % 4
    for g in range(4):
        right = shifted(parts[g], RIGHT_SLOT[g] * SLOT, 2)
        left = shifted(parts[g], (LEFT_SLOT[g] - 3) * SLOT, 2)
        first = right if g == 0 else jnp.where(slot == RIGHT_SLOT[g] % 4, right, first)
        last = left if g == 0 else jnp.where(slot == LEFT_SLOT[g] % 4, left, last)
    ya[...] = jnp.where(even_y, last, first)
    yb[...] = jnp.where(even_y, first, last)
    ba[...] = ya[pl.ds(high // 2, PAIRS)]
    bb[...] = yb[pl.ds(high // 2, PAIRS)]


def widen(rows, place_ref, own, xa, xb, ya, yb, aa, ab, ba, bb, s_ref, k_ref):
    even_x, even_y = place_ref[0] == 0, place_ref[1] == 0
    inner_x, inner_y = place_ref[4] != 0, place_ref[5] != 0
    inner_both = jnp.logical_and(inner_x, inner_y)
    beside = pl.ds(jnp.where(even_x, 0, rows // 2 - PAIRS), PAIRS)
    xa, ya, aa, ab = xa[...], ya[...], aa[beside], ab[beside]
    xb, ba = (jnp.where(inner_x, ref[...], 0.0) for ref in (xb, ba))
    yb, ab = (jnp.where(inner_y, part, 0.0) for part in (yb[...], ab))
    bb = jnp.where(inner_both, bb[...], 0.0)
    before = [jnp.where(even_x, b, a) for a, b in ((aa, ba), (ab, bb))]
    after = [jnp.where(even_x, a, b) for a, b in ((aa, ba), (ab, bb))]
    for start, inner, (a, b) in (
        (0, jnp.where(even_x, xb, xa), before),
        (HALO, own[...], (ya, yb)),
        (HALO + rows, jnp.where(even_x, xa, xb), after),
    ):
        right, left = jnp.where(even_y, a, b), jnp.where(even_y, b, a)
        lane = iota_of(right, 2)
        odd_slot = (lane // SLOT) % 2 == 1
        merged = (jnp.where(odd_slot, left, right), jnp.where(odd_slot, right, left))
        count, layers = right.shape[:2]
        pairs = inner.reshape(count, 2, 2, layers, LANES)
        for which, wide in enumerate((s_ref, k_ref)):
            found = []
            for h in range(2):
                slot = RIGHT_SLOT[2 * which + h]
                block = pairs[:, h, which]
                found.append((
                    jnp.where(lane < HALF, block, shifted(merged[which], HALF - slot * SLOT, 2)),
                    jnp.where(lane < HALF, shifted(block, HALF, 2), shifted(merged[which], -slot * SLOT, 2)),
                ))
            for s in range(2):
                both = jnp.stack([found[0][s], found[1][s]], axis=1)
                wide[pl.ds(start, 2 * count), s] = both.reshape(2 * count, layers, LANES)


def descend_kernel(
    rows, place_ref, own, xa, xb, ya, yb, aa, ab, ba, bb,
    fine_u, fine_g, fine_co, mid_v, mid_g, mid_co, packed, s_ref, k_ref, k1,
):
    h0, h1, m = HALO, HALO // 2, rows // 2
    half = h0 + m
    widen(rows, place_ref, own, xa, xb, ya, yb, aa, ab, ba, bb, s_ref, k_ref)

    def coarser(at, size):
        here = pl.ds(2 * at, 2 * size)
        k1[pl.ds(at, size)] = 0.25 * pair_sum_rows(k_ref[here, 0] + k_ref[here, 1])

    rows_loop(0, half, K1_CHUNK, coarser)
    fine_coefficients(k_ref, s_ref, fine_co, fine_g, h0 - 22, h0 + rows + 22, FINE_SET)
    mid_coefficients(k1, mid_co, h1 - 10, h1 + m + 10, MID_SET)
    descend(rows, place_ref, fine_g, fine_u, fine_g, fine_co, mid_v, mid_g, mid_co, 10, packed, k1[pl.ds(h1, m)])


def descend(rows, place_ref, fine_first, fine_u, fine_g, fine_co, mid_v, mid_g, mid_co, reach, packed, k1=None):
    h0, h1, m = HALO, HALO // 2, rows // 2
    sweep_fine(fine_first, fine_u, fine_co, fine_g, h0 - 2 * reach - 1, h0 + rows + 2 * reach + 1)

    def down(at, size):
        v, new = swept_fine(fine_u, fine_co, fine_g, 2 * at, 2 * size)
        here = pl.ds(2 * at, 2 * size)
        left = fine_co[BACK, here, 0] * (new[0] - v[0]) + fine_co[BACK, here, 1] * (new[1] - v[1])
        mid_g[pl.ds(at, size)] = mid_co[INV, pl.ds(at, size)] * pair_sum_rows(left)

    rows_loop(h1 - reach, h1 + m + reach, DOWN_CHUNK, down)
    sweep(mid_g, mid_v, mid_co, mid_g, h1 - reach + 1, h1 + m + reach - 1)
    v, new = swept(mid_v, mid_co, mid_g, h1, m)
    left = mid_co[BACK, pl.ds(h1, m)] * (new - v)
    low = left if k1 is None else jnp.concatenate([left, 0.25 * k1], axis=0)
    low = coarse_rows(pair_sum_lanes(pair_sum_rows(low)), place_ref)
    for which in range(low.shape[0] // packed.shape[0]):
        for p in range(packed.shape[0]):
            packed[p, which] = low[which * packed.shape[0] + p]


def unpack(place_ref, mine, other, which, target, scale, npx, npy, block):
    even_x = place_ref[0] == 0
    per = 4
    width = LANES // per
    group_of = BLOCKS if npx % BLOCKS == 0 else 1

    def body(step, carry):
        for i in range(group_of):
            ix = step * group_of + i
            for p in range(block // per):
                for q in range(npy // per):
                    devices = [ix * npy + per * q + j for j in range(per)]
                    here = even_x if p == 0 else jnp.logical_not(even_x)
                    parts = [jnp.where(here, mine[i, which], other[i, which]) for i in devices]
                    group = iota_of(parts[0], 1) // width
                    for g in range(per):
                        row = parts[-g % per]
                        for quarter in range(1, per):
                            row = jnp.where(group == quarter, parts[(quarter - g) % per], row)
                        row = shifted(row, -g * width, 1)
                        at = PAD + ix * block + per * p + g
                        lanes = pl.ds(q * LANES, LANES)
                        if scale is not None:
                            row = row * scale[INV, at, :, lanes]
                        target[at, :, lanes] = row
        return carry

    if npx == group_of:
        body(0, 0)
    else:
        lax.fori_loop(0, npx // group_of, body, 0)


def coarse_coefficients(rows2, strips_ref, k2, co, sums):
    width = k2.shape[2]

    def body(at, size):
        k = k2[pl.ds(at, size)]
        lane = iota_of(k, 2)
        open_s, open_n = lane > 0, lane < width - 1
        found = weights(
            k, k2[pl.ds(at - 1, size)], k2[pl.ds(at + 1, size)],
            jnp.where(open_s, shifted(k, 1, 2), 0.0), jnp.where(open_n, shifted(k, -1, 2), 0.0), 16.0 * z_coupling,
        )
        found[S] = jnp.where(open_s, found[S], 0.0)
        found[N] = jnp.where(open_n, found[N], 0.0)
        for which in range(INV + 1):
            co[which, pl.ds(at, size)] = found[which]

    rows_loop(PAD, PAD + rows2, LOW_SET, body)
    zero = jnp.zeros(k2.shape[1:], F32)
    for start, end in strips(strips_ref):
        co[W, PAD + start] = zero
        co[E, PAD + end - 1] = zero
    sums[...] = 1.0 / (relaxation * strip_sums(co.at[BACK], strips_ref, rows2, sums))


def strips(strips_ref):
    ends = [0]
    for index in range(strips_ref.shape[0]):
        ends.append(ends[-1] + strips_ref[index])
    return list(zip(ends[:-1], ends[1:]))


def strip_sums(values, strips_ref, rows2, scratch):
    whole = values[pl.ds(PAD, rows2)]
    row = iota_of(whole, 0)
    before = 0.0
    last = scratch.shape[0] - 1
    for index, (_, end) in enumerate(strips(strips_ref)):
        until = jnp.sum(whole if index == last else jnp.where(row < end, whole, 0.0), axis=0)
        scratch[index] = until - before
        before = until
    total = jnp.sum(jnp.sum(scratch[...], axis=2, keepdims=True), axis=1, keepdims=True)
    return jnp.broadcast_to(total, scratch.shape)


def coarse_solve(rows2, strips_ref, co, sums, g, a, b, over):
    zero = jnp.zeros(g.shape[1:], F32)
    for ref in (g, a, b):
        ref[PAD - 1] = zero
        ref[PAD + rows2] = zero
    for r in range(PAD - 1):
        b[r] = zero
        b[PAD + rows2 + 1 + r] = zero
    at = g
    for index in range(COARSE_SWEEPS - 1):
        to = b if index % 2 == 0 else a
        sweep(at, to, co, g, PAD, PAD + rows2)
        at = to

    def left(first, size):
        v, new = swept(b, co, g, first, size)
        a[pl.ds(first, size)] = co[BACK, pl.ds(first, size)] * (new - v)

    rows_loop(PAD, PAD + rows2, CHUNK, left)
    over[...] = sums[...] * strip_sums(a, strips_ref, rows2, over)


def correct(rows, place_ref, strips_ref, e2, over, mid_v, target, reach):
    h1, m = HALO // 2, rows // 2
    low = -(-reach // 2)
    block = rows // 4
    layers, width = e2.shape[1:]
    span = block + 2 * low
    first_row = place_ref[2] * block - low
    window = e2[pl.ds(first_row + PAD, span)]
    row = iota_of(window, 0) + first_row
    for index, (start, end) in enumerate(strips(strips_ref)):
        window = window + jnp.where((row >= start) & (row < end), over[index][None], 0.0)
    first = place_ref[3] * (HALF // 2)

    def place(row, col):
        from_own = jnp.where(col >= LANES - SLOT, col - LANES, col)
        used = (col < HALF + SLOT) | (col >= LANES - SLOT)
        return used & (row == (from_own + LANES) // 2 - HALF + first)

    spread = exact_dot(window.reshape(span * layers, width), one_hot((width, LANES), place))
    spread = spread.reshape(span, layers, LANES)
    wide = jnp.broadcast_to(spread[:, None], (span, 2, layers, LANES)).reshape(2 * span, layers, LANES)
    start = (h1 - reach) - 2 * (h1 // 2 - low)
    here = pl.ds(h1 - reach, m + 2 * reach)
    target[here] = mid_v[here] + wide[start : start + m + 2 * reach]


def ascend(rows, reach, fine_reach, mid_a, mid_b, mid_co, mid_g, fine_u, fine_a, fine_b, fine_co, fine_g):
    h0, h1, m = HALO, HALO // 2, rows // 2
    sweep(mid_a, mid_b, mid_co, mid_g, h1 - reach + 1, h1 + m + reach - 1)
    sweep(mid_b, mid_a, mid_co, mid_g, h1 - reach + 2, h1 + m + reach - 2)

    def add(at, size):
        fine = fine_u[pl.ds(2 * at, 2 * size)]
        both = fine.reshape((size, 2) + fine.shape[1:]) + mid_a[pl.ds(at, size)][:, None, None]
        fine_a[pl.ds(2 * at, 2 * size)] = both.reshape(fine.shape)

    rows_loop(h1 - reach + 2, h1 + m + reach - 2, ADD_CHUNK, add)
    sweep_fine(fine_a, fine_b, fine_co, fine_g, h0 - fine_reach - 1, h0 + rows + fine_reach + 1)
    sweep_fine(fine_b, fine_a, fine_co, fine_g, h0 - fine_reach, h0 + rows + fine_reach)


def middle_kernel(
    rows, npx, npy, place_ref, strips_ref, mine, other, fine_u, fine_g, fine_co, mid_v, mid_g, mid_co,
    fine_out, mid_v_out, mid_g_out, packed, low_co, sums,
    k2, g2, a2, b2, over, va, vb, fa, fb,
):
    block = rows // 4
    rows2 = npx * block
    zero = jnp.zeros(k2.shape[1:], F32)
    k2[PAD - 1] = zero
    k2[PAD + rows2] = zero
    unpack(place_ref, mine, other, 1, k2, None, npx, npy, block)
    coarse_coefficients(rows2, strips_ref, k2, low_co, sums)
    unpack(place_ref, mine, other, 0, g2, low_co, npx, npy, block)
    coarse_solve(rows2, strips_ref, low_co, sums, g2, a2, b2, over)
    correct(rows, place_ref, strips_ref, b2, over, mid_v, va, 9)
    ascend(rows, 9, 11, va, vb, mid_co, mid_g, fine_u, fa, fb, fine_co, fine_g)
    sweep_fine(fa, fb, fine_co, fine_g, HALO - 10, HALO + rows + 10)
    descend(rows, place_ref, fb, fine_out, fine_g, fine_co, mid_v_out, mid_g_out, mid_co, 4, packed)


def last_kernel(
    rows, npx, npy, place_ref, strips_ref, mine, other, fine_u, fine_g, fine_co, mid_v, mid_g, mid_co, low_co, sums,
    out, g2, a2, b2, over, va, vb, fa, fb,
):
    block = rows // 4
    rows2 = npx * block
    unpack(place_ref, mine, other, 0, g2, low_co, npx, npy, block)
    coarse_solve(rows2, strips_ref, low_co, sums, g2, a2, b2, over)
    correct(rows, place_ref, strips_ref, b2, over, mid_v, va, 3)
    ascend(rows, 3, 0, va, vb, mid_co, mid_g, fine_u, fa, fb, fine_co, fine_g)
    layers = fa.shape[2]
    here = pl.ds(HALO, rows)
    even, odd = fa[here, 0], fa[here, 1]
    both = jnp.where(iota_of(even, 2) < HALF, even, shifted(odd, HALF, 2))

    def place(row, col):
        return col == 2 * (row % HALF) + row // HALF

    natural = exact_dot(both.reshape(rows * layers, LANES), one_hot((LANES, LANES), place))
    for r in range(rows):
        out[pl.ds(r, layers, stride=rows), :] = natural[r * layers : (r + 1) * layers]


def neighbour_swaps(xa, xb, ya, yb, ba, bb):
    npx, npy = lax.axis_size("px"), lax.axis_size("py")

    def swap(block, partner):
        pairs = []
        for x in range(npx):
            for y in range(npy):
                to_x, to_y = partner(x, y, 0 < x < npx - 1, 0 < y < npy - 1)
                pairs.append((x * npy + y, to_x * npy + to_y))
        return lax.ppermute(block, ("px", "py"), pairs)

    def far(i):
        return ((i + 1) ^ 1) - 1

    def corner(x, y, inner_x, inner_y):
        if not inner_y:
            return x ^ 1, y
        return far(x) if inner_x else x, far(y)

    ya = swap(ya, lambda x, y, inner_x, inner_y: (x, y ^ 1))
    xa = swap(xa, lambda x, y, inner_x, inner_y: (x ^ 1, y))
    yb = swap(yb, lambda x, y, inner_x, inner_y: (x, far(y)) if inner_y else (x ^ 1, y))
    xb = swap(xb, lambda x, y, inner_x, inner_y: (far(x), y) if inner_x else (x, y ^ 1))
    ba, bb, xa = lax.optimization_barrier((ba, bb, xa))
    bb = swap(bb, corner)
    ba = swap(ba, lambda x, y, inner_x, inner_y: (far(x) if inner_x else x, y ^ 1))
    aa, ab = (swap(part, lambda x, y, inner_x, inner_y: (x ^ 1, y)) for part in (ya, yb))
    return xa, xb, ya, yb, aa, ab, ba, bb


def arr(*shape):
    return jax.ShapeDtypeStruct(shape, F32)


def shards(source, coefficient, strip_rows):
    npx, npy = lax.axis_size("px"), lax.axis_size("py")
    layers, rows, _ = source.shape
    total, mids = rows + 2 * HALO, (rows + 2 * HALO) // 2
    rows2, width2 = npx * rows // 4, npy * LANES // 4
    px, py = lax.axis_index("px"), lax.axis_index("py")
    inner_x, inner_y = ((i > 0) & (i < n - 1) for i, n in ((px, npx), (py, npy)))
    place = jnp.stack([px % 2, py % 2, px, py, inner_x, inner_y]).astype(jnp.int32)
    fine, mid = arr(total, 2, layers, LANES), arr(mids, layers, LANES)
    low, strip_sums = arr(rows2 + 2 * PAD, layers, width2), arr(strip_rows.shape[0], layers, width2)
    fine_cos, mid_cos, low_cos = (arr(n, *item.shape) for n, item in ((7, fine), (8, mid), (8, low)))
    halo, columns, corner = (arr(*n, layers, LANES) for n in ((HALO, 2), (rows // 2,), (PAIRS,)))
    room = min(48, 12 + 24 * rows2 * layers * width2 * 4 // 2**20)

    def call(body, name, smem, vmem, out_shape, scratch):
        return pl.pallas_call(
            functools.partial(body, rows),
            out_shape=out_shape,
            in_specs=[SMEM] * smem + [VMEM] * vmem,
            out_specs=jax.tree.map(lambda _: VMEM, out_shape),
            scratch_shapes=[pltpu.VMEM(item.shape, F32) for item in scratch],
            compiler_params=pltpu.CompilerParams(vmem_limit_bytes=room * 2**20),
            name=name,
        )

    both = jnp.stack([source, coefficient]).reshape(2 * layers * rows, LANES)
    own, *sent = call(
        cut_kernel, "cut", 1, 1, (arr(rows, 2, layers, LANES),) + (halo,) * 2 + (columns,) * 2 + (corner,) * 2, ()
    )(place, both)
    fine_u, fine_g, fine_co, mid_v, mid_g, mid_co, packed = call(
        descend_kernel, "descend", 1, 9, (fine, fine, fine_cos, mid, mid, mid_cos, arr(2, 2, layers, LANES)),
        (fine, fine, mid),
    )(place, own, *neighbour_swaps(*sent))

    def gather(block):
        shape = (npx // 2, 2, npy) + block.shape[1:]
        every = jnp.broadcast_to(block[None, :, None], shape).reshape((npx * npy,) + block.shape[1:])
        half = lax.all_to_all(every, ("px", "py"), 0, 0, tiled=True)
        return half, lax.ppermute(half, "px", [(i, i ^ 1) for i in range(npx)])

    def sized(body):
        return lambda rows, *refs: body(rows, npx, npy, *refs)

    fine_u, mid_v, mid_g, packed, low_co, sums = call(
        sized(middle_kernel), "middle", 2, 8, (fine, mid, mid, arr(2, 1, layers, LANES), low_cos, strip_sums),
        (low, low, low, low, strip_sums, mid, mid, fine, fine),
    )(place, strip_rows, *gather(packed), fine_u, fine_g, fine_co, mid_v, mid_g, mid_co)
    out = call(
        sized(last_kernel), "last", 2, 10, arr(layers * rows, LANES),
        (low, low, low, strip_sums, mid, mid, fine, fine),
    )(place, strip_rows, *gather(packed), fine_u, fine_g, fine_co, mid_v, mid_g, mid_co, low_co, sums)
    return out.reshape(source.shape)


def solution(mesh):
    placed = (P(None, "px", "py"), P(None, "px", "py"), P())
    return jax.shard_map(
        shards, mesh=mesh, in_specs=placed, out_specs=P(None, "px", "py"), check_vma=False
    )
```

```python
import functools

import jax
import jax.numpy as jnp
from jax import lax
from jax.experimental import pallas as pl
from jax.experimental.pallas import tpu as pltpu
from jax.sharding import PartitionSpec as P

COARSE_SWEEPS = 6
relaxation = 0.8
z_coupling = 0.25

HALO = 24
SIDE = 32
PAD = 8
LANES = 128
HALF = LANES // 2
SLOT = SIDE // 2
VMEM = pl.BlockSpec(memory_space=pltpu.VMEM)
SMEM = pl.BlockSpec(memory_space=pltpu.SMEM)
F32 = jnp.float32


def shifted(values, amount, axis):
    return pltpu.roll(values, amount % values.shape[axis], axis)


def iota_of(values, axis):
    return lax.broadcasted_iota(jnp.int32, values.shape, axis % values.ndim)


def rows_loop(low, high, chunk, body):
    chunk = min(chunk, high - low)
    count = -(-(high - low) // chunk)
    chunk = -(-(high - low) // count)

    def step(index, carry):
        body(jnp.minimum(low + index * chunk, high - chunk), chunk)
        return carry

    if count == 1:
        body(low, chunk)
    else:
        lax.fori_loop(0, count, step, 0)


def pair_sum_rows(values):
    count = values.shape[0] // 2
    pairs = values.reshape((count, 2) + values.shape[1:])
    return pairs[:, 0] + pairs[:, 1]


def pair_sum_lanes(values):
    return values + jnp.where(iota_of(values, -1) % 2 == 0, shifted(values, -1, 2), shifted(values, 1, 2))


def exact_dot(left, right):
    total = None
    for last in (False, False, True):
        part = left.astype(jnp.bfloat16)
        term = lax.dot_general(part, right, (((1,), (0,)), ((), ())), preferred_element_type=F32)
        total = term if total is None else total + term
        if not last:
            left = left - part.astype(F32)
    return total


def one_hot(shape, place):
    row = lax.broadcasted_iota(jnp.int32, shape, 0)
    col = lax.broadcasted_iota(jnp.int32, shape, 1)
    return jnp.where(place(row, col), 1.0, 0.0).astype(jnp.bfloat16)


W, E, S, N, D, U, BACK, INV = range(8)


def weights(k, west, east, south, north, z_factor):
    layer = iota_of(k, -2)
    west, east, south, north = (k + other for other in (west, east, south, north))
    axis = k.ndim - 2
    down = jnp.where(layer == 0, 0.0, z_factor * (k + shifted(k, 1, axis)))
    up = jnp.where(layer == k.shape[axis] - 1, 0.0, z_factor * (k + shifted(k, -1, axis)))
    diagonal = west + east + south + north + down + up
    rough = pl.reciprocal(diagonal, approx=True)
    rough = rough * (2.0 - diagonal * rough)
    inverse = rough * (2.0 * relaxation - relaxation * (diagonal * rough))
    inverse = jnp.where(k > 0.0, inverse, 0.0)
    scaled = [inverse * face for face in (west, east, south, north, down, up)]
    return scaled + [(0.5 / relaxation) * diagonal, 2.0 * inverse]


def fine_coefficients(k_ref, s_ref, co, g_ref, low, high, chunk):
    def body(at, size):
        here, before, after = pl.ds(at, size), pl.ds(at - 1, size), pl.ds(at + 1, size)
        k = [k_ref[here, s] for s in range(2)]
        sides = ((shifted(k[1], 1, 2), k[1]), (k[0], shifted(k[0], -1, 2)))
        for s in range(2):
            found = weights(k[s], k_ref[before, s], k_ref[after, s], *sides[s], z_coupling)
            for which in range(INV):
                co[which, here, s] = found[which]
            g_ref[here, s] = found[INV] * s_ref[here, s]

    rows_loop(low, high, chunk, body)


def mid_coefficients(k_ref, co, low, high, chunk):
    def body(at, size):
        here = pl.ds(at, size)
        k = k_ref[here]
        found = weights(
            k, k_ref[pl.ds(at - 1, size)], k_ref[pl.ds(at + 1, size)], shifted(k, 1, 2), shifted(k, -1, 2),
            4.0 * z_coupling,
        )
        for which in range(INV + 1):
            co[which, here] = found[which]

    rows_loop(low, high, chunk, body)


def swept_fine(v_ref, co, g_ref, at, size):
    here = pl.ds(at, size)
    around = v_ref[pl.ds(at - 1, size + 2)]
    v = [around[1:-1, s] for s in range(2)]
    sides = ((shifted(v[1], 1, 2), v[1]), (v[0], shifted(v[0], -1, 2)))
    new = []
    for s in range(2):
        total = g_ref[here, s] + (1.0 - relaxation) * v[s]
        total = total + co[W, here, s] * around[:-2, s]
        total = total + co[E, here, s] * around[2:, s]
        total = total + co[D, here, s] * shifted(v[s], 1, 1)
        total = total + co[U, here, s] * shifted(v[s], -1, 1)
        total = total + co[S, here, s] * sides[s][0]
        total = total + co[N, here, s] * sides[s][1]
        new.append(total)
    return v, new


def swept(v_ref, co, g_ref, at, size):
    here = pl.ds(at, size)
    around = v_ref[pl.ds(at - 1, size + 2)]
    v = around[1:-1]
    total = g_ref[here] + (1.0 - relaxation) * v
    total = total + co[W, here] * around[:-2]
    total = total + co[E, here] * around[2:]
    total = total + co[D, here] * shifted(v, 1, 1)
    total = total + co[U, here] * shifted(v, -1, 1)
    total = total + co[S, here] * shifted(v, 1, 2)
    total = total + co[N, here] * shifted(v, -1, 2)
    return v, total


def sweep_fine(v_ref, out_ref, co, g_ref, low, high):
    def body(at, size):
        new = swept_fine(v_ref, co, g_ref, at, size)[1]
        for s in range(2):
            out_ref[pl.ds(at, size), s] = new[s]

    rows_loop(low, high, FINE_CHUNK, body)


def sweep(v_ref, out_ref, co, g_ref, low, high):
    def body(at, size):
        out_ref[pl.ds(at, size)] = swept(v_ref, co, g_ref, at, size)[1]

    rows_loop(low, high, CHUNK, body)


FINE_CHUNK = 80
CHUNK = 64
DOWN_CHUNK = 36
FINE_SET = 80
MID_SET = 40
LOW_SET = 64
ADD_CHUNK = 40
K1_CHUNK = 40
BLOCKS = 8


def coarse_rows(values, place_ref):
    per = LANES // (HALF // 2)
    count, layers = values.shape[:2]
    pick = one_hot((LANES, LANES), lambda row, col: (row < HALF) & (row == 2 * col))
    cells = exact_dot(values.reshape(count * layers, LANES), pick).reshape(count // per, per, layers, LANES)
    packed = [shifted(cells[:, g], (place_ref[3] + g) % per * (HALF // 2), 2) for g in range(per)]
    return packed[0] + packed[1] + packed[2] + packed[3]


RIGHT_SLOT = (0, 2, 1, 3)
LEFT_SLOT = (3, 5, 4, 6)
PAIRS = HALO // 2


def cut_kernel(rows, place_ref, both, own, xa, xb, ya, yb, ba, bb):
    layers = own.shape[2]
    order = one_hot((LANES, LANES), lambda row, col: col == (row % 2) * HALF + row // 2)
    parts = []
    for which in range(2):
        natural = [both[pl.ds(which * layers * rows + r, layers, stride=rows), :] for r in range(rows)]
        part = exact_dot(jnp.concatenate(natural, axis=0), order).reshape(rows, layers, LANES)
        own[:, which] = part
        pairs = part.reshape(rows // 2, 2, layers, LANES)
        parts += [pairs[:, 0], pairs[:, 1]]
    even_x, even_y = place_ref[0] == 0, place_ref[1] == 0
    low, high = jnp.where(even_x, rows - HALO, 0), jnp.where(even_x, 0, rows - HALO)
    xa[...] = own[pl.ds(low, HALO)]
    xb[...] = own[pl.ds(high, HALO)]
    slot = (iota_of(parts[0], 2) // SLOT) % 4
    for g in range(4):
        right = shifted(parts[g], RIGHT_SLOT[g] * SLOT, 2)
        left = shifted(parts[g], (LEFT_SLOT[g] - 3) * SLOT, 2)
        first = right if g == 0 else jnp.where(slot == RIGHT_SLOT[g] % 4, right, first)
        last = left if g == 0 else jnp.where(slot == LEFT_SLOT[g] % 4, left, last)
    ya[...] = jnp.where(even_y, last, first)
    yb[...] = jnp.where(even_y, first, last)
    ba[...] = ya[pl.ds(high // 2, PAIRS)]
    bb[...] = yb[pl.ds(high // 2, PAIRS)]


def widen(rows, place_ref, own, xa, xb, ya, yb, aa, ab, ba, bb, s_ref, k_ref):
    even_x, even_y = place_ref[0] == 0, place_ref[1] == 0
    inner_x, inner_y = place_ref[4] != 0, place_ref[5] != 0
    inner_both = jnp.logical_and(inner_x, inner_y)
    beside = pl.ds(jnp.where(even_x, 0, rows // 2 - PAIRS), PAIRS)
    xa, ya, aa, ab = xa[...], ya[...], aa[beside], ab[beside]
    xb, ba = (jnp.where(inner_x, ref[...], 0.0) for ref in (xb, ba))
    yb, ab = (jnp.where(inner_y, part, 0.0) for part in (yb[...], ab))
    bb = jnp.where(inner_both, bb[...], 0.0)
    before = [jnp.where(even_x, b, a) for a, b in ((aa, ba), (ab, bb))]
    after = [jnp.where(even_x, a, b) for a, b in ((aa, ba), (ab, bb))]
    for start, inner, (a, b) in (
        (0, jnp.where(even_x, xb, xa), before),
        (HALO, own[...], (ya, yb)),
        (HALO + rows, jnp.where(even_x, xa, xb), after),
    ):
        right, left = jnp.where(even_y, a, b), jnp.where(even_y, b, a)
        lane = iota_of(right, 2)
        odd_slot = (lane // SLOT) % 2 == 1
        merged = (jnp.where(odd_slot, left, right), jnp.where(odd_slot, right, left))
        count, layers = right.shape[:2]
        pairs = inner.reshape(count, 2, 2, layers, LANES)
        for which, wide in enumerate((s_ref, k_ref)):
            found = []
            for h in range(2):
                slot = RIGHT_SLOT[2 * which + h]
                block = pairs[:, h, which]
                found.append((
                    jnp.where(lane < HALF, block, shifted(merged[which], HALF - slot * SLOT, 2)),
                    jnp.where(lane < HALF, shifted(block, HALF, 2), shifted(merged[which], -slot * SLOT, 2)),
                ))
            for s in range(2):
                both = jnp.stack([found[0][s], found[1][s]], axis=1)
                wide[pl.ds(start, 2 * count), s] = both.reshape(2 * count, layers, LANES)


def descend_kernel(
    rows, place_ref, own, xa, xb, ya, yb, aa, ab, ba, bb,
    fine_u, fine_g, fine_co, mid_v, mid_g, mid_co, packed, s_ref, k_ref, k1,
):
    h0, h1, m = HALO, HALO // 2, rows // 2
    half = h0 + m
    widen(rows, place_ref, own, xa, xb, ya, yb, aa, ab, ba, bb, s_ref, k_ref)

    def coarser(at, size):
        here = pl.ds(2 * at, 2 * size)
        k1[pl.ds(at, size)] = 0.25 * pair_sum_rows(k_ref[here, 0] + k_ref[here, 1])

    rows_loop(0, half, K1_CHUNK, coarser)
    fine_coefficients(k_ref, s_ref, fine_co, fine_g, h0 - 22, h0 + rows + 22, FINE_SET)
    mid_coefficients(k1, mid_co, h1 - 10, h1 + m + 10, MID_SET)
    descend(rows, place_ref, fine_g, fine_u, fine_g, fine_co, mid_v, mid_g, mid_co, 10, packed, k1[pl.ds(h1, m)])


def descend(rows, place_ref, fine_first, fine_u, fine_g, fine_co, mid_v, mid_g, mid_co, reach, packed, k1=None):
    h0, h1, m = HALO, HALO // 2, rows // 2
    sweep_fine(fine_first, fine_u, fine_co, fine_g, h0 - 2 * reach - 1, h0 + rows + 2 * reach + 1)

    def down(at, size):
        v, new = swept_fine(fine_u, fine_co, fine_g, 2 * at, 2 * size)
        here = pl.ds(2 * at, 2 * size)
        left = fine_co[BACK, here, 0] * (new[0] - v[0]) + fine_co[BACK, here, 1] * (new[1] - v[1])
        mid_g[pl.ds(at, size)] = mid_co[INV, pl.ds(at, size)] * pair_sum_rows(left)

    rows_loop(h1 - reach, h1 + m + reach, DOWN_CHUNK, down)
    sweep(mid_g, mid_v, mid_co, mid_g, h1 - reach + 1, h1 + m + reach - 1)
    v, new = swept(mid_v, mid_co, mid_g, h1, m)
    left = mid_co[BACK, pl.ds(h1, m)] * (new - v)
    low = left if k1 is None else jnp.concatenate([left, 0.25 * k1], axis=0)
    low = coarse_rows(pair_sum_lanes(pair_sum_rows(low)), place_ref)
    for which in range(low.shape[0] // packed.shape[0]):
        for p in range(packed.shape[0]):
            packed[p, which] = low[which * packed.shape[0] + p]


def unpack(place_ref, mine, other, which, target, scale, npx, npy, block):
    even_x = place_ref[0] == 0
    per = 4
    width = LANES // per
    group_of = BLOCKS if npx % BLOCKS == 0 else 1

    def body(step, carry):
        for i in range(group_of):
            ix = step * group_of + i
            for p in range(block // per):
                for q in range(npy // per):
                    devices = [ix * npy + per * q + j for j in range(per)]
                    here = even_x if p == 0 else jnp.logical_not(even_x)
                    parts = [jnp.where(here, mine[i, which], other[i, which]) for i in devices]
                    group = iota_of(parts[0], 1) // width
                    for g in range(per):
                        row = parts[-g % per]
                        for quarter in range(1, per):
                            row = jnp.where(group == quarter, parts[(quarter - g) % per], row)
                        row = shifted(row, -g * width, 1)
                        at = PAD + ix * block + per * p + g
                        lanes = pl.ds(q * LANES, LANES)
                        if scale is not None:
                            row = row * scale[INV, at, :, lanes]
                        target[at, :, lanes] = row
        return carry

    if npx == group_of:
        body(0, 0)
    else:
        lax.fori_loop(0, npx // group_of, body, 0)


def coarse_coefficients(rows2, strips_ref, k2, co, sums):
    width = k2.shape[2]

    def body(at, size):
        k = k2[pl.ds(at, size)]
        lane = iota_of(k, 2)
        open_s, open_n = lane > 0, lane < width - 1
        found = weights(
            k, k2[pl.ds(at - 1, size)], k2[pl.ds(at + 1, size)],
            jnp.where(open_s, shifted(k, 1, 2), 0.0), jnp.where(open_n, shifted(k, -1, 2), 0.0), 16.0 * z_coupling,
        )
        found[S] = jnp.where(open_s, found[S], 0.0)
        found[N] = jnp.where(open_n, found[N], 0.0)
        for which in range(INV + 1):
            co[which, pl.ds(at, size)] = found[which]

    rows_loop(PAD, PAD + rows2, LOW_SET, body)
    zero = jnp.zeros(k2.shape[1:], F32)
    for start, end in strips(strips_ref):
        co[W, PAD + start] = zero
        co[E, PAD + end - 1] = zero
    sums[...] = 1.0 / (relaxation * strip_sums(co.at[BACK], strips_ref, rows2, sums))


def strips(strips_ref):
    ends = [0]
    for index in range(strips_ref.shape[0]):
        ends.append(ends[-1] + strips_ref[index])
    return list(zip(ends[:-1], ends[1:]))


def strip_sums(values, strips_ref, rows2, scratch):
    whole = values[pl.ds(PAD, rows2)]
    row = iota_of(whole, 0)
    before = 0.0
    last = scratch.shape[0] - 1
    for index, (_, end) in enumerate(strips(strips_ref)):
        until = jnp.sum(whole if index == last else jnp.where(row < end, whole, 0.0), axis=0)
        scratch[index] = until - before
        before = until
    total = jnp.sum(jnp.sum(scratch[...], axis=2, keepdims=True), axis=1, keepdims=True)
    return jnp.broadcast_to(total, scratch.shape)


def coarse_solve(rows2, strips_ref, co, sums, g, a, b, over):
    zero = jnp.zeros(g.shape[1:], F32)
    for ref in (g, a, b):
        ref[PAD - 1] = zero
        ref[PAD + rows2] = zero
    for r in range(PAD - 1):
        b[r] = zero
        b[PAD + rows2 + 1 + r] = zero
    at = g
    for index in range(COARSE_SWEEPS - 1):
        to = b if index % 2 == 0 else a
        sweep(at, to, co, g, PAD, PAD + rows2)
        at = to

    def left(first, size):
        v, new = swept(b, co, g, first, size)
        a[pl.ds(first, size)] = co[BACK, pl.ds(first, size)] * (new - v)

    rows_loop(PAD, PAD + rows2, CHUNK, left)
    over[...] = sums[...] * strip_sums(a, strips_ref, rows2, over)


def correct(rows, place_ref, strips_ref, e2, over, mid_v, target, reach):
    h1, m = HALO // 2, rows // 2
    low = -(-reach // 2)
    block = rows // 4
    layers, width = e2.shape[1:]
    span = block + 2 * low
    first_row = place_ref[2] * block - low
    window = e2[pl.ds(first_row + PAD, span)]
    row = iota_of(window, 0) + first_row
    for index, (start, end) in enumerate(strips(strips_ref)):
        window = window + jnp.where((row >= start) & (row < end), over[index][None], 0.0)
    first = place_ref[3] * (HALF // 2)

    def place(row, col):
        from_own = jnp.where(col >= LANES - SLOT, col - LANES, col)
        used = (col < HALF + SLOT) | (col >= LANES - SLOT)
        return used & (row == (from_own + LANES) // 2 - HALF + first)

    spread = exact_dot(window.reshape(span * layers, width), one_hot((width, LANES), place))
    spread = spread.reshape(span, layers, LANES)
    wide = jnp.broadcast_to(spread[:, None], (span, 2, layers, LANES)).reshape(2 * span, layers, LANES)
    start = (h1 - reach) - 2 * (h1 // 2 - low)
    here = pl.ds(h1 - reach, m + 2 * reach)
    target[here] = mid_v[here] + wide[start : start + m + 2 * reach]


def ascend(rows, reach, fine_reach, mid_a, mid_b, mid_co, mid_g, fine_u, fine_a, fine_b, fine_co, fine_g):
    h0, h1, m = HALO, HALO // 2, rows // 2
    sweep(mid_a, mid_b, mid_co, mid_g, h1 - reach + 1, h1 + m + reach - 1)
    sweep(mid_b, mid_a, mid_co, mid_g, h1 - reach + 2, h1 + m + reach - 2)

    def add(at, size):
        fine = fine_u[pl.ds(2 * at, 2 * size)]
        both = fine.reshape((size, 2) + fine.shape[1:]) + mid_a[pl.ds(at, size)][:, None, None]
        fine_a[pl.ds(2 * at, 2 * size)] = both.reshape(fine.shape)

    rows_loop(h1 - reach + 2, h1 + m + reach - 2, ADD_CHUNK, add)
    sweep_fine(fine_a, fine_b, fine_co, fine_g, h0 - fine_reach - 1, h0 + rows + fine_reach + 1)
    sweep_fine(fine_b, fine_a, fine_co, fine_g, h0 - fine_reach, h0 + rows + fine_reach)


def middle_kernel(
    rows, npx, npy, place_ref, strips_ref, mine, other, fine_u, fine_g, fine_co, mid_v, mid_g, mid_co,
    fine_out, mid_v_out, mid_g_out, packed, low_co, sums,
    k2, g2, a2, b2, over, va, vb, fa, fb,
):
    block = rows // 4
    rows2 = npx * block
    zero = jnp.zeros(k2.shape[1:], F32)
    k2[PAD - 1] = zero
    k2[PAD + rows2] = zero
    unpack(place_ref, mine, other, 1, k2, None, npx, npy, block)
    coarse_coefficients(rows2, strips_ref, k2, low_co, sums)
    unpack(place_ref, mine, other, 0, g2, low_co, npx, npy, block)
    coarse_solve(rows2, strips_ref, low_co, sums, g2, a2, b2, over)
    correct(rows, place_ref, strips_ref, b2, over, mid_v, va, 9)
    ascend(rows, 9, 11, va, vb, mid_co, mid_g, fine_u, fa, fb, fine_co, fine_g)
    sweep_fine(fa, fb, fine_co, fine_g, HALO - 10, HALO + rows + 10)
    descend(rows, place_ref, fb, fine_out, fine_g, fine_co, mid_v_out, mid_g_out, mid_co, 4, packed)


def last_kernel(
    rows, npx, npy, place_ref, strips_ref, mine, other, fine_u, fine_g, fine_co, mid_v, mid_g, mid_co, low_co, sums,
    out, g2, a2, b2, over, va, vb, fa, fb,
):
    block = rows // 4
    rows2 = npx * block
    unpack(place_ref, mine, other, 0, g2, low_co, npx, npy, block)
    coarse_solve(rows2, strips_ref, low_co, sums, g2, a2, b2, over)
    correct(rows, place_ref, strips_ref, b2, over, mid_v, va, 3)
    ascend(rows, 3, 0, va, vb, mid_co, mid_g, fine_u, fa, fb, fine_co, fine_g)
    layers = fa.shape[2]
    here = pl.ds(HALO, rows)
    even, odd = fa[here, 0], fa[here, 1]
    both = jnp.where(iota_of(even, 2) < HALF, even, shifted(odd, HALF, 2))

    def place(row, col):
        return col == 2 * (row % HALF) + row // HALF

    natural = exact_dot(both.reshape(rows * layers, LANES), one_hot((LANES, LANES), place))
    for r in range(rows):
        out[pl.ds(r, layers, stride=rows), :] = natural[r * layers : (r + 1) * layers]


def neighbour_swaps(xa, xb, ya, yb, ba, bb):
    npx, npy = lax.axis_size("px"), lax.axis_size("py")

    def swap(block, partner):
        pairs = []
        for x in range(npx):
            for y in range(npy):
                to_x, to_y = partner(x, y, 0 < x < npx - 1, 0 < y < npy - 1)
                pairs.append((x * npy + y, to_x * npy + to_y))
        return lax.ppermute(block, ("px", "py"), pairs)

    def far(i):
        return ((i + 1) ^ 1) - 1

    def corner(x, y, inner_x, inner_y):
        if not inner_y:
            return x ^ 1, y
        return far(x) if inner_x else x, far(y)

    ya = swap(ya, lambda x, y, inner_x, inner_y: (x, y ^ 1))
    xa = swap(xa, lambda x, y, inner_x, inner_y: (x ^ 1, y))
    yb = swap(yb, lambda x, y, inner_x, inner_y: (x, far(y)) if inner_y else (x ^ 1, y))
    xb = swap(xb, lambda x, y, inner_x, inner_y: (far(x), y) if inner_x else (x, y ^ 1))
    ba, bb, xa = lax.optimization_barrier((ba, bb, xa))
    bb = swap(bb, corner)
    ba = swap(ba, lambda x, y, inner_x, inner_y: (far(x) if inner_x else x, y ^ 1))
    aa, ab = (swap(part, lambda x, y, inner_x, inner_y: (x ^ 1, y)) for part in (ya, yb))
    return xa, xb, ya, yb, aa, ab, ba, bb


def arr(*shape):
    return jax.ShapeDtypeStruct(shape, F32)


def shards(source, coefficient, strip_rows):
    npx, npy = lax.axis_size("px"), lax.axis_size("py")
    layers, rows, _ = source.shape
    total, mids = rows + 2 * HALO, (rows + 2 * HALO) // 2
    rows2, width2 = npx * rows // 4, npy * LANES // 4
    px, py = lax.axis_index("px"), lax.axis_index("py")
    inner_x, inner_y = ((i > 0) & (i < n - 1) for i, n in ((px, npx), (py, npy)))
    place = jnp.stack([px % 2, py % 2, px, py, inner_x, inner_y]).astype(jnp.int32)
    fine, mid = arr(total, 2, layers, LANES), arr(mids, layers, LANES)
    low, strip_sums = arr(rows2 + 2 * PAD, layers, width2), arr(strip_rows.shape[0], layers, width2)
    fine_cos, mid_cos, low_cos = (arr(n, *item.shape) for n, item in ((7, fine), (8, mid), (8, low)))
    halo, columns, corner = (arr(*n, layers, LANES) for n in ((HALO, 2), (rows // 2,), (PAIRS,)))
    room = min(48, 12 + 24 * rows2 * layers * width2 * 4 // 2**20)

    def call(body, name, smem, vmem, out_shape, scratch):
        return pl.pallas_call(
            functools.partial(body, rows),
            out_shape=out_shape,
            in_specs=[SMEM] * smem + [VMEM] * vmem,
            out_specs=jax.tree.map(lambda _: VMEM, out_shape),
            scratch_shapes=[pltpu.VMEM(item.shape, F32) for item in scratch],
            compiler_params=pltpu.CompilerParams(vmem_limit_bytes=room * 2**20),
            name=name,
        )

    both = jnp.stack([source, coefficient]).reshape(2 * layers * rows, LANES)
    own, *sent = call(
        cut_kernel, "cut", 1, 1, (arr(rows, 2, layers, LANES),) + (halo,) * 2 + (columns,) * 2 + (corner,) * 2, ()
    )(place, both)
    fine_u, fine_g, fine_co, mid_v, mid_g, mid_co, packed = call(
        descend_kernel, "descend", 1, 9, (fine, fine, fine_cos, mid, mid, mid_cos, arr(2, 2, layers, LANES)),
        (fine, fine, mid),
    )(place, own, *neighbour_swaps(*sent))

    def gather(block):
        shape = (npx // 2, 2, npy) + block.shape[1:]
        every = jnp.broadcast_to(block[None, :, None], shape).reshape((npx * npy,) + block.shape[1:])
        half = lax.all_to_all(every, ("px", "py"), 0, 0, tiled=True)
        return half, lax.ppermute(half, "px", [(i, i ^ 1) for i in range(npx)])

    def sized(body):
        return lambda rows, *refs: body(rows, npx, npy, *refs)

    fine_u, mid_v, mid_g, packed, low_co, sums = call(
        sized(middle_kernel), "middle", 2, 8, (fine, mid, mid, arr(2, 1, layers, LANES), low_cos, strip_sums),
        (low, low, low, low, strip_sums, mid, mid, fine, fine),
    )(place, strip_rows, *gather(packed), fine_u, fine_g, fine_co, mid_v, mid_g, mid_co)
    out = call(
        sized(last_kernel), "last", 2, 10, arr(layers * rows, LANES),
        (low, low, low, strip_sums, mid, mid, fine, fine),
    )(place, strip_rows, *gather(packed), fine_u, fine_g, fine_co, mid_v, mid_g, mid_co, low_co, sums)
    return out.reshape(source.shape)


def solution(mesh):
    placed = (P(None, "px", "py"), P(None, "px", "py"), P())
    return jax.shard_map(
        shards, mesh=mesh, in_specs=placed, out_specs=P(None, "px", "py"), check_vma=False
    )
```

```python
import functools

import jax
import jax.numpy as jnp
from jax import lax
from jax.experimental import pallas as pl
from jax.experimental.pallas import tpu as pltpu
from jax.sharding import PartitionSpec as P

COARSE_SWEEPS = 6
relaxation = 0.8
z_coupling = 0.25

HALO = 24
SIDE = 32
PAD = 8
LANES = 128
HALF = LANES // 2
SLOT = SIDE // 2
VMEM = pl.BlockSpec(memory_space=pltpu.VMEM)
SMEM = pl.BlockSpec(memory_space=pltpu.SMEM)
F32 = jnp.float32


def shifted(values, amount, axis):
    return pltpu.roll(values, amount % values.shape[axis], axis)


def iota_of(values, axis):
    return lax.broadcasted_iota(jnp.int32, values.shape, axis % values.ndim)


def rows_loop(low, high, chunk, body):
    chunk = min(chunk, high - low)
    count = -(-(high - low) // chunk)
    chunk = -(-(high - low) // count)

    def step(index, carry):
        body(jnp.minimum(low + index * chunk, high - chunk), chunk)
        return carry

    if count == 1:
        body(low, chunk)
    else:
        lax.fori_loop(0, count, step, 0)


def pair_sum_rows(values):
    count = values.shape[0] // 2
    pairs = values.reshape((count, 2) + values.shape[1:])
    return pairs[:, 0] + pairs[:, 1]


def pair_sum_lanes(values):
    return values + jnp.where(iota_of(values, -1) % 2 == 0, shifted(values, -1, 2), shifted(values, 1, 2))


def exact_dot(left, right):
    total = None
    for last in (False, False, True):
        part = left.astype(jnp.bfloat16)
        term = lax.dot_general(part, right, (((1,), (0,)), ((), ())), preferred_element_type=F32)
        total = term if total is None else total + term
        if not last:
            left = left - part.astype(F32)
    return total


def one_hot(shape, place):
    row = lax.broadcasted_iota(jnp.int32, shape, 0)
    col = lax.broadcasted_iota(jnp.int32, shape, 1)
    return jnp.where(place(row, col), 1.0, 0.0).astype(jnp.bfloat16)


W, E, S, N, D, U, BACK, INV = range(8)


def weights(k, west, east, south, north, z_factor):
    layer = iota_of(k, -2)
    west, east, south, north = (k + other for other in (west, east, south, north))
    axis = k.ndim - 2
    down = jnp.where(layer == 0, 0.0, z_factor * (k + shifted(k, 1, axis)))
    up = jnp.where(layer == k.shape[axis] - 1, 0.0, z_factor * (k + shifted(k, -1, axis)))
    diagonal = west + east + south + north + down + up
    rough = pl.reciprocal(diagonal, approx=True)
    rough = rough * (2.0 - diagonal * rough)
    inverse = rough * (2.0 * relaxation - relaxation * (diagonal * rough))
    inverse = jnp.where(k > 0.0, inverse, 0.0)
    scaled = [inverse * face for face in (west, east, south, north, down, up)]
    return scaled + [(0.5 / relaxation) * diagonal, 2.0 * inverse]


def fine_coefficients(k_ref, s_ref, co, g_ref, low, high, chunk):
    def body(at, size):
        here, before, after = pl.ds(at, size), pl.ds(at - 1, size), pl.ds(at + 1, size)
        k = [k_ref[here, s] for s in range(2)]
        sides = ((shifted(k[1], 1, 2), k[1]), (k[0], shifted(k[0], -1, 2)))
        for s in range(2):
            found = weights(k[s], k_ref[before, s], k_ref[after, s], *sides[s], z_coupling)
            for which in range(INV):
                co[which, here, s] = found[which]
            g_ref[here, s] = found[INV] * s_ref[here, s]

    rows_loop(low, high, chunk, body)


def mid_coefficients(k_ref, co, low, high, chunk):
    def body(at, size):
        here = pl.ds(at, size)
        k = k_ref[here]
        found = weights(
            k, k_ref[pl.ds(at - 1, size)], k_ref[pl.ds(at + 1, size)], shifted(k, 1, 2), shifted(k, -1, 2),
            4.0 * z_coupling,
        )
        for which in range(INV + 1):
            co[which, here] = found[which]

    rows_loop(low, high, chunk, body)


def swept_fine(v_ref, co, g_ref, at, size):
    here = pl.ds(at, size)
    around = v_ref[pl.ds(at - 1, size + 2)]
    v = [around[1:-1, s] for s in range(2)]
    sides = ((shifted(v[1], 1, 2), v[1]), (v[0], shifted(v[0], -1, 2)))
    new = []
    for s in range(2):
        total = g_ref[here, s] + (1.0 - relaxation) * v[s]
        total = total + co[W, here, s] * around[:-2, s]
        total = total + co[E, here, s] * around[2:, s]
        total = total + co[D, here, s] * shifted(v[s], 1, 1)
        total = total + co[U, here, s] * shifted(v[s], -1, 1)
        total = total + co[S, here, s] * sides[s][0]
        total = total + co[N, here, s] * sides[s][1]
        new.append(total)
    return v, new


def swept(v_ref, co, g_ref, at, size):
    here = pl.ds(at, size)
    around = v_ref[pl.ds(at - 1, size + 2)]
    v = around[1:-1]
    total = g_ref[here] + (1.0 - relaxation) * v
    total = total + co[W, here] * around[:-2]
    total = total + co[E, here] * around[2:]
    total = total + co[D, here] * shifted(v, 1, 1)
    total = total + co[U, here] * shifted(v, -1, 1)
    total = total + co[S, here] * shifted(v, 1, 2)
    total = total + co[N, here] * shifted(v, -1, 2)
    return v, total


def sweep_fine(v_ref, out_ref, co, g_ref, low, high):
    def body(at, size):
        new = swept_fine(v_ref, co, g_ref, at, size)[1]
        for s in range(2):
            out_ref[pl.ds(at, size), s] = new[s]

    rows_loop(low, high, FINE_CHUNK, body)


def sweep(v_ref, out_ref, co, g_ref, low, high):
    def body(at, size):
        out_ref[pl.ds(at, size)] = swept(v_ref, co, g_ref, at, size)[1]

    rows_loop(low, high, CHUNK, body)


FINE_CHUNK = 80
CHUNK = 64
DOWN_CHUNK = 36
FINE_SET = 80
MID_SET = 40
LOW_SET = 64
ADD_CHUNK = 40
K1_CHUNK = 40
BLOCKS = 8


def coarse_rows(values, place_ref):
    per = LANES // (HALF // 2)
    count, layers = values.shape[:2]
    pick = one_hot((LANES, LANES), lambda row, col: (row < HALF) & (row == 2 * col))
    cells = exact_dot(values.reshape(count * layers, LANES), pick).reshape(count // per, per, layers, LANES)
    packed = [shifted(cells[:, g], (place_ref[3] + g) % per * (HALF // 2), 2) for g in range(per)]
    return packed[0] + packed[1] + packed[2] + packed[3]


RIGHT_SLOT = (0, 2, 1, 3)
LEFT_SLOT = (3, 5, 4, 6)
PAIRS = HALO // 2


def cut_kernel(rows, place_ref, both, own, xa, xb, ya, yb, ba, bb):
    layers = own.shape[2]
    pick = [[pl.ds(which * layers * rows + r, layers, stride=rows) for which in range(2)] for r in range(rows)]
    left = jnp.concatenate(
        [jnp.concatenate([both[at, :] for at in pair], axis=1) for pair in pick], axis=0
    )

    def place(row, col):
        y = row % LANES
        return col == (row // LANES) * LANES + (y % 2) * HALF + y // 2

    sorted_y = exact_dot(left, one_hot((2 * LANES, 2 * LANES), place))
    parts = []
    for which in range(2):
        part = sorted_y[:, which * LANES : (which + 1) * LANES].reshape(rows, layers, LANES)
        own[:, which] = part
        pairs = part.reshape(rows // 2, 2, layers, LANES)
        parts += [pairs[:, 0], pairs[:, 1]]
    even_x, even_y = place_ref[0] == 0, place_ref[1] == 0
    low, high = jnp.where(even_x, rows - HALO, 0), jnp.where(even_x, 0, rows - HALO)
    xa[...] = own[pl.ds(low, HALO)]
    xb[...] = own[pl.ds(high, HALO)]
    slot = (iota_of(parts[0], 2) // SLOT) % 4
    for g in range(4):
        right = shifted(parts[g], RIGHT_SLOT[g] * SLOT, 2)
        left = shifted(parts[g], (LEFT_SLOT[g] - 3) * SLOT, 2)
        first = right if g == 0 else jnp.where(slot == RIGHT_SLOT[g] % 4, right, first)
        last = left if g == 0 else jnp.where(slot == LEFT_SLOT[g] % 4, left, last)
    ya[...] = jnp.where(even_y, last, first)
    yb[...] = jnp.where(even_y, first, last)
    ba[...] = ya[pl.ds(high // 2, PAIRS)]
    bb[...] = yb[pl.ds(high // 2, PAIRS)]


def widen(rows, place_ref, own, xa, xb, ya, yb, aa, ab, ba, bb, s_ref, k_ref):
    even_x, even_y = place_ref[0] == 0, place_ref[1] == 0
    inner_x, inner_y = place_ref[4] != 0, place_ref[5] != 0
    inner_both = jnp.logical_and(inner_x, inner_y)
    beside = pl.ds(jnp.where(even_x, 0, rows // 2 - PAIRS), PAIRS)
    xa, ya, aa, ab = xa[...], ya[...], aa[beside], ab[beside]
    xb, ba = (jnp.where(inner_x, ref[...], 0.0) for ref in (xb, ba))
    yb, ab = (jnp.where(inner_y, part, 0.0) for part in (yb[...], ab))
    bb = jnp.where(inner_both, bb[...], 0.0)
    before = [jnp.where(even_x, b, a) for a, b in ((aa, ba), (ab, bb))]
    after = [jnp.where(even_x, a, b) for a, b in ((aa, ba), (ab, bb))]
    for start, inner, (a, b) in (
        (0, jnp.where(even_x, xb, xa), before),
        (HALO, own[...], (ya, yb)),
        (HALO + rows, jnp.where(even_x, xa, xb), after),
    ):
        right, left = jnp.where(even_y, a, b), jnp.where(even_y, b, a)
        lane = iota_of(right, 2)
        odd_slot = (lane // SLOT) % 2 == 1
        merged = (jnp.where(odd_slot, left, right), jnp.where(odd_slot, right, left))
        count, layers = right.shape[:2]
        pairs = inner.reshape(count, 2, 2, layers, LANES)
        for which, wide in enumerate((s_ref, k_ref)):
            found = []
            for h in range(2):
                slot = RIGHT_SLOT[2 * which + h]
                block = pairs[:, h, which]
                found.append((
                    jnp.where(lane < HALF, block, shifted(merged[which], HALF - slot * SLOT, 2)),
                    jnp.where(lane < HALF, shifted(block, HALF, 2), shifted(merged[which], -slot * SLOT, 2)),
                ))
            for s in range(2):
                both = jnp.stack([found[0][s], found[1][s]], axis=1)
                wide[pl.ds(start, 2 * count), s] = both.reshape(2 * count, layers, LANES)


def descend_kernel(
    rows, place_ref, own, xa, xb, ya, yb, aa, ab, ba, bb,
    fine_u, fine_g, fine_co, mid_v, mid_g, mid_co, packed, s_ref, k_ref, k1,
):
    h0, h1, m = HALO, HALO // 2, rows // 2
    half = h0 + m
    widen(rows, place_ref, own, xa, xb, ya, yb, aa, ab, ba, bb, s_ref, k_ref)

    def coarser(at, size):
        here = pl.ds(2 * at, 2 * size)
        k1[pl.ds(at, size)] = 0.25 * pair_sum_rows(k_ref[here, 0] + k_ref[here, 1])

    rows_loop(0, half, K1_CHUNK, coarser)
    fine_coefficients(k_ref, s_ref, fine_co, fine_g, h0 - 22, h0 + rows + 22, FINE_SET)
    mid_coefficients(k1, mid_co, h1 - 10, h1 + m + 10, MID_SET)
    descend(rows, place_ref, fine_g, fine_u, fine_g, fine_co, mid_v, mid_g, mid_co, 10, packed, k1[pl.ds(h1, m)])


def descend(rows, place_ref, fine_first, fine_u, fine_g, fine_co, mid_v, mid_g, mid_co, reach, packed, k1=None):
    h0, h1, m = HALO, HALO // 2, rows // 2
    sweep_fine(fine_first, fine_u, fine_co, fine_g, h0 - 2 * reach - 1, h0 + rows + 2 * reach + 1)

    def down(at, size):
        v, new = swept_fine(fine_u, fine_co, fine_g, 2 * at, 2 * size)
        here = pl.ds(2 * at, 2 * size)
        left = fine_co[BACK, here, 0] * (new[0] - v[0]) + fine_co[BACK, here, 1] * (new[1] - v[1])
        mid_g[pl.ds(at, size)] = mid_co[INV, pl.ds(at, size)] * pair_sum_rows(left)

    rows_loop(h1 - reach, h1 + m + reach, DOWN_CHUNK, down)
    sweep(mid_g, mid_v, mid_co, mid_g, h1 - reach + 1, h1 + m + reach - 1)
    v, new = swept(mid_v, mid_co, mid_g, h1, m)
    left = mid_co[BACK, pl.ds(h1, m)] * (new - v)
    low = left if k1 is None else jnp.concatenate([left, 0.25 * k1], axis=0)
    low = coarse_rows(pair_sum_lanes(pair_sum_rows(low)), place_ref)
    for which in range(low.shape[0] // packed.shape[0]):
        for p in range(packed.shape[0]):
            packed[p, which] = low[which * packed.shape[0] + p]


def unpack(place_ref, mine, other, which, target, scale, npx, npy, block):
    even_x = place_ref[0] == 0
    per = 4
    width = LANES // per
    group_of = BLOCKS if npx % BLOCKS == 0 else 1

    def body(step, carry):
        for i in range(group_of):
            ix = step * group_of + i
            for p in range(block // per):
                for q in range(npy // per):
                    devices = [ix * npy + per * q + j for j in range(per)]
                    here = even_x if p == 0 else jnp.logical_not(even_x)
                    parts = [jnp.where(here, mine[i, which], other[i, which]) for i in devices]
                    group = iota_of(parts[0], 1) // width
                    for g in range(per):
                        row = parts[-g % per]
                        for quarter in range(1, per):
                            row = jnp.where(group == quarter, parts[(quarter - g) % per], row)
                        row = shifted(row, -g * width, 1)
                        at = PAD + ix * block + per * p + g
                        lanes = pl.ds(q * LANES, LANES)
                        if scale is not None:
                            row = row * scale[INV, at, :, lanes]
                        target[at, :, lanes] = row
        return carry

    if npx == group_of:
        body(0, 0)
    else:
        lax.fori_loop(0, npx // group_of, body, 0)


def coarse_coefficients(rows2, strips_ref, k2, co, sums):
    width = k2.shape[2]

    def body(at, size):
        k = k2[pl.ds(at, size)]
        lane = iota_of(k, 2)
        open_s, open_n = lane > 0, lane < width - 1
        found = weights(
            k, k2[pl.ds(at - 1, size)], k2[pl.ds(at + 1, size)],
            jnp.where(open_s, shifted(k, 1, 2), 0.0), jnp.where(open_n, shifted(k, -1, 2), 0.0), 16.0 * z_coupling,
        )
        found[S] = jnp.where(open_s, found[S], 0.0)
        found[N] = jnp.where(open_n, found[N], 0.0)
        for which in range(INV + 1):
            co[which, pl.ds(at, size)] = found[which]

    rows_loop(PAD, PAD + rows2, LOW_SET, body)
    zero = jnp.zeros(k2.shape[1:], F32)
    for start, end in strips(strips_ref):
        co[W, PAD + start] = zero
        co[E, PAD + end - 1] = zero
    sums[...] = 1.0 / (relaxation * strip_sums(co.at[BACK], strips_ref, rows2, sums))


def strips(strips_ref):
    ends = [0]
    for index in range(strips_ref.shape[0]):
        ends.append(ends[-1] + strips_ref[index])
    return list(zip(ends[:-1], ends[1:]))


def strip_sums(values, strips_ref, rows2, scratch):
    whole = values[pl.ds(PAD, rows2)]
    row = iota_of(whole, 0)
    before = 0.0
    last = scratch.shape[0] - 1
    for index, (_, end) in enumerate(strips(strips_ref)):
        until = jnp.sum(whole if index == last else jnp.where(row < end, whole, 0.0), axis=0)
        scratch[index] = until - before
        before = until
    total = jnp.sum(jnp.sum(scratch[...], axis=2, keepdims=True), axis=1, keepdims=True)
    return jnp.broadcast_to(total, scratch.shape)


def coarse_solve(rows2, strips_ref, co, sums, g, a, b, over):
    zero = jnp.zeros(g.shape[1:], F32)
    for ref in (g, a, b):
        ref[PAD - 1] = zero
        ref[PAD + rows2] = zero
    for r in range(PAD - 1):
        b[r] = zero
        b[PAD + rows2 + 1 + r] = zero
    at = g
    for index in range(COARSE_SWEEPS - 1):
        to = b if index % 2 == 0 else a
        sweep(at, to, co, g, PAD, PAD + rows2)
        at = to

    def left(first, size):
        v, new = swept(b, co, g, first, size)
        a[pl.ds(first, size)] = co[BACK, pl.ds(first, size)] * (new - v)

    rows_loop(PAD, PAD + rows2, CHUNK, left)
    over[...] = sums[...] * strip_sums(a, strips_ref, rows2, over)


def correct(rows, place_ref, strips_ref, e2, over, mid_v, target, reach):
    h1, m = HALO // 2, rows // 2
    low = -(-reach // 2)
    block = rows // 4
    layers, width = e2.shape[1:]
    span = block + 2 * low
    first_row = place_ref[2] * block - low
    window = e2[pl.ds(first_row + PAD, span)]
    row = iota_of(window, 0) + first_row
    for index, (start, end) in enumerate(strips(strips_ref)):
        window = window + jnp.where((row >= start) & (row < end), over[index][None], 0.0)
    first = place_ref[3] * (HALF // 2)

    def place(row, col):
        from_own = jnp.where(col >= LANES - SLOT, col - LANES, col)
        used = (col < HALF + SLOT) | (col >= LANES - SLOT)
        return used & (row == (from_own + LANES) // 2 - HALF + first)

    spread = exact_dot(window.reshape(span * layers, width), one_hot((width, LANES), place))
    spread = spread.reshape(span, layers, LANES)
    wide = jnp.broadcast_to(spread[:, None], (span, 2, layers, LANES)).reshape(2 * span, layers, LANES)
    start = (h1 - reach) - 2 * (h1 // 2 - low)
    here = pl.ds(h1 - reach, m + 2 * reach)
    target[here] = mid_v[here] + wide[start : start + m + 2 * reach]


def ascend(rows, reach, fine_reach, mid_a, mid_b, mid_co, mid_g, fine_u, fine_a, fine_b, fine_co, fine_g):
    h0, h1, m = HALO, HALO // 2, rows // 2
    sweep(mid_a, mid_b, mid_co, mid_g, h1 - reach + 1, h1 + m + reach - 1)
    sweep(mid_b, mid_a, mid_co, mid_g, h1 - reach + 2, h1 + m + reach - 2)

    def add(at, size):
        fine = fine_u[pl.ds(2 * at, 2 * size)]
        both = fine.reshape((size, 2) + fine.shape[1:]) + mid_a[pl.ds(at, size)][:, None, None]
        fine_a[pl.ds(2 * at, 2 * size)] = both.reshape(fine.shape)

    rows_loop(h1 - reach + 2, h1 + m + reach - 2, ADD_CHUNK, add)
    sweep_fine(fine_a, fine_b, fine_co, fine_g, h0 - fine_reach - 1, h0 + rows + fine_reach + 1)
    sweep_fine(fine_b, fine_a, fine_co, fine_g, h0 - fine_reach, h0 + rows + fine_reach)


def middle_kernel(
    rows, npx, npy, place_ref, strips_ref, mine, other, fine_u, fine_g, fine_co, mid_v, mid_g, mid_co,
    fine_out, mid_v_out, mid_g_out, packed, low_co, sums,
    k2, g2, a2, b2, over, va, vb, fa, fb,
):
    block = rows // 4
    rows2 = npx * block
    zero = jnp.zeros(k2.shape[1:], F32)
    k2[PAD - 1] = zero
    k2[PAD + rows2] = zero
    unpack(place_ref, mine, other, 1, k2, None, npx, npy, block)
    coarse_coefficients(rows2, strips_ref, k2, low_co, sums)
    unpack(place_ref, mine, other, 0, g2, low_co, npx, npy, block)
    coarse_solve(rows2, strips_ref, low_co, sums, g2, a2, b2, over)
    correct(rows, place_ref, strips_ref, b2, over, mid_v, va, 9)
    ascend(rows, 9, 11, va, vb, mid_co, mid_g, fine_u, fa, fb, fine_co, fine_g)
    sweep_fine(fa, fb, fine_co, fine_g, HALO - 10, HALO + rows + 10)
    descend(rows, place_ref, fb, fine_out, fine_g, fine_co, mid_v_out, mid_g_out, mid_co, 4, packed)


def last_kernel(
    rows, npx, npy, place_ref, strips_ref, mine, other, fine_u, fine_g, fine_co, mid_v, mid_g, mid_co, low_co, sums,
    out, g2, a2, b2, over, va, vb, fa, fb,
):
    block = rows // 4
    rows2 = npx * block
    unpack(place_ref, mine, other, 0, g2, low_co, npx, npy, block)
    coarse_solve(rows2, strips_ref, low_co, sums, g2, a2, b2, over)
    correct(rows, place_ref, strips_ref, b2, over, mid_v, va, 3)
    ascend(rows, 3, 0, va, vb, mid_co, mid_g, fine_u, fa, fb, fine_co, fine_g)
    layers = fa.shape[2]
    here = pl.ds(HALO, rows)
    even, odd = fa[here, 0], fa[here, 1]
    both = jnp.where(iota_of(even, 2) < HALF, even, shifted(odd, HALF, 2))

    def place(row, col):
        return col == 2 * (row % HALF) + row // HALF

    natural = exact_dot(both.reshape(rows * layers, LANES), one_hot((LANES, LANES), place))
    for r in range(rows):
        out[pl.ds(r, layers, stride=rows), :] = natural[r * layers : (r + 1) * layers]


def neighbour_swaps(xa, xb, ya, yb, ba, bb):
    npx, npy = lax.axis_size("px"), lax.axis_size("py")

    def swap(block, partner):
        pairs = []
        for x in range(npx):
            for y in range(npy):
                to_x, to_y = partner(x, y, 0 < x < npx - 1, 0 < y < npy - 1)
                pairs.append((x * npy + y, to_x * npy + to_y))
        return lax.ppermute(block, ("px", "py"), pairs)

    def far(i):
        return ((i + 1) ^ 1) - 1

    def corner(x, y, inner_x, inner_y):
        if not inner_y:
            return x ^ 1, y
        return far(x) if inner_x else x, far(y)

    xa = swap(xa, lambda x, y, inner_x, inner_y: (x ^ 1, y))
    xb = swap(xb, lambda x, y, inner_x, inner_y: (far(x), y) if inner_x else (x, y ^ 1))
    ya, yb, ba, bb, xa = lax.optimization_barrier((ya, yb, ba, bb, xa))
    ya = swap(ya, lambda x, y, inner_x, inner_y: (x, y ^ 1))
    yb = swap(yb, lambda x, y, inner_x, inner_y: (x, far(y)) if inner_y else (x ^ 1, y))
    ba = swap(ba, lambda x, y, inner_x, inner_y: (far(x) if inner_x else x, y ^ 1))
    bb = swap(bb, corner)
    aa, ab = (swap(part, lambda x, y, inner_x, inner_y: (x ^ 1, y)) for part in (ya, yb))
    return xa, xb, ya, yb, aa, ab, ba, bb


def arr(*shape):
    return jax.ShapeDtypeStruct(shape, F32)


def shards(source, coefficient, strip_rows):
    npx, npy = lax.axis_size("px"), lax.axis_size("py")
    layers, rows, _ = source.shape
    total, mids = rows + 2 * HALO, (rows + 2 * HALO) // 2
    rows2, width2 = npx * rows // 4, npy * LANES // 4
    px, py = lax.axis_index("px"), lax.axis_index("py")
    inner_x, inner_y = ((i > 0) & (i < n - 1) for i, n in ((px, npx), (py, npy)))
    place = jnp.stack([px % 2, py % 2, px, py, inner_x, inner_y]).astype(jnp.int32)
    fine, mid = arr(total, 2, layers, LANES), arr(mids, layers, LANES)
    low, strip_sums = arr(rows2 + 2 * PAD, layers, width2), arr(strip_rows.shape[0], layers, width2)
    fine_cos, mid_cos, low_cos = (arr(n, *item.shape) for n, item in ((7, fine), (8, mid), (8, low)))
    halo, columns, corner = (arr(*n, layers, LANES) for n in ((HALO, 2), (rows // 2,), (PAIRS,)))
    room = min(48, 12 + 24 * rows2 * layers * width2 * 4 // 2**20)

    def call(body, name, smem, vmem, out_shape, scratch):
        return pl.pallas_call(
            functools.partial(body, rows),
            out_shape=out_shape,
            in_specs=[SMEM] * smem + [VMEM] * vmem,
            out_specs=jax.tree.map(lambda _: VMEM, out_shape),
            scratch_shapes=[pltpu.VMEM(item.shape, F32) for item in scratch],
            compiler_params=pltpu.CompilerParams(vmem_limit_bytes=room * 2**20),
            name=name,
        )

    both = jnp.stack([source, coefficient]).reshape(2 * layers * rows, LANES)
    own, *sent = call(
        cut_kernel, "cut", 1, 1, (arr(rows, 2, layers, LANES),) + (halo,) * 2 + (columns,) * 2 + (corner,) * 2, ()
    )(place, both)
    fine_u, fine_g, fine_co, mid_v, mid_g, mid_co, packed = call(
        descend_kernel, "descend", 1, 9, (fine, fine, fine_cos, mid, mid, mid_cos, arr(2, 2, layers, LANES)),
        (fine, fine, mid),
    )(place, own, *neighbour_swaps(*sent))

    def gather(block):
        shape = (npx // 2, 2, npy) + block.shape[1:]
        every = jnp.broadcast_to(block[None, :, None], shape).reshape((npx * npy,) + block.shape[1:])
        half = lax.all_to_all(every, ("px", "py"), 0, 0, tiled=True)
        return half, lax.ppermute(half, "px", [(i, i ^ 1) for i in range(npx)])

    def sized(body):
        return lambda rows, *refs: body(rows, npx, npy, *refs)

    fine_u, mid_v, mid_g, packed, low_co, sums = call(
        sized(middle_kernel), "middle", 2, 8, (fine, mid, mid, arr(2, 1, layers, LANES), low_cos, strip_sums),
        (low, low, low, low, strip_sums, mid, mid, fine, fine),
    )(place, strip_rows, *gather(packed), fine_u, fine_g, fine_co, mid_v, mid_g, mid_co)
    out = call(
        sized(last_kernel), "last", 2, 10, arr(layers * rows, LANES),
        (low, low, low, strip_sums, mid, mid, fine, fine),
    )(place, strip_rows, *gather(packed), fine_u, fine_g, fine_co, mid_v, mid_g, mid_co, low_co, sums)
    return out.reshape(source.shape)


def solution(mesh):
    placed = (P(None, "px", "py"), P(None, "px", "py"), P())
    return jax.shard_map(
        shards, mesh=mesh, in_specs=placed, out_specs=P(None, "px", "py"), check_vma=False
    )
```
